768 devices in a mesh: slide: 8 (over x, core), gy: 12 (over z), gx: 8 (over y).
Axes of the slice: x: 4, y: 8, z: 12, core: 2. Of those that a mesh axis runs over, the one named last changes fastest.
Arguments:
- features: bfloat16 [8, 192, 512, 256], P('slide', 'gy', 'gx'), may hold values from -6 to 6
- depth_weight: bfloat16 [3, 3, 256], replicated, may hold values from -2 to 2
- point_weight: bfloat16 [256, 256], replicated, may hold values from -0.375 to 0.375
- classifier: float32 [2, 256, 256], replicated
- valid_count: int32 [8, 12, 8], P('slide', 'gy', 'gx'), may hold values from 512 to 1024, as said below
- labels: int32 [8], P('slide'), may hold values from 0 to 1
Outputs:
- loss_value: float32 [], replicated
- depth_gradient: float32 [3, 3, 256], replicated
- point_gradient: float32 [256, 256], replicated
- classifier_gradient: float32 [2, 256, 256], replicated
- feature_gradient: bfloat16 [8, 192, 512, 256], P('slide', 'gy', 'gx')
The draws below stay inside these ranges and needn't reach their ends.
Inputs may be any that keep to these rules, and one draw needn't show every extreme that they name: `valid_count`: every tile holds 512 or more valid pixels, and tile 0 of every slide holds exactly 1024.
All inputs are finite; a program needn't handle non-finite values.
Results may differ from the reference program's by a relative error of at most 0.0064.
The reference program's roundings to bfloat16 on the way count: a program that leaves them out, or rounds other values in their place, can miss the bound.
Values may be sent and summed in bfloat16 or wider, within the bound.
No kernel may reach another device: no remote copies, remote signals or barrier semaphores. Data moves between devices by JAX's collectives and lax.ppermute only.
A program may use at most 32 MiB of HBM per device.

```python
import jax
import jax.numpy as jnp
from jax import lax

C = 256
NCLS = 2
ITERS = 5
R = 16
W_DEV = 64
SLIDES = 8
TILES_Y = 12
TILES_X = 8
ROWS = 192
COLS = 512
PIX = 1024


def draw_classifier(key, part):
    key = jax.random.fold_in(key, 11)
    values = 0.15 * jax.random.normal(key, (NCLS, C, C), jnp.float32)
    return values


def draw_valid_count(key, part):
    key = jax.random.fold_in(key, 23)
    counts = jax.random.randint(key, (SLIDES, TILES_Y, TILES_X), PIX // 2, PIX + 1)
    counts = counts.at[:, 0, 0].set(PIX)
    return counts.astype(jnp.int32)


def plant(drawn, rng, smallest, largest):
    spot = [jax.random.randint(jax.random.fold_in(rng, axis), (), 0, length) for axis, length in enumerate(drawn.shape)]
    widest = drawn.shape.index(max(drawn.shape))
    neighbour = spot[:widest] + [(spot[widest] + 1) % drawn.shape[widest]] + spot[widest + 1:]
    return drawn.at[tuple(spot)].set(smallest).at[tuple(neighbour)].set(largest)


def block_levels(key, extent, pieces, smallest, largest):
    gain = 1.0
    for dim, shards_of in pieces:
        steps = jax.random.uniform(jax.random.fold_in(jax.random.fold_in(key, 6), dim), (shards_of,), jnp.float32, smallest / len(pieces), largest / len(pieces))
        gain = gain * jnp.repeat(jnp.exp(steps), extent[dim] // shards_of).reshape((-1,) + (1,) * (len(extent) - 1 - dim))
    return gain


def noise(stream_key, shape, deviation, reach, cuts=(), kind=jnp.bfloat16):
    values = deviation * jax.random.normal(stream_key, shape, jnp.float32)
    if cuts:
        values = values * block_levels(stream_key, shape, cuts, -0.22, 0.18)
    return jnp.clip(values, -reach, reach).astype(kind)


def setup_inputs(seed: int = 0) -> dict:
    key_list = jax.random.split(jax.random.key(seed), 7)
    return {
        "features": noise(key_list[0], (SLIDES, ROWS, COLS, C), 1.0, 6.0, ((0, 8), (1, 12), (2, 8))),
        "depth_weight": noise(key_list[1], (3, 3, C), 9 ** -0.5, 2.0),
        "point_weight": noise(key_list[2], (C, C), C ** -0.5, 0.375),
        "classifier": draw_classifier(jax.random.fold_in(key_list[6], 71), 0),
        "valid_count": draw_valid_count(jax.random.fold_in(key_list[6], 71), 0),
        "labels": plant(jax.random.randint(key_list[5], (SLIDES,), 0, NCLS), jax.random.fold_in(key_list[5], 1), 0, NCLS - 1).astype(jnp.int32),
    }


def matmul_high(left, right):
    return jnp.dot(left, right, precision=lax.Precision.HIGHEST)

def cov_root(second_in, first_in, pixel_count):
    identity = jnp.eye(second_in.shape[0], dtype=second_in.dtype)
    mean_vec = first_in / pixel_count
    sigma = second_in / pixel_count - jnp.outer(mean_vec, mean_vec)
    trace_val = jnp.trace(sigma)
    ymat = sigma / trace_val
    zmat = identity
    for step_index in range(ITERS):
        middle = 0.5 * (3.0 * identity - matmul_high(zmat, ymat))
        ymat = matmul_high(ymat, middle)
        zmat = matmul_high(middle, zmat)
    return jnp.sqrt(trace_val) * ymat

def depthwise(padded, weights, height, width):
    result = jnp.zeros((height, width, padded.shape[2]), jnp.float32)
    for offset_row in range(3):
        for offset_col in range(3):
            result = result + padded[offset_row:offset_row + height, offset_col:offset_col + width].astype(jnp.float32) * weights[offset_row, offset_col].astype(jnp.float32)
    return result

def reference(features, depth_weight, point_weight, classifier, valid_count, labels):
    loss_total = jnp.zeros((), jnp.float32)
    depth_total = jnp.zeros((3, 3, C), jnp.float32)
    point_total = jnp.zeros((C, C), jnp.float32)
    class_total = jnp.zeros((NCLS, C, C), jnp.float32)
    grads = []
    row_ids = jnp.arange(ROWS, dtype=jnp.int32)
    col_ids = jnp.arange(COLS, dtype=jnp.int32)
    position = ((row_ids % R)[:, None] * W_DEV + (col_ids % W_DEV)[None, :]).reshape(-1)
    for slide_index in range(SLIDES):
        slide_feats = features[slide_index]
        padded = jnp.pad(slide_feats, ((1, 1), (1, 1), (0, 0)))
        hidden = depthwise(padded, depth_weight, ROWS, COLS).astype(jnp.bfloat16)
        flat_hidden = hidden.reshape(ROWS * COLS, C)
        point_out = jnp.dot(flat_hidden, point_weight, preferred_element_type=jnp.float32).astype(jnp.bfloat16)
        tile_counts = jnp.repeat(jnp.repeat(valid_count[slide_index], R, axis=0), W_DEV, axis=1).reshape(-1)
        pixel_mask = (position < tile_counts).astype(jnp.float32)
        masked = point_out * pixel_mask[:, None].astype(jnp.bfloat16)
        second_sum = lax.dot_general(masked, point_out, (((0,), (0,)), ((), ())), preferred_element_type=jnp.float32)
        first_sum = lax.optimization_barrier(jnp.sum(masked.astype(jnp.float32), axis=0))
        pixel_count = jnp.sum(pixel_mask)
        pooled, pullback = jax.vjp(lambda second_in, first_in: cov_root(second_in, first_in, pixel_count), second_sum, first_sum)
        logits = jnp.tensordot(classifier, pooled, axes=([1, 2], [0, 1]), precision=lax.Precision.HIGHEST)
        log_peak = jnp.max(logits)
        log_total = log_peak + jnp.log(jnp.sum(jnp.exp(logits - log_peak)))
        class_probs = jnp.exp(logits - log_total)
        onehot = (jnp.arange(NCLS, dtype=jnp.int32) == labels[slide_index]).astype(jnp.float32)
        loss_total = loss_total + jnp.sum(onehot * (log_total - logits)) / SLIDES
        logit_slope = (class_probs - onehot) / SLIDES
        class_total = class_total + pooled[None] * logit_slope[:, None, None]
        back_pooled = jnp.tensordot(logit_slope, classifier, axes=(0, 0), precision=lax.Precision.HIGHEST)
        back_second, back_first = pullback(back_pooled)
        symmetric = back_second + back_second.T
        back_mapped = (pixel_mask[:, None] * (matmul_high(point_out.astype(jnp.float32), symmetric) + back_first[None, :])).astype(jnp.bfloat16)
        back_hidden = jnp.dot(back_mapped, point_weight.T, preferred_element_type=jnp.float32).astype(jnp.bfloat16)
        point_total = point_total + lax.dot_general(flat_hidden, back_mapped, (((0,), (0,)), ((), ())), preferred_element_type=jnp.float32)
        back_grid = back_hidden.reshape(ROWS, COLS, C)
        rows_list = []
        for offset_row in range(3):
            cols_list = []
            for offset_col in range(3):
                cols_list.append(lax.optimization_barrier(jnp.sum(padded[offset_row:offset_row + ROWS, offset_col:offset_col + COLS].astype(jnp.float32) * back_grid.astype(jnp.float32), axis=(0, 1))))
            rows_list.append(jnp.stack(cols_list))
        depth_total = depth_total + jnp.stack(rows_list)
        back_pad = jnp.pad(back_grid, ((1, 1), (1, 1), (0, 0)))
        feature_sum = jnp.zeros((ROWS, COLS, C), jnp.float32)
        for offset_row in range(3):
            for offset_col in range(3):
                feature_sum = feature_sum + back_pad[2 - offset_row:2 - offset_row + ROWS, 2 - offset_col:2 - offset_col + COLS].astype(jnp.float32) * depth_weight[offset_row, offset_col].astype(jnp.float32)
        grads.append(feature_sum.astype(jnp.bfloat16))
    return (loss_total, depth_total, point_total, class_total, jnp.stack(grads))
```

```python
import functools

import jax
import jax.numpy as jnp
from jax import lax
from jax.experimental import pallas as pl
from jax.experimental.pallas import tpu as pltpu
from jax.sharding import PartitionSpec as P

ITERS = 5
RIM = 2
LEFT = 8
LANES = 128
F32 = jnp.float32
BF16 = jnp.bfloat16
VMEM = pl.BlockSpec(memory_space=pltpu.VMEM)
SMEM = pl.BlockSpec(memory_space=pltpu.SMEM)
PARAMS = pltpu.CompilerParams(vmem_limit_bytes=40 * 1024 * 1024)


def iota(shape, dim):
    return lax.broadcasted_iota(jnp.int32, shape, dim)


def total(x):
    return jnp.sum(jnp.sum(x, axis=1, keepdims=True), axis=0, keepdims=True)


def dot(left, right):
    return jnp.dot(left, right, preferred_element_type=F32)


def split(x):
    high = x.astype(BF16)
    return high, (x - high.astype(F32)).astype(BF16)


def mm(left, right):
    lhs = jnp.concatenate([left[0], left[1], left[0]], axis=1)
    rhs = jnp.concatenate([right[0], right[0], right[1]], axis=0)
    return dot(lhs, rhs)


def stack(*pairs):
    return tuple(jnp.concatenate([pair[i] for pair in pairs], axis=0) for i in range(2))


def shifted(x, step):
    return pltpu.roll(x, step % x.shape[0], 0)


def tri_pack(full):
    half = full.shape[0] // 2
    row, col = iota((half, half), 0), iota((half, half), 1)
    first, upper, second = full[:half, :half], full[:half, half:], full[half:, half:]
    both = jnp.where(row <= col, first, second)
    diag = jnp.sum(jnp.where(row == col, second, 0.0), axis=0, keepdims=True)
    return upper, both, diag


def tri_unpack(upper, both, diag):
    half = both.shape[0]
    row, col = iota((half, half), 0), iota((half, half), 1)
    turned = both.T
    first = jnp.where(row <= col, both, turned)
    second = jnp.where(row > col, both, jnp.where(row == col, diag, turned))
    return jnp.concatenate(
        [jnp.concatenate([first, upper], axis=1), jnp.concatenate([upper.T, second], axis=1)],
        axis=0,
    )


def assemble(ext, tile, up, down, left, right):
    height, width, channels = tile.shape
    rows = height + 2 * RIM
    ext[:, 0:LEFT, :] = jnp.zeros((rows, LEFT, channels), F32)
    ext[:, LEFT + width : 2 * LEFT + width, :] = jnp.zeros((rows, LEFT, channels), F32)
    ext[RIM : RIM + height, LEFT : LEFT + width, :] = tile[...].astype(F32)
    ext[0:RIM, LEFT : LEFT + width, :] = up[...].astype(F32)
    ext[RIM + height : rows, LEFT : LEFT + width, :] = down[...].astype(F32)
    ext[:, LEFT - RIM : LEFT, :] = left[...].astype(F32)
    ext[:, LEFT + width : LEFT + width + RIM, :] = right[...].astype(F32)


def forward_kernel(
    planes, count, tile, up, down, left, right, weights, point, mapped, packed, ext, hidden, inner
):
    height, width, channels = tile.shape
    wide = ext.shape[1]
    assemble(ext, tile, up, down, left, right)
    valid = count[0]

    for lane in range(0, channels, LANES):
        part = slice(lane, lane + LANES)
        taps = [weights[k : k + 1, part] for k in range(9)]

        def body(r, carry, part=part, taps=taps):
            rows = [ext[r + a, :, part] for a in range(3)]
            cols = [sum(rows[a] * taps[3 * a + b] for a in range(3)) for b in range(3)]
            value = cols[1] + shifted(cols[0], 1) + shifted(cols[2], -1)
            hidden[pl.ds(pl.multiple_of(r * wide, 16), wide), part] = value.astype(BF16)

            @pl.when((r >= 1) & (r <= height))
            def _():
                raster = (r - 1) * width + iota((width, LANES), 0)
                kept = jnp.where(raster < valid, value[LEFT : LEFT + width], 0.0)
                start = pl.multiple_of((r - 1) * width, 16)
                inner[pl.ds(start, width), part] = kept.astype(BF16)

            return carry

        lax.fori_loop(0, height + 2, body, 0)

    mapped[...] = dot(hidden[...], point[...]).astype(BF16)
    kept = inner[...]
    gram = lax.dot_general(kept, kept, (((0,), (0,)), ((), ())), preferred_element_type=F32)
    sums = jnp.sum(kept.astype(F32), axis=0, keepdims=True)
    upper, both, diag = tri_pack(gram)
    chunks = packed.shape[1] // LANES
    spare = chunks * planes - 2 * LANES - 3
    flat = jnp.concatenate(
        [upper, both, diag, sums[:, :LANES], sums[:, LANES:], jnp.zeros((spare, LANES), F32)],
        axis=0,
    )
    for q in range(chunks):
        packed[:, q * LANES : (q + 1) * LANES] = flat[q * planes : (q + 1) * planes]


def plane_sum_kernel(count, terms, out):
    planes, lanes = terms.shape
    summed = jnp.sum(terms[...], axis=0, keepdims=True)
    out[:, :lanes] = jnp.broadcast_to(summed, (planes, lanes))
    out[:, lanes:] = jnp.full((planes, LANES), count[0].astype(F32))


def cov_kernel(
    grid_y, grid_x, slides, place, label, gathered, tile, up, down, left, right, weights, point,
    point_turned, classifier, mapped, gradient, sent, ext, back,
):
    height, width, channels = tile.shape
    planes = grid_y * grid_x
    wide = ext.shape[1]
    half = channels // 2
    chunks = gathered.shape[1] // LANES - 1
    pixels = (height + 2) * wide

    flat = jnp.concatenate(
        [gathered[:, q * LANES : (q + 1) * LANES] for q in range(chunks)], axis=0
    )
    counts = gathered[:, chunks * LANES : (chunks + 1) * LANES]
    inverse = 1.0 / jnp.sum(counts, axis=0, keepdims=True)[:, 0:1]
    gram = tri_unpack(flat[:half], flat[half : 2 * half], flat[2 * half : 2 * half + 1])
    sums = jnp.concatenate(
        [flat[2 * half + 1 : 2 * half + 2], flat[2 * half + 2 : 2 * half + 3]], axis=1
    )
    center = sums * inverse
    spread = jnp.broadcast_to(center, (channels, channels))
    moment = gram * inverse - spread * spread.T

    mixing, mixing_turned = point[...], point_turned[...]
    high, low = split(moment)
    moved = dot(
        jnp.concatenate([high, low], axis=1), jnp.concatenate([mixing, mixing], axis=0)
    )
    moved_pair = split(moved)
    sigma = dot(
        jnp.concatenate([mixing_turned, mixing_turned], axis=1),
        jnp.concatenate(moved_pair, axis=0),
    )
    sigma = 0.5 * (sigma + sigma.T)
    eye = iota((channels, channels), 0) == iota((channels, channels), 1)
    trace = total(jnp.where(eye, sigma, 0.0))
    start = sigma * (1.0 / trace)

    toward = classifier[0] - classifier[1]
    toward = toward + toward.T
    wmat, ymat, dw, dy = start, start, toward, toward
    for step in range(ITERS):
        w_pair, dw_pair = split(wmat), split(dw)
        if step == 0:
            square = mm(w_pair, w_pair)
            cross = mm(w_pair, dw_pair)
            yw, dyw = square, cross + cross.T
        else:
            first = mm(stack(w_pair, split(ymat), split(dy)), w_pair)
            second = mm(stack(w_pair, split(ymat)), dw_pair)
            square, yw = first[:channels], first[channels : 2 * channels]
            cross = second[:channels]
            dyw = first[2 * channels :] + second[channels:]
        ymat = 1.5 * ymat - 0.5 * yw
        dy = 1.5 * dy - 0.5 * dyw
        if step + 1 < ITERS:
            dsquare = cross + cross.T
            square_pair = split(square)
            third = mm(stack(square_pair, split(dsquare)), w_pair)
            cube = third[:channels]
            dcube = third[channels:] + mm(square_pair, dw_pair)
            wmat = 2.25 * wmat - 1.5 * square + 0.25 * cube
            dw = 2.25 * dw - 1.5 * dsquare + 0.25 * dcube

    root = jnp.sqrt(trace)
    pooled = root * ymat
    logit0 = total(classifier[0] * pooled)
    logit1 = total(classifier[1] * pooled)
    peak = jnp.maximum(logit0, logit1)
    lse = peak + jnp.log(jnp.exp(logit0 - peak) + jnp.exp(logit1 - peak))
    is_zero = label[0] == 0
    slope = jnp.where(is_zero, -jnp.exp(logit1 - lse), jnp.exp(logit0 - lse)) * (1.0 / slides)
    loss = (lse - jnp.where(is_zero, logit0, logit1)) * (1.0 / slides)

    level = 0.5 * total(toward * ymat) - total(dy * start)
    slant = (dy + jnp.where(eye, level, 0.0)) * (slope / root)
    slant = 0.5 * (slant + slant.T)
    point_term = mm(moved_pair, split(slant))
    class_term = slope * pooled
    class_term = 0.5 * (class_term + class_term.T)

    symmetric = slant * inverse
    sym_pair = split(symmetric)
    center_pair = split(jnp.broadcast_to(center, (8, channels)))
    mean = dot(
        jnp.concatenate(center_pair, axis=1), jnp.concatenate([mixing, mixing], axis=0)
    )
    offset = -mm(split(mean), sym_pair)[0:1]

    row_id = iota((planes, LANES), 0)
    spots = []
    for dy_ in (-1, 0, 1):
        for dx_ in (-1, 0, 1):
            near_y, near_x = place[0] + dy_, place[1] + dx_
            inside = (near_y >= 0) & (near_y < grid_y) & (near_x >= 0) & (near_x < grid_x)
            spot = jnp.where(inside, near_y * grid_x + near_x, -1)
            near = jnp.sum(jnp.where(row_id == spot, counts, 0.0), axis=0, keepdims=True)
            spots.append(near[:, 0:1])

    both = dot(mapped[...], sym_pair[0]) + dot(mapped[...], sym_pair[1]) + offset
    lane_col = iota((wide, channels), 0) - LEFT
    inner_col = jnp.where(lane_col < 0, lane_col + width, jnp.where(lane_col >= width, lane_col - width, lane_col))
    seen = (lane_col >= -1) & (lane_col <= width)
    limits = []
    for k in range(3):
        limit = jnp.where(
            lane_col < 0, spots[3 * k], jnp.where(lane_col >= width, spots[3 * k + 2], spots[3 * k + 1])
        )
        limits.append(jnp.where(seen, limit, -1.0))
    pieces = []
    for r in range(height + 2):
        tile_row = (r - 1) % height
        limit = limits[0 if r == 0 else (2 if r == height + 1 else 1)]
        raster = (tile_row * width + inner_col).astype(F32)
        pieces.append(jnp.where(raster < limit, both[r * wide : (r + 1) * wide], 0.0).astype(BF16))
    back_mapped = jnp.concatenate(pieces, axis=0)
    back_hidden = dot(back_mapped, mixing_turned).astype(BF16)
    back[...] = back_hidden.astype(F32).reshape(height + 2, wide, channels)

    assemble(ext, tile, up, down, left, right)
    depth = []
    for lane in range(0, channels, LANES):
        part = slice(lane, lane + LANES)
        taps = [weights[k : k + 1, part] for k in range(9)]
        column = iota((wide, LANES), 0)
        within = (column >= LEFT) & (column < LEFT + width)

        def body(i, sums, part=part, taps=taps, within=within):
            rows = [back[i + a, :, part] for a in range(3)]
            cols = [sum(rows[2 - a] * taps[3 * a + b] for a in range(3)) for b in range(3)]
            value = cols[1] + shifted(cols[0], -1) + shifted(cols[2], 1)
            gradient[i, :, part] = value[LEFT : LEFT + width].astype(BF16)
            own = jnp.where(within, rows[1], 0.0)
            moved_own = [shifted(own, -1), own, shifted(own, 1)]
            feats = [ext[i + 1 + a, :, part] for a in range(3)]
            out = []
            for a in range(3):
                for b in range(3):
                    product = (feats[a] * moved_own[b]).reshape(wide // 8, 8, LANES)
                    out.append(sums[3 * a + b] + jnp.sum(product, axis=0))
            return tuple(out)

        sums = lax.fori_loop(
            0, height, body, tuple(jnp.zeros((8, LANES), F32) for _ in range(9))
        )
        depth.append(
            jnp.concatenate([jnp.sum(s, axis=0, keepdims=True) for s in sums], axis=0)
        )
    depth = jnp.concatenate(depth, axis=1)

    upper, tri, diag = tri_pack(class_term)
    class_flat = jnp.concatenate([upper, tri], axis=0)
    scale = 1.0 / planes
    extra = jnp.concatenate([diag, jnp.broadcast_to(loss, (1, half))], axis=1) * scale
    small = jnp.concatenate([depth, extra, jnp.zeros((6, channels), F32)], axis=0)
    rp, rc, rd = channels // slides, channels // slides // 2, 16 // slides
    for k in range(slides):
        sent[k, 0:rp, :] = point_term[k * rp : (k + 1) * rp]
        sent[k, rp : rp + rc, 0:half] = class_flat[k * rp : k * rp + rc]
        sent[k, rp : rp + rc, half:channels] = class_flat[k * rp + rc : (k + 1) * rp]
        sent[k, rp + rc : rp + rc + 8, :] = jnp.concatenate(
            [small[k * rd : (k + 1) * rd], jnp.zeros((8 - rd, channels), F32)], axis=0
        ) if rd < 8 else small[k * rd : (k + 1) * rd]


def slide_sum_kernel(rd, terms, shares, spread):
    planes = spread.shape[0]
    slides, rows, channels = terms.shape
    summed = terms[0]
    for k in range(1, slides):
        summed = summed + terms[k]
    shares[...] = summed[: rows - 8]
    tail = summed[rows - 8 : rows]
    for q in range(rd):
        spread[:, q * channels : (q + 1) * channels] = jnp.broadcast_to(
            tail[q : q + 1], (planes, channels)
        )


def join_kernel(shares, spread, out):
    slides, rows, channels = out.shape
    rd = spread.shape[1] // channels
    summed = jnp.sum(spread[...], axis=0, keepdims=True)
    tail = [summed[:, q * channels : (q + 1) * channels] for q in range(rd)]
    if rd < 8:
        tail.append(jnp.zeros((8 - rd, channels), F32))
    tail = jnp.concatenate(tail, axis=0)
    for k in range(slides):
        out[k, 0 : rows - 8, :] = shares[...]
        out[k, rows - 8 : rows, :] = tail


def finish_kernel(terms, loss, depth, point, classes):
    slides, rows, channels = terms.shape
    half = channels // 2
    rp, rc, rd = channels // slides, channels // slides // 2, 16 // slides
    flat, small = [], []
    for k in range(slides):
        point[k * rp : (k + 1) * rp, :] = terms[k, 0:rp, :]
        flat += [terms[k, rp : rp + rc, 0:half], terms[k, rp : rp + rc, half:channels]]
        small.append(terms[k, rp + rc : rp + rc + rd, :])
    flat = jnp.concatenate(flat, axis=0)
    small = jnp.concatenate(small, axis=0)
    full = tri_unpack(flat[:half], flat[half:], small[9:10, :half])
    classes[0] = full
    classes[1] = -full
    for a in range(3):
        depth[a] = small[3 * a : 3 * a + 3]
    loss[...] = small[9:10, half : half + 1]


def per_device(features, depth_weight, point_weight, classifier, valid_count, labels):
    slides, grid_y, grid_x = (lax.axis_size(axis) for axis in ("slide", "gy", "gx"))
    planes = grid_y * grid_x
    tile = features[0]
    height, width, channels = tile.shape
    wide = width + 2 * LEFT

    def edges(low_part, high_part, axis):
        forward = [(i, i + 1) for i in range(lax.axis_size(axis) - 1)]
        backward = [(target, source) for source, target in forward]
        return lax.ppermute(high_part, axis, forward), lax.ppermute(low_part, axis, backward)

    up, down = edges(tile[:RIM], tile[height - RIM :], "gy")

    def strip(start):
        return jnp.concatenate([part[:, start : start + RIM] for part in (up, tile, down)], axis=0)

    left, right = edges(strip(0), strip(width - RIM), "gx")

    weights = depth_weight.reshape(9, channels).astype(F32)
    point_turned = point_weight.T
    count = valid_count.reshape(1)
    place = jnp.stack([lax.axis_index("gy"), lax.axis_index("gx")]).astype(jnp.int32)
    halo = (tile, up, down, left, right)
    chunks = -(-(channels + 3) // planes)

    mapped, packed = pl.pallas_call(
        functools.partial(forward_kernel, planes),
        out_shape=(
            jax.ShapeDtypeStruct(((height + 2) * wide, channels), BF16),
            jax.ShapeDtypeStruct((planes, chunks * LANES), F32),
        ),
        in_specs=[SMEM] + [VMEM] * 7,
        out_specs=(VMEM, VMEM),
        scratch_shapes=[
            pltpu.VMEM((height + 2 * RIM, wide, channels), F32),
            pltpu.VMEM(((height + 2) * wide, channels), BF16),
            pltpu.VMEM((height * width, channels), BF16),
        ],
        compiler_params=PARAMS,
        name="forward",
    )(count, *halo, weights, point_weight)

    packed = lax.all_to_all(packed, ("gy", "gx"), 0, 0)
    packed = pl.pallas_call(
        plane_sum_kernel,
        out_shape=jax.ShapeDtypeStruct((planes, (chunks + 1) * LANES), F32),
        in_specs=[SMEM, VMEM],
        out_specs=VMEM,
        name="plane_sum",
    )(count, packed)
    gathered = lax.all_to_all(packed, ("gy", "gx"), 0, 0)

    rp, rd = channels // slides, 16 // slides
    rows = rp + rp // 2 + 8
    gradient, sent = pl.pallas_call(
        functools.partial(cov_kernel, grid_y, grid_x, slides),
        out_shape=(
            jax.ShapeDtypeStruct((height, width, channels), BF16),
            jax.ShapeDtypeStruct((slides, rows, channels), F32),
        ),
        in_specs=[SMEM, SMEM] + [VMEM] * 11,
        out_specs=(VMEM, VMEM),
        scratch_shapes=[
            pltpu.VMEM((height + 2 * RIM, wide, channels), F32),
            pltpu.VMEM((height + 2, wide, channels), F32),
        ],
        compiler_params=PARAMS,
        name="covariance",
    )(place, labels, gathered, *halo, weights, point_weight, point_turned, classifier, mapped)

    received = lax.all_to_all(sent, "slide", 0, 0)
    shares, spread = pl.pallas_call(
        functools.partial(slide_sum_kernel, rd),
        out_shape=(
            jax.ShapeDtypeStruct((rows - 8, channels), F32),
            jax.ShapeDtypeStruct((planes, rd * channels), F32),
        ),
        in_specs=[VMEM],
        out_specs=(VMEM, VMEM),
        name="slide_sum",
    )(received)
    spread = lax.all_to_all(spread, ("gy", "gx"), 0, 0)
    joined = pl.pallas_call(
        join_kernel,
        out_shape=jax.ShapeDtypeStruct((slides, rows, channels), F32),
        in_specs=[VMEM, VMEM],
        out_specs=VMEM,
        name="join",
    )(shares, spread)
    joined = lax.all_to_all(joined, "slide", 0, 0)
    loss, depth, point, classes = pl.pallas_call(
        finish_kernel,
        out_shape=(
            jax.ShapeDtypeStruct((1, 1), F32),
            jax.ShapeDtypeStruct((3, 3, channels), F32),
            jax.ShapeDtypeStruct((channels, channels), F32),
            jax.ShapeDtypeStruct(classifier.shape, F32),
        ),
        in_specs=[VMEM],
        out_specs=(VMEM, VMEM, VMEM, VMEM),
        name="finish",
    )(joined)
    return loss.reshape(()), depth, point, classes, gradient[None]


def solution(mesh):
    placed = (P("slide", "gy", "gx", None), P(), P(), P(), P("slide", "gy", "gx"), P("slide"))
    return jax.shard_map(
        per_device,
        mesh=mesh,
        in_specs=placed,
        out_specs=(P(), P(), P(), P(), P("slide", "gy", "gx", None)),
        check_vma=False,
    )
```

```python
import functools

import jax
import jax.numpy as jnp
from jax import lax
from jax.experimental import pallas as pl
from jax.experimental.pallas import tpu as pltpu
from jax.sharding import PartitionSpec as P

ITERS = 5
RIM = 2
LEFT = 8
LANES = 128
F32 = jnp.float32
BF16 = jnp.bfloat16
VMEM = pl.BlockSpec(memory_space=pltpu.VMEM)
SMEM = pl.BlockSpec(memory_space=pltpu.SMEM)
PARAMS = pltpu.CompilerParams(vmem_limit_bytes=24 * 1024 * 1024)


def iota(shape, dim):
    return lax.broadcasted_iota(jnp.int32, shape, dim)


def total(x):
    return jnp.sum(jnp.sum(x, axis=1, keepdims=True), axis=0, keepdims=True)


def dot(left, right):
    return jnp.dot(left, right, preferred_element_type=F32)


def split(x):
    high = x.astype(BF16)
    return high, (x - high.astype(F32)).astype(BF16)


def mm(left, right):
    lhs = jnp.concatenate([left[0], left[1], left[0]], axis=1)
    rhs = jnp.concatenate([right[0], right[0], right[1]], axis=0)
    return dot(lhs, rhs)


def stack(*pairs):
    return tuple(jnp.concatenate([pair[i] for pair in pairs], axis=0) for i in range(2))


def shifted(x, step):
    return pltpu.roll(x, step % x.shape[0], 0)


def tri_pack(full):
    half = full.shape[0] // 2
    row, col = iota((half, half), 0), iota((half, half), 1)
    first, upper, second = full[:half, :half], full[:half, half:], full[half:, half:]
    both = jnp.where(row <= col, first, second)
    diag = jnp.sum(jnp.where(row == col, second, 0.0), axis=0, keepdims=True)
    return upper, both, diag


def tri_unpack(upper, both, diag):
    half = both.shape[0]
    row, col = iota((half, half), 0), iota((half, half), 1)
    turned = both.T
    first = jnp.where(row <= col, both, turned)
    second = jnp.where(row > col, both, jnp.where(row == col, diag, turned))
    return jnp.concatenate(
        [jnp.concatenate([first, upper], axis=1), jnp.concatenate([upper.T, second], axis=1)],
        axis=0,
    )


def assemble(ext, tile, up, down, left, right):
    height, width, channels = tile.shape
    rows = height + 2 * RIM
    ext[:, 0:LEFT, :] = jnp.zeros((rows, LEFT, channels), F32)
    ext[:, LEFT + width : 2 * LEFT + width, :] = jnp.zeros((rows, LEFT, channels), F32)
    ext[RIM : RIM + height, LEFT : LEFT + width, :] = tile[...].astype(F32)
    ext[0:RIM, LEFT : LEFT + width, :] = up[...].astype(F32)
    ext[RIM + height : rows, LEFT : LEFT + width, :] = down[...].astype(F32)
    ext[:, LEFT - RIM : LEFT, :] = left[...].astype(F32)
    ext[:, LEFT + width : LEFT + width + RIM, :] = right[...].astype(F32)


def forward_kernel(
    planes, count, tile, up, down, left, right, weights, hidden, packed, ext, inner
):
    height, width, channels = tile.shape
    wide = ext.shape[1]
    assemble(ext, tile, up, down, left, right)
    valid = count[0]

    for lane in range(0, channels, LANES):
        part = slice(lane, lane + LANES)
        taps = [weights[k : k + 1, part] for k in range(9)]

        def body(r, carry, part=part, taps=taps):
            rows = [ext[r + a, :, part] for a in range(3)]
            cols = [sum(rows[a] * taps[3 * a + b] for a in range(3)) for b in range(3)]
            value = cols[1] + shifted(cols[0], 1) + shifted(cols[2], -1)
            hidden[pl.ds(pl.multiple_of(r * wide, 16), wide), part] = value.astype(BF16)

            @pl.when((r >= 1) & (r <= height))
            def _():
                raster = (r - 1) * width + iota((width, LANES), 0)
                kept = jnp.where(raster < valid, value[LEFT : LEFT + width], 0.0)
                start = pl.multiple_of((r - 1) * width, 16)
                inner[pl.ds(start, width), part] = kept.astype(BF16)

            return carry

        lax.fori_loop(0, height + 2, body, 0)

    kept = inner[...]
    gram = lax.dot_general(kept, kept, (((0,), (0,)), ((), ())), preferred_element_type=F32)
    sums = jnp.sum(kept.astype(F32), axis=0, keepdims=True)
    upper, both, diag = tri_pack(gram)
    chunks = packed.shape[1] - 1
    spare = chunks * planes - 2 * LANES - 3
    flat = jnp.concatenate(
        [upper, both, diag, sums[:, :LANES], sums[:, LANES:], jnp.zeros((spare, LANES), F32)],
        axis=0,
    )
    for q in range(chunks):
        packed[:, q, :] = flat[q * planes : (q + 1) * planes]
    packed[:, chunks, :] = jnp.zeros((planes, LANES), F32)


def plane_sum_kernel(count, terms, out):
    planes, rows, lanes = terms.shape
    summed = jnp.sum(terms[...], axis=0)
    valid = jnp.full((rows, lanes), count[0].astype(F32))
    summed = jnp.where(iota((rows, lanes), 0) == rows - 1, valid, summed)
    out[...] = jnp.broadcast_to(summed[None], out.shape)


def prepare_kernel(
    hidden, point, tile, up, down, left, right, classifier, mapped, ext, toward
):
    mapped[...] = dot(hidden[...], point[...]).astype(BF16)
    assemble(ext, tile, up, down, left, right)
    gap = classifier[0] - classifier[1]
    toward[...] = gap + gap.T


def cov_kernel(
    grid_y, grid_x, slides, place, label, gathered, ext, mapped, toward_ref, point, point_turned,
    classifier, back, sent,
):
    planes = grid_y * grid_x
    wide, channels = ext.shape[1:]
    height, width = ext.shape[0] - 2 * RIM, wide - 2 * LEFT
    half = channels // 2
    chunks = gathered.shape[1] - 1

    flat = jnp.concatenate([gathered[:, q, :] for q in range(chunks)], axis=0)
    counts = gathered[:, chunks, :]
    inverse = 1.0 / jnp.sum(counts, axis=0, keepdims=True)[:, 0:1]
    gram = tri_unpack(flat[:half], flat[half : 2 * half], flat[2 * half : 2 * half + 1])
    sums = jnp.concatenate(
        [flat[2 * half + 1 : 2 * half + 2], flat[2 * half + 2 : 2 * half + 3]], axis=1
    )
    center = sums * inverse
    spread = jnp.broadcast_to(center, (channels, channels))
    moment = gram * inverse - spread * spread.T

    mixing, mixing_turned = point[...], point_turned[...]
    high, low = split(moment)
    moved = dot(
        jnp.concatenate([high, low], axis=1), jnp.concatenate([mixing, mixing], axis=0)
    )
    moved_pair = split(moved)
    sigma = dot(
        jnp.concatenate([mixing_turned, mixing_turned], axis=1),
        jnp.concatenate(moved_pair, axis=0),
    )
    sigma = 0.5 * (sigma + sigma.T)
    eye = iota((channels, channels), 0) == iota((channels, channels), 1)
    trace = total(jnp.where(eye, sigma, 0.0))
    start = sigma * (1.0 / trace)

    toward = toward_ref[...]
    wmat, ymat, dw, dy = start, start, toward, toward
    for step in range(ITERS):
        w_pair, dw_pair = split(wmat), split(dw)
        if step == 0:
            square = mm(w_pair, w_pair)
            cross = mm(w_pair, dw_pair)
            yw, dyw = square, cross + cross.T
        else:
            first = mm(stack(w_pair, split(ymat), split(dy)), w_pair)
            second = mm(stack(w_pair, split(ymat)), dw_pair)
            square, yw = first[:channels], first[channels : 2 * channels]
            cross = second[:channels]
            dyw = first[2 * channels :] + second[channels:]
        ymat = 1.5 * ymat - 0.5 * yw
        dy = 1.5 * dy - 0.5 * dyw
        if step + 1 < ITERS:
            dsquare = cross + cross.T
            square_pair = split(square)
            third = mm(stack(square_pair, split(dsquare)), w_pair)
            cube = third[:channels]
            dcube = third[channels:] + mm(square_pair, dw_pair)
            wmat = 2.25 * wmat - 1.5 * square + 0.25 * cube
            dw = 2.25 * dw - 1.5 * dsquare + 0.25 * dcube

    root = jnp.sqrt(trace)
    pooled = root * ymat
    logit0 = total(classifier[0] * pooled)
    logit1 = total(classifier[1] * pooled)
    peak = jnp.maximum(logit0, logit1)
    lse = peak + jnp.log(jnp.exp(logit0 - peak) + jnp.exp(logit1 - peak))
    is_zero = label[0] == 0
    slope = jnp.where(is_zero, -jnp.exp(logit1 - lse), jnp.exp(logit0 - lse)) * (1.0 / slides)
    loss = (lse - jnp.where(is_zero, logit0, logit1)) * (1.0 / slides)

    level = 0.5 * total(toward * ymat) - total(dy * start)
    slant = (dy + jnp.where(eye, level, 0.0)) * (slope / root)
    slant = 0.5 * (slant + slant.T)
    point_term = mm(moved_pair, split(slant))
    class_term = slope * pooled
    class_term = 0.5 * (class_term + class_term.T)

    symmetric = slant * inverse
    sym_pair = split(symmetric)
    center_pair = split(jnp.broadcast_to(center, (8, channels)))
    mean = dot(
        jnp.concatenate(center_pair, axis=1), jnp.concatenate([mixing, mixing], axis=0)
    )
    offset = -mm(split(mean), sym_pair)[0:1]

    row_id = iota((planes, LANES), 0)
    spots = []
    for dy_ in (-1, 0, 1):
        for dx_ in (-1, 0, 1):
            near_y, near_x = place[0] + dy_, place[1] + dx_
            inside = (near_y >= 0) & (near_y < grid_y) & (near_x >= 0) & (near_x < grid_x)
            spot = jnp.where(inside, near_y * grid_x + near_x, -1)
            near = jnp.sum(jnp.where(row_id == spot, counts, 0.0), axis=0, keepdims=True)
            spots.append(near[:, 0:1])

    both = dot(mapped[...], sym_pair[0]) + dot(mapped[...], sym_pair[1]) + offset
    lane_col = iota((wide, channels), 0) - LEFT
    inner_col = jnp.where(lane_col < 0, lane_col + width, jnp.where(lane_col >= width, lane_col - width, lane_col))
    seen = (lane_col >= -1) & (lane_col <= width)
    limits = []
    for k in range(3):
        limit = jnp.where(
            lane_col < 0, spots[3 * k], jnp.where(lane_col >= width, spots[3 * k + 2], spots[3 * k + 1])
        )
        limits.append(jnp.where(seen, limit, -1.0))
    pieces = []
    for r in range(height + 2):
        tile_row = (r - 1) % height
        limit = limits[0 if r == 0 else (2 if r == height + 1 else 1)]
        raster = (tile_row * width + inner_col).astype(F32)
        pieces.append(jnp.where(raster < limit, both[r * wide : (r + 1) * wide], 0.0).astype(BF16))
    back_mapped = jnp.concatenate(pieces, axis=0)
    back_hidden = dot(back_mapped, mixing_turned).astype(BF16)
    back[...] = back_hidden.astype(F32).reshape(height + 2, wide, channels)

    depth = []
    for lane in range(0, channels, LANES):
        part = slice(lane, lane + LANES)
        column = iota((wide, LANES), 0)
        within = (column >= LEFT) & (column < LEFT + width)

        def body(i, sums, part=part, within=within):
            own = jnp.where(within, back[i + 1, :, part], 0.0)
            moved_own = [shifted(own, -1), own, shifted(own, 1)]
            feats = [ext[i + 1 + a, :, part] for a in range(3)]
            out = []
            for a in range(3):
                for b in range(3):
                    product = (feats[a] * moved_own[b]).reshape(wide // 8, 8, LANES)
                    out.append(sums[3 * a + b] + jnp.sum(product, axis=0))
            return tuple(out)

        sums = lax.fori_loop(
            0, height, body, tuple(jnp.zeros((8, LANES), F32) for _ in range(9))
        )
        depth.append(
            jnp.concatenate([jnp.sum(s, axis=0, keepdims=True) for s in sums], axis=0)
        )
    depth = jnp.concatenate(depth, axis=1)

    upper, tri, diag = tri_pack(class_term)
    class_flat = jnp.concatenate([upper, tri], axis=0)
    scale = 1.0 / planes
    extra = jnp.concatenate([diag, jnp.broadcast_to(loss, (1, half))], axis=1) * scale
    small = jnp.concatenate([depth, extra, jnp.zeros((6, channels), F32)], axis=0)
    rp, rc, rd = channels // slides, channels // slides // 2, 16 // slides
    pad = [jnp.zeros((8 - rd, channels), F32)] if rd < 8 else []
    for k in range(slides):
        sent[k, 0:rp, :] = point_term[k * rp : (k + 1) * rp]
        sent[k, rp : rp + rc, 0:half] = class_flat[k * rp : k * rp + rc]
        sent[k, rp : rp + rc, half:channels] = class_flat[k * rp + rc : (k + 1) * rp]
        sent[k, rp + rc : rp + rc + 8, :] = jnp.concatenate(
            [small[k * rd : (k + 1) * rd]] + pad, axis=0
        )


def spread_kernel(back, weights, gradient):
    height, width, channels = gradient.shape
    for lane in range(0, channels, LANES):
        part = slice(lane, lane + LANES)
        taps = [weights[k : k + 1, part] for k in range(9)]

        def body(i, carry, part=part, taps=taps):
            rows = [back[i + a, :, part] for a in range(3)]
            cols = [sum(rows[2 - a] * taps[3 * a + b] for a in range(3)) for b in range(3)]
            value = cols[1] + shifted(cols[0], -1) + shifted(cols[2], 1)
            gradient[i, :, part] = value[LEFT : LEFT + width].astype(BF16)
            return carry

        lax.fori_loop(0, height, body, 0)


def slide_sum_kernel(rd, terms, shares, spread):
    slides, rows, channels = terms.shape
    main = rows - 8
    summed = terms[0]
    for k in range(1, slides):
        summed = summed + terms[k]
    shares[...] = summed[:main].astype(BF16)
    tail = summed[main : main + rd]
    lines = jnp.concatenate(
        [tail[q : q + 1, p : p + LANES] for q in range(rd) for p in range(0, channels, LANES)],
        axis=0,
    )
    spread[...] = jnp.broadcast_to(lines[None], spread.shape)


def join_kernel(shares, spread, out):
    slides, rows, channels = out.shape
    summed = jnp.sum(spread[...], axis=0)
    per = channels // LANES
    rd = summed.shape[0] // per
    tail = jnp.concatenate(
        [
            jnp.concatenate([summed[per * q + p : per * q + p + 1] for p in range(per)], axis=1)
            for q in range(rd)
        ],
        axis=0,
    )
    high, low = split(tail)
    tail = jnp.concatenate([high, low, jnp.zeros((16 - 2 * rd, channels), BF16)], axis=0)
    for k in range(slides):
        out[k, 0 : rows - 16, :] = shares[...]
        out[k, rows - 16 : rows, :] = tail


def finish_kernel(terms, loss, depth, point, classes):
    slides, rows, channels = terms.shape
    half = channels // 2
    rp, rc, rd = channels // slides, channels // slides // 2, 16 // slides
    flat, small = [], []
    for k in range(slides):
        piece = terms[k].astype(F32)
        point[k * rp : (k + 1) * rp, :] = piece[:rp]
        flat += [piece[rp : rp + rc, :half], piece[rp : rp + rc, half:]]
        tail = piece[rp + rc :]
        small.append(tail[:rd] + tail[rd : 2 * rd])
    flat = jnp.concatenate(flat, axis=0)
    small = jnp.concatenate(small, axis=0)
    full = tri_unpack(flat[:half], flat[half:], small[9:10, :half])
    classes[0] = full
    classes[1] = -full
    for a in range(3):
        depth[a] = small[3 * a : 3 * a + 3]
    loss[...] = small[9:10, half : half + 1]


def per_device(features, depth_weight, point_weight, classifier, valid_count, labels):
    slides, grid_y, grid_x = (lax.axis_size(axis) for axis in ("slide", "gy", "gx"))
    planes = grid_y * grid_x
    tile = features[0]
    height, width, channels = tile.shape
    wide = width + 2 * LEFT

    def edges(low_part, high_part, axis):
        forward = [(i, i + 1) for i in range(lax.axis_size(axis) - 1)]
        backward = [(target, source) for source, target in forward]
        return lax.ppermute(high_part, axis, forward), lax.ppermute(low_part, axis, backward)

    up, down = edges(tile[:RIM], tile[height - RIM :], "gy")

    def strip(start):
        return jnp.concatenate([part[:, start : start + RIM] for part in (up, tile, down)], axis=0)

    left, right = edges(strip(0), strip(width - RIM), "gx")

    weights = depth_weight.reshape(9, channels).astype(F32)
    point_turned = point_weight.T
    count = valid_count.reshape(1)
    place = jnp.stack([lax.axis_index("gy"), lax.axis_index("gx")]).astype(jnp.int32)
    halo = (tile, up, down, left, right)
    chunks = -(-(channels + 3) // planes)

    pixels = (height + 2) * wide
    ext_shape = (height + 2 * RIM, wide, channels)

    hidden, packed = pl.pallas_call(
        functools.partial(forward_kernel, planes),
        out_shape=(
            jax.ShapeDtypeStruct((pixels, channels), BF16),
            jax.ShapeDtypeStruct((planes, chunks + 1, LANES), F32),
        ),
        in_specs=[SMEM] + [VMEM] * 6,
        out_specs=(VMEM, VMEM),
        scratch_shapes=[pltpu.VMEM(ext_shape, F32), pltpu.VMEM((height * width, channels), BF16)],
        compiler_params=PARAMS,
        name="forward",
    )(count, *halo, weights)

    packed = lax.all_to_all(packed, ("gy", "gx"), 0, 0)

    mapped, ext, toward = pl.pallas_call(
        prepare_kernel,
        out_shape=(
            jax.ShapeDtypeStruct((pixels, channels), BF16),
            jax.ShapeDtypeStruct(ext_shape, F32),
            jax.ShapeDtypeStruct((channels, channels), F32),
        ),
        in_specs=[VMEM] * 8,
        out_specs=(VMEM, VMEM, VMEM),
        compiler_params=PARAMS,
        cost_estimate=pl.CostEstimate(
            flops=2 * pixels * channels * channels, bytes_accessed=5 << 20, transcendentals=0
        ),
        name="prepare",
    )(hidden, point_weight, *halo, classifier)

    packed = pl.pallas_call(
        plane_sum_kernel,
        out_shape=jax.ShapeDtypeStruct((planes, chunks + 1, LANES), F32),
        in_specs=[SMEM, VMEM],
        out_specs=VMEM,
        name="plane_sum",
    )(count, packed)
    gathered = lax.all_to_all(packed, ("gy", "gx"), 0, 0)

    rp, rd = channels // slides, 16 // slides
    main = rp + rp // 2
    back, sent = pl.pallas_call(
        functools.partial(cov_kernel, grid_y, grid_x, slides),
        out_shape=(
            jax.ShapeDtypeStruct((height + 2, wide, channels), F32),
            jax.ShapeDtypeStruct((slides, main + 8, channels), F32),
        ),
        in_specs=[SMEM, SMEM] + [VMEM] * 7,
        out_specs=(VMEM, VMEM),
        compiler_params=PARAMS,
        name="covariance",
    )(place, labels, gathered, ext, mapped, toward, point_weight, point_turned, classifier)

    received = lax.all_to_all(sent, "slide", 0, 0)
    gradient = pl.pallas_call(
        spread_kernel,
        out_shape=jax.ShapeDtypeStruct((height, width, channels), BF16),
        in_specs=[VMEM, VMEM],
        out_specs=VMEM,
        compiler_params=PARAMS,
        cost_estimate=pl.CostEstimate(
            flops=20 * pixels * channels, bytes_accessed=4 << 20, transcendentals=0
        ),
        name="spread",
    )(back, weights)
    shares, spread = pl.pallas_call(
        functools.partial(slide_sum_kernel, rd),
        out_shape=(
            jax.ShapeDtypeStruct((main, channels), BF16),
            jax.ShapeDtypeStruct((planes, rd * channels // LANES, LANES), F32),
        ),
        in_specs=[VMEM],
        out_specs=(VMEM, VMEM),
        name="slide_sum",
    )(received)
    spread = lax.all_to_all(spread, ("gy", "gx"), 0, 0)
    joined = pl.pallas_call(
        join_kernel,
        out_shape=jax.ShapeDtypeStruct((slides, main + 16, channels), BF16),
        in_specs=[VMEM, VMEM],
        out_specs=VMEM,
        name="join",
    )(shares, spread)
    joined = lax.all_to_all(joined, "slide", 0, 0)
    loss, depth, point, classes = pl.pallas_call(
        finish_kernel,
        out_shape=(
            jax.ShapeDtypeStruct((1, 1), F32),
            jax.ShapeDtypeStruct((3, 3, channels), F32),
            jax.ShapeDtypeStruct((channels, channels), F32),
            jax.ShapeDtypeStruct(classifier.shape, F32),
        ),
        in_specs=[VMEM],
        out_specs=(VMEM, VMEM, VMEM, VMEM),
        name="finish",
    )(joined)
    return loss.reshape(()), depth, point, classes, gradient[None]


def solution(mesh):
    placed = (P("slide", "gy", "gx", None), P(), P(), P(), P("slide", "gy", "gx"), P("slide"))
    return jax.shard_map(
        per_device,
        mesh=mesh,
        in_specs=placed,
        out_specs=(P(), P(), P(), P(), P("slide", "gy", "gx", None)),
        check_vma=False,
    )
```

```python
import functools

import jax
import jax.numpy as jnp
from jax import lax
from jax.experimental import pallas as pl
from jax.experimental.pallas import tpu as pltpu
from jax.sharding import PartitionSpec as P

ITERS = 5
RIM = 2
LEFT = 8
LANES = 128
F32 = jnp.float32
BF16 = jnp.bfloat16
VMEM = pl.BlockSpec(memory_space=pltpu.VMEM)
SMEM = pl.BlockSpec(memory_space=pltpu.SMEM)
PARAMS = pltpu.CompilerParams(vmem_limit_bytes=16 * 1024 * 1024)
SMALL = pltpu.CompilerParams(vmem_limit_bytes=4 * 1024 * 1024)


def iota(shape, dim):
    return lax.broadcasted_iota(jnp.int32, shape, dim)


def total(x):
    return jnp.sum(jnp.sum(x, axis=1, keepdims=True), axis=0, keepdims=True)


def dot(left, right):
    return jnp.dot(left, right, preferred_element_type=F32)


def split(x):
    high = x.astype(BF16)
    return high, (x - high.astype(F32)).astype(BF16)


def mm(left, right):
    lhs = jnp.concatenate([left[0], left[1], left[0]], axis=1)
    rhs = jnp.concatenate([right[0], right[0], right[1]], axis=0)
    return dot(lhs, rhs)


def stack(*pairs):
    return tuple(jnp.concatenate([pair[i] for pair in pairs], axis=0) for i in range(2))


def shifted(x, step):
    return pltpu.roll(x, step % x.shape[0], 0)


def tri_pack(full):
    half = full.shape[0] // 2
    row, col = iota((half, half), 0), iota((half, half), 1)
    first, upper, second = full[:half, :half], full[:half, half:], full[half:, half:]
    both = jnp.where(row <= col, first, second)
    diag = jnp.sum(jnp.where(row == col, second, 0.0), axis=0, keepdims=True)
    return upper, both, diag


def tri_unpack(upper, both, diag):
    half = both.shape[0]
    row, col = iota((half, half), 0), iota((half, half), 1)
    turned = both.T
    first = jnp.where(row <= col, both, turned)
    second = jnp.where(row > col, both, jnp.where(row == col, diag, turned))
    return jnp.concatenate(
        [jnp.concatenate([first, upper], axis=1), jnp.concatenate([upper.T, second], axis=1)],
        axis=0,
    )


def assemble(ext, tile, up, down, left, right):
    height, width, channels = tile.shape
    rows = height + 2 * RIM
    ext[:, 0:LEFT, :] = jnp.zeros((rows, LEFT, channels), F32)
    ext[:, LEFT + width : 2 * LEFT + width, :] = jnp.zeros((rows, LEFT, channels), F32)
    ext[RIM : RIM + height, LEFT : LEFT + width, :] = tile[...].astype(F32)
    ext[0:RIM, LEFT : LEFT + width, :] = up[...].astype(F32)
    ext[RIM + height : rows, LEFT : LEFT + width, :] = down[...].astype(F32)
    ext[:, LEFT - RIM : LEFT, :] = left[...].astype(F32)
    ext[:, LEFT + width : LEFT + width + RIM, :] = right[...].astype(F32)


def forward_kernel(
    planes, count, tile, up, down, left, right, weights, hidden, packed, ext, inner
):
    height, width, channels = tile.shape
    wide = ext.shape[1]
    assemble(ext, tile, up, down, left, right)
    valid = count[0]

    for lane in range(0, channels, LANES):
        part = slice(lane, lane + LANES)
        taps = [weights[k // 3, k % 3 : k % 3 + 1, part].astype(F32) for k in range(9)]

        def body(r, carry, part=part, taps=taps):
            rows = [ext[r + a, :, part] for a in range(3)]
            cols = [sum(rows[a] * taps[3 * a + b] for a in range(3)) for b in range(3)]
            value = cols[1] + shifted(cols[0], 1) + shifted(cols[2], -1)
            hidden[pl.ds(pl.multiple_of(r * wide, 16), wide), part] = value.astype(BF16)

            @pl.when((r >= 1) & (r <= height))
            def _():
                raster = (r - 1) * width + iota((width, LANES), 0)
                kept = jnp.where(raster < valid, value[LEFT : LEFT + width], 0.0)
                start = pl.multiple_of((r - 1) * width, 16)
                inner[pl.ds(start, width), part] = kept.astype(BF16)

            return carry

        lax.fori_loop(0, height + 2, body, 0)

    kept = inner[...]
    gram = lax.dot_general(kept, kept, (((0,), (0,)), ((), ())), preferred_element_type=F32)
    sums = jnp.sum(kept.astype(F32), axis=0, keepdims=True)
    upper, both, diag = tri_pack(gram)
    chunks = packed.shape[1] - 1
    spare = chunks * planes - 2 * LANES - 3
    flat = jnp.concatenate(
        [upper, both, diag, sums[:, :LANES], sums[:, LANES:], jnp.zeros((spare, LANES), F32)],
        axis=0,
    )
    for q in range(chunks):
        packed[:, q, :] = flat[q * planes : (q + 1) * planes]
    packed[:, chunks, :] = jnp.zeros((planes, LANES), F32)


def plane_sum_kernel(count, terms, out):
    planes, rows, lanes = terms.shape
    summed = jnp.sum(terms[...], axis=0)
    valid = jnp.full((rows, lanes), count[0].astype(F32))
    summed = jnp.where(iota((rows, lanes), 0) == rows - 1, valid, summed)
    out[...] = jnp.broadcast_to(summed[None], out.shape)


def prepare_kernel(
    hidden, point, tile, up, down, left, right, classifier, mapped, ext, toward
):
    mapped[...] = dot(hidden[...], point[...]).astype(BF16)
    assemble(ext, tile, up, down, left, right)
    gap = classifier[0] - classifier[1]
    toward[...] = gap + gap.T


def cov_kernel(
    grid_y, grid_x, slides, place, label, gathered, ext, mapped, toward_ref, point, point_turned,
    classifier, back, sent,
):
    planes = grid_y * grid_x
    wide, channels = ext.shape[1:]
    height, width = ext.shape[0] - 2 * RIM, wide - 2 * LEFT
    half = channels // 2
    chunks = gathered.shape[1] - 1

    flat = jnp.concatenate([gathered[:, q, :] for q in range(chunks)], axis=0)
    counts = gathered[:, chunks, :]
    inverse = 1.0 / jnp.sum(counts, axis=0, keepdims=True)[:, 0:1]
    gram = tri_unpack(flat[:half], flat[half : 2 * half], flat[2 * half : 2 * half + 1])
    sums = jnp.concatenate(
        [flat[2 * half + 1 : 2 * half + 2], flat[2 * half + 2 : 2 * half + 3]], axis=1
    )
    center = sums * inverse
    spread = jnp.broadcast_to(center, (channels, channels))
    moment = gram * inverse - spread * spread.T

    mixing, mixing_turned = point[...], point_turned[...]
    high, low = split(moment)
    moved = dot(
        jnp.concatenate([high, low], axis=1), jnp.concatenate([mixing, mixing], axis=0)
    )
    moved_pair = split(moved)
    sigma = dot(
        jnp.concatenate([mixing_turned, mixing_turned], axis=1),
        jnp.concatenate(moved_pair, axis=0),
    )
    sigma = 0.5 * (sigma + sigma.T)
    eye = iota((channels, channels), 0) == iota((channels, channels), 1)
    trace = total(jnp.where(eye, sigma, 0.0))
    start = sigma * (1.0 / trace)

    toward = toward_ref[...]
    wmat, ymat, dw, dy = start, start, toward, toward
    for step in range(ITERS):
        w_pair, dw_pair = split(wmat), split(dw)
        if step == 0:
            square = mm(w_pair, w_pair)
            cross = mm(w_pair, dw_pair)
            yw, dyw = square, cross + cross.T
        else:
            first = mm(stack(w_pair, split(ymat), split(dy)), w_pair)
            second = mm(stack(w_pair, split(ymat)), dw_pair)
            square, yw = first[:channels], first[channels : 2 * channels]
            cross = second[:channels]
            dyw = first[2 * channels :] + second[channels:]
        ymat = 1.5 * ymat - 0.5 * yw
        dy = 1.5 * dy - 0.5 * dyw
        if step + 1 < ITERS:
            dsquare = cross + cross.T
            square_pair = split(square)
            third = mm(stack(square_pair, split(dsquare)), w_pair)
            cube = third[:channels]
            dcube = third[channels:] + mm(square_pair, dw_pair)
            wmat = 2.25 * wmat - 1.5 * square + 0.25 * cube
            dw = 2.25 * dw - 1.5 * dsquare + 0.25 * dcube

    root = jnp.sqrt(trace)
    pooled = root * ymat
    logit0 = total(classifier[0] * pooled)
    logit1 = total(classifier[1] * pooled)
    peak = jnp.maximum(logit0, logit1)
    lse = peak + jnp.log(jnp.exp(logit0 - peak) + jnp.exp(logit1 - peak))
    is_zero = label[0] == 0
    slope = jnp.where(is_zero, -jnp.exp(logit1 - lse), jnp.exp(logit0 - lse)) * (1.0 / slides)
    loss = (lse - jnp.where(is_zero, logit0, logit1)) * (1.0 / slides)

    level = 0.5 * total(toward * ymat) - total(dy * start)
    slant = (dy + jnp.where(eye, level, 0.0)) * (slope / root)
    slant = 0.5 * (slant + slant.T)
    point_term = mm(moved_pair, split(slant))
    class_term = slope * pooled
    class_term = 0.5 * (class_term + class_term.T)

    symmetric = slant * inverse
    sym_pair = split(symmetric)
    center_pair = split(jnp.broadcast_to(center, (8, channels)))
    mean = dot(
        jnp.concatenate(center_pair, axis=1), jnp.concatenate([mixing, mixing], axis=0)
    )
    offset = -mm(split(mean), sym_pair)[0:1]

    row_id = iota((planes, LANES), 0)
    spots = []
    for dy_ in (-1, 0, 1):
        for dx_ in (-1, 0, 1):
            near_y, near_x = place[0] + dy_, place[1] + dx_
            inside = (near_y >= 0) & (near_y < grid_y) & (near_x >= 0) & (near_x < grid_x)
            spot = jnp.where(inside, near_y * grid_x + near_x, -1)
            near = jnp.sum(jnp.where(row_id == spot, counts, 0.0), axis=0, keepdims=True)
            spots.append(near[:, 0:1])

    both = dot(mapped[...], sym_pair[0]) + dot(mapped[...], sym_pair[1]) + offset
    lane_col = iota((wide, channels), 0) - LEFT
    inner_col = jnp.where(lane_col < 0, lane_col + width, jnp.where(lane_col >= width, lane_col - width, lane_col))
    seen = (lane_col >= -1) & (lane_col <= width)
    limits = []
    for k in range(3):
        limit = jnp.where(
            lane_col < 0, spots[3 * k], jnp.where(lane_col >= width, spots[3 * k + 2], spots[3 * k + 1])
        )
        limits.append(jnp.where(seen, limit, -1.0))
    pieces = []
    for r in range(height + 2):
        tile_row = (r - 1) % height
        limit = limits[0 if r == 0 else (2 if r == height + 1 else 1)]
        raster = (tile_row * width + inner_col).astype(F32)
        pieces.append(jnp.where(raster < limit, both[r * wide : (r + 1) * wide], 0.0).astype(BF16))
    back_mapped = jnp.concatenate(pieces, axis=0)
    back_hidden = dot(back_mapped, mixing_turned).astype(BF16)
    back[...] = back_hidden.astype(F32).reshape(height + 2, wide, channels)

    depth = []
    for lane in range(0, channels, LANES):
        part = slice(lane, lane + LANES)
        column = iota((wide, LANES), 0)
        within = (column >= LEFT) & (column < LEFT + width)

        def body(i, sums, part=part, within=within):
            own = jnp.where(within, back[i + 1, :, part], 0.0)
            moved_own = [shifted(own, -1), own, shifted(own, 1)]
            feats = [ext[i + 1 + a, :, part] for a in range(3)]
            out = []
            for a in range(3):
                for b in range(3):
                    product = (feats[a] * moved_own[b]).reshape(wide // 8, 8, LANES)
                    out.append(sums[3 * a + b] + jnp.sum(product, axis=0))
            return tuple(out)

        sums = lax.fori_loop(
            0, height, body, tuple(jnp.zeros((8, LANES), F32) for _ in range(9))
        )
        depth.append(
            jnp.concatenate([jnp.sum(s, axis=0, keepdims=True) for s in sums], axis=0)
        )
    depth = jnp.concatenate(depth, axis=1)

    upper, tri, diag = tri_pack(class_term)
    class_flat = jnp.concatenate([upper, tri], axis=0)
    scale = 1.0 / planes
    extra = jnp.concatenate([diag, jnp.broadcast_to(loss, (1, half))], axis=1) * scale
    small = jnp.concatenate([depth, extra, jnp.zeros((6, channels), F32)], axis=0)
    rp, rc, rd = channels // slides, channels // slides // 2, 16 // slides
    pad = [jnp.zeros((8 - rd, channels), F32)] if rd < 8 else []
    for k in range(slides):
        sent[k, 0:rp, :] = point_term[k * rp : (k + 1) * rp]
        sent[k, rp : rp + rc, 0:half] = class_flat[k * rp : k * rp + rc]
        sent[k, rp : rp + rc, half:channels] = class_flat[k * rp + rc : (k + 1) * rp]
        sent[k, rp + rc : rp + rc + 8, :] = jnp.concatenate(
            [small[k * rd : (k + 1) * rd]] + pad, axis=0
        )


def spread_kernel(back, weights, gradient):
    height, width, channels = gradient.shape
    for lane in range(0, channels, LANES):
        part = slice(lane, lane + LANES)
        taps = [weights[k // 3, k % 3 : k % 3 + 1, part].astype(F32) for k in range(9)]

        def body(i, carry, part=part, taps=taps):
            rows = [back[i + a, :, part] for a in range(3)]
            cols = [sum(rows[2 - a] * taps[3 * a + b] for a in range(3)) for b in range(3)]
            value = cols[1] + shifted(cols[0], -1) + shifted(cols[2], 1)
            gradient[i, :, part] = value[LEFT : LEFT + width].astype(BF16)
            return carry

        lax.fori_loop(0, height, body, 0)


def slide_sum_kernel(rd, terms, shares, spread):
    slides, rows, channels = terms.shape
    main = rows - 8
    summed = terms[0]
    for k in range(1, slides):
        summed = summed + terms[k]
    shares[...] = summed[:main].astype(BF16)
    tail = summed[main : main + rd]
    lines = jnp.concatenate(
        [tail[q : q + 1, p : p + LANES] for q in range(rd) for p in range(0, channels, LANES)],
        axis=0,
    )
    spread[...] = jnp.broadcast_to(lines[None], spread.shape)


def join_kernel(shares, spread, out):
    slides, rows, channels = out.shape
    summed = jnp.sum(spread[...], axis=0)
    per = channels // LANES
    rd = summed.shape[0] // per
    tail = jnp.concatenate(
        [
            jnp.concatenate([summed[per * q + p : per * q + p + 1] for p in range(per)], axis=1)
            for q in range(rd)
        ],
        axis=0,
    )
    high, low = split(tail)
    tail = jnp.concatenate([high, low, jnp.zeros((16 - 2 * rd, channels), BF16)], axis=0)
    for k in range(slides):
        out[k, 0 : rows - 16, :] = shares[...]
        out[k, rows - 16 : rows, :] = tail


def finish_kernel(terms, loss, depth, point, classes):
    slides, rows, channels = terms.shape
    half = channels // 2
    rp, rc, rd = channels // slides, channels // slides // 2, 16 // slides
    flat, small = [], []
    for k in range(slides):
        piece = terms[k].astype(F32)
        point[k * rp : (k + 1) * rp, :] = piece[:rp]
        flat += [piece[rp : rp + rc, :half], piece[rp : rp + rc, half:]]
        tail = piece[rp + rc :]
        small.append(tail[:rd] + tail[rd : 2 * rd])
    flat = jnp.concatenate(flat, axis=0)
    small = jnp.concatenate(small, axis=0)
    full = tri_unpack(flat[:half], flat[half:], small[9:10, :half])
    classes[0] = full
    classes[1] = -full
    for a in range(3):
        depth[a] = small[3 * a : 3 * a + 3]
    loss[...] = small[9:10, half : half + 1]


def per_device(features, depth_weight, point_weight, classifier, valid_count, labels):
    slides, grid_y, grid_x = (lax.axis_size(axis) for axis in ("slide", "gy", "gx"))
    planes = grid_y * grid_x
    tile = features[0]
    height, width, channels = tile.shape
    wide = width + 2 * LEFT

    def edges(low_part, high_part, axis):
        forward = [(i, i + 1) for i in range(lax.axis_size(axis) - 1)]
        backward = [(target, source) for source, target in forward]
        return lax.ppermute(high_part, axis, forward), lax.ppermute(low_part, axis, backward)

    up, down = edges(tile[:RIM], tile[height - RIM :], "gy")

    def strip(start):
        return jnp.concatenate([part[:, start : start + RIM] for part in (up, tile, down)], axis=0)

    left, right = edges(strip(0), strip(width - RIM), "gx")

    point_turned = point_weight.T
    count = valid_count.reshape(1)
    place = jnp.stack([lax.axis_index("gy"), lax.axis_index("gx")]).astype(jnp.int32)
    halo = (tile, up, down, left, right)
    chunks = -(-(channels + 3) // planes)

    pixels = (height + 2) * wide
    ext_shape = (height + 2 * RIM, wide, channels)

    hidden, packed = pl.pallas_call(
        functools.partial(forward_kernel, planes),
        out_shape=(
            jax.ShapeDtypeStruct((pixels, channels), BF16),
            jax.ShapeDtypeStruct((planes, chunks + 1, LANES), F32),
        ),
        in_specs=[SMEM] + [VMEM] * 6,
        out_specs=(VMEM, VMEM),
        scratch_shapes=[pltpu.VMEM(ext_shape, F32), pltpu.VMEM((height * width, channels), BF16)],
        compiler_params=PARAMS,
        name="forward",
    )(count, *halo, depth_weight)

    packed = lax.all_to_all(packed, ("gy", "gx"), 0, 0)

    mapped, ext, toward = pl.pallas_call(
        prepare_kernel,
        out_shape=(
            jax.ShapeDtypeStruct((pixels, channels), BF16),
            jax.ShapeDtypeStruct(ext_shape, F32),
            jax.ShapeDtypeStruct((channels, channels), F32),
        ),
        in_specs=[VMEM] * 8,
        out_specs=(VMEM, VMEM, VMEM),
        compiler_params=PARAMS,
        cost_estimate=pl.CostEstimate(
            flops=2 * pixels * channels * channels, bytes_accessed=5 << 20, transcendentals=0
        ),
        name="prepare",
    )(hidden, point_weight, *halo, classifier)

    packed = pl.pallas_call(
        plane_sum_kernel,
        out_shape=jax.ShapeDtypeStruct((planes, chunks + 1, LANES), F32),
        in_specs=[SMEM, VMEM],
        out_specs=VMEM,
        compiler_params=SMALL,
        name="plane_sum",
    )(count, packed)
    gathered = lax.all_to_all(packed, ("gy", "gx"), 0, 0)

    rp, rd = channels // slides, 16 // slides
    main = rp + rp // 2
    back, sent = pl.pallas_call(
        functools.partial(cov_kernel, grid_y, grid_x, slides),
        out_shape=(
            jax.ShapeDtypeStruct((height + 2, wide, channels), F32),
            jax.ShapeDtypeStruct((slides, main + 8, channels), F32),
        ),
        in_specs=[SMEM, SMEM] + [VMEM] * 7,
        out_specs=(VMEM, VMEM),
        compiler_params=PARAMS,
        name="covariance",
    )(place, labels, gathered, ext, mapped, toward, point_weight, point_turned, classifier)

    received = lax.all_to_all(sent, "slide", 0, 0)
    gradient = pl.pallas_call(
        spread_kernel,
        out_shape=jax.ShapeDtypeStruct((height, width, channels), BF16),
        in_specs=[VMEM, VMEM],
        out_specs=VMEM,
        compiler_params=PARAMS,
        cost_estimate=pl.CostEstimate(
            flops=20 * pixels * channels, bytes_accessed=4 << 20, transcendentals=0
        ),
        name="spread",
    )(back, depth_weight)
    shares, spread = pl.pallas_call(
        functools.partial(slide_sum_kernel, rd),
        out_shape=(
            jax.ShapeDtypeStruct((main, channels), BF16),
            jax.ShapeDtypeStruct((planes, rd * channels // LANES, LANES), F32),
        ),
        in_specs=[VMEM],
        out_specs=(VMEM, VMEM),
        compiler_params=SMALL,
        name="slide_sum",
    )(received)
    spread = lax.all_to_all(spread, ("gy", "gx"), 0, 0)
    joined = pl.pallas_call(
        join_kernel,
        out_shape=jax.ShapeDtypeStruct((slides, main + 16, channels), BF16),
        in_specs=[VMEM, VMEM],
        out_specs=VMEM,
        compiler_params=SMALL,
        name="join",
    )(shares, spread)
    joined = lax.all_to_all(joined, "slide", 0, 0)
    loss, depth, point, classes = pl.pallas_call(
        finish_kernel,
        out_shape=(
            jax.ShapeDtypeStruct((1, 1), F32),
            jax.ShapeDtypeStruct((3, 3, channels), F32),
            jax.ShapeDtypeStruct((channels, channels), F32),
            jax.ShapeDtypeStruct(classifier.shape, F32),
        ),
        in_specs=[VMEM],
        out_specs=(VMEM, VMEM, VMEM, VMEM),
        compiler_params=SMALL,
        name="finish",
    )(joined)
    return loss.reshape(()), depth, point, classes, gradient[None]


def solution(mesh):
    placed = (P("slide", "gy", "gx", None), P(), P(), P(), P("slide", "gy", "gx"), P("slide"))
    return jax.shard_map(
        per_device,
        mesh=mesh,
        in_specs=placed,
        out_specs=(P(), P(), P(), P(), P("slide", "gy", "gx", None)),
        check_vma=False,
    )
```

```python
import functools

import jax
import jax.numpy as jnp
from jax import lax
from jax.experimental import pallas as pl
from jax.experimental.pallas import tpu as pltpu
from jax.sharding import PartitionSpec as P

ITERS = 5
RIM = 2
LEFT = 8
LANES = 128
F32 = jnp.float32
BF16 = jnp.bfloat16
VMEM = pl.BlockSpec(memory_space=pltpu.VMEM)
SMEM = pl.BlockSpec(memory_space=pltpu.SMEM)
PARAMS = pltpu.CompilerParams(vmem_limit_bytes=16 * 1024 * 1024)
SMALL = pltpu.CompilerParams(vmem_limit_bytes=4 * 1024 * 1024)


def iota(shape, dim):
    return lax.broadcasted_iota(jnp.int32, shape, dim)


def total(x):
    return jnp.sum(jnp.sum(x, axis=1, keepdims=True), axis=0, keepdims=True)


def dot(left, right):
    return jnp.dot(left, right, preferred_element_type=F32)


def split(x):
    high = x.astype(BF16)
    return high, (x - high.astype(F32)).astype(BF16)


def mm(left, right):
    lhs = jnp.concatenate([left[0], left[1], left[0]], axis=1)
    rhs = jnp.concatenate([right[0], right[0], right[1]], axis=0)
    return dot(lhs, rhs)


def stack(*pairs):
    return tuple(jnp.concatenate([pair[i] for pair in pairs], axis=0) for i in range(2))


def beside(*pairs):
    return tuple(jnp.concatenate([pair[i] for pair in pairs], axis=1) for i in range(2))


def shifted(x, step):
    return pltpu.roll(x, step % x.shape[0], 0)


def tri_pack(full):
    half = full.shape[0] // 2
    row, col = iota((half, half), 0), iota((half, half), 1)
    first, upper, second = full[:half, :half], full[:half, half:], full[half:, half:]
    both = jnp.where(row <= col, first, second)
    diag = jnp.sum(jnp.where(row == col, second, 0.0), axis=0, keepdims=True)
    return upper, both, diag


def tri_unpack(upper, both, diag):
    half = both.shape[0]
    row, col = iota((half, half), 0), iota((half, half), 1)
    turned = both.T
    first = jnp.where(row <= col, both, turned)
    second = jnp.where(row > col, both, jnp.where(row == col, diag, turned))
    return jnp.concatenate(
        [jnp.concatenate([first, upper], axis=1), jnp.concatenate([upper.T, second], axis=1)],
        axis=0,
    )


def assemble(ext, tile, up, down, left, right):
    height, width, channels = tile.shape
    rows = height + 2 * RIM
    ext[:, 0:LEFT, :] = jnp.zeros((rows, LEFT, channels), F32)
    ext[:, LEFT + width : 2 * LEFT + width, :] = jnp.zeros((rows, LEFT, channels), F32)
    ext[RIM : RIM + height, LEFT : LEFT + width, :] = tile[...].astype(F32)
    ext[0:RIM, LEFT : LEFT + width, :] = up[...].astype(F32)
    ext[RIM + height : rows, LEFT : LEFT + width, :] = down[...].astype(F32)
    ext[:, LEFT - RIM : LEFT, :] = left[...].astype(F32)
    ext[:, LEFT + width : LEFT + width + RIM, :] = right[...].astype(F32)


def load_kernel(
    tile, weights, point, classifier, tile_out, low, high, taps, turned, toward
):
    width = tile.shape[1]
    tile_out[...] = tile[...]
    low[...] = tile[:, :RIM, :]
    high[...] = tile[:, width - RIM :, :]
    taps[...] = jnp.concatenate([weights[a].astype(F32) for a in range(3)], axis=0)
    turned[...] = point[...].astype(F32).T.astype(BF16)
    gap = classifier[0] - classifier[1]
    toward[...] = gap + gap.T


def forward_kernel(
    planes, count, tile, up, down, left, right, weights, point, mapped, packed, ext, hidden, inner
):
    height, width, channels = tile.shape
    wide = ext.shape[1]
    assemble(ext, tile, up, down, left, right)
    valid = count[0]

    for lane in range(0, channels, LANES):
        part = slice(lane, lane + LANES)
        taps = [weights[k : k + 1, part] for k in range(9)]

        def body(r, carry, part=part, taps=taps):
            rows = [ext[r + a, :, part] for a in range(3)]
            cols = [sum(rows[a] * taps[3 * a + b] for a in range(3)) for b in range(3)]
            value = cols[1] + shifted(cols[0], 1) + shifted(cols[2], -1)
            hidden[pl.ds(pl.multiple_of(r * wide, 16), wide), part] = value.astype(BF16)

            @pl.when((r >= 1) & (r <= height))
            def _():
                raster = (r - 1) * width + iota((width, LANES), 0)
                kept = jnp.where(raster < valid, value[LEFT : LEFT + width], 0.0)
                start = pl.multiple_of((r - 1) * width, 16)
                inner[pl.ds(start, width), part] = kept.astype(BF16)

            return carry

        lax.fori_loop(0, height + 2, body, 0)

    kept = inner[...]
    gram = lax.dot_general(kept, kept, (((0,), (0,)), ((), ())), preferred_element_type=F32)
    mapped[...] = dot(hidden[...], point[...]).astype(BF16)
    sums = jnp.sum(kept.astype(F32), axis=0, keepdims=True)
    upper, both, diag = tri_pack(gram)
    chunks = packed.shape[1] - 1
    spare = chunks * planes - 2 * LANES - 3
    flat = jnp.concatenate(
        [upper, both, diag, sums[:, :LANES], sums[:, LANES:], jnp.zeros((spare, LANES), F32)],
        axis=0,
    )
    for q in range(chunks):
        packed[:, q, :] = flat[q * planes : (q + 1) * planes]
    packed[:, chunks, :] = jnp.zeros((planes, LANES), F32)


def plane_sum_kernel(count, terms, out):
    planes, rows, lanes = terms.shape
    summed = jnp.sum(terms[...], axis=0)
    valid = jnp.full((rows, lanes), count[0].astype(F32))
    summed = jnp.where(iota((rows, lanes), 0) == rows - 1, valid, summed)
    out[...] = jnp.broadcast_to(summed[None], out.shape)


def cov_kernel(
    grid_y, grid_x, slides, place, label, gathered, ext, mapped, toward_ref, point, point_turned,
    classifier, back_out, sent, back, sem,
):
    planes = grid_y * grid_x
    wide, channels = ext.shape[1:]
    height, width = ext.shape[0] - 2 * RIM, wide - 2 * LEFT
    half = channels // 2
    chunks = gathered.shape[1] - 1

    flat = jnp.concatenate([gathered[:, q, :] for q in range(chunks)], axis=0)
    counts = gathered[:, chunks, :]
    inverse = 1.0 / jnp.sum(counts, axis=0, keepdims=True)[:, 0:1]
    gram = tri_unpack(flat[:half], flat[half : 2 * half], flat[2 * half : 2 * half + 1])
    sums = jnp.concatenate(
        [flat[2 * half + 1 : 2 * half + 2], flat[2 * half + 2 : 2 * half + 3]], axis=1
    )
    center = sums * inverse
    spread = jnp.broadcast_to(center, (channels, channels))
    moment = gram * inverse - spread * spread.T

    mixing, mixing_turned = point[...], point_turned[...]
    high, low = split(moment)
    moved = dot(
        jnp.concatenate([high, low], axis=1), jnp.concatenate([mixing, mixing], axis=0)
    )
    moved_pair = split(moved)
    sigma = dot(
        jnp.concatenate([mixing_turned, mixing_turned], axis=1),
        jnp.concatenate(moved_pair, axis=0),
    )
    sigma = 0.5 * (sigma + sigma.T)
    eye = iota((channels, channels), 0) == iota((channels, channels), 1)
    trace = total(jnp.where(eye, sigma, 0.0))
    start = sigma * (1.0 / trace)

    toward = toward_ref[...]
    wmat, ymat, dw, dy = start, start, toward, toward
    for step in range(ITERS):
        w_pair, dw_pair = split(wmat), split(dw)
        both = beside(w_pair, dw_pair)
        if step == 0:
            first = mm(w_pair, both)
            square, cross = first[:, :channels], first[:, channels:]
            yw, dyw = square, cross + cross.T
        elif step + 1 < ITERS:
            first = mm(stack(w_pair, split(ymat)), both)
            square, cross = first[:channels, :channels], first[:channels, channels:]
            yw = first[channels:, :channels]
            dyw = first[channels:, channels:] + mm(split(dy), w_pair)
        else:
            first = mm(split(ymat), both)
            yw = first[:, :channels]
            dyw = first[:, channels:] + mm(split(dy), w_pair)
        ymat = 1.5 * ymat - 0.5 * yw
        dy = 1.5 * dy - 0.5 * dyw
        if step + 1 < ITERS:
            dsquare = cross + cross.T
            third = mm(split(square), both)
            dcube = third[:, channels:] + mm(split(dsquare), w_pair)
            wmat = 2.25 * wmat - 1.5 * square + 0.25 * third[:, :channels]
            dw = 2.25 * dw - 1.5 * dsquare + 0.25 * dcube

    root = jnp.sqrt(trace)
    pooled = root * ymat
    logit0 = total(classifier[0] * pooled)
    logit1 = total(classifier[1] * pooled)
    peak = jnp.maximum(logit0, logit1)
    lse = peak + jnp.log(jnp.exp(logit0 - peak) + jnp.exp(logit1 - peak))
    is_zero = label[0] == 0
    slope = jnp.where(is_zero, -jnp.exp(logit1 - lse), jnp.exp(logit0 - lse)) * (1.0 / slides)
    loss = (lse - jnp.where(is_zero, logit0, logit1)) * (1.0 / slides)

    level = 0.5 * total(toward * ymat) - total(dy * start)
    slant = (dy + jnp.where(eye, level, 0.0)) * (slope / root)
    slant = 0.5 * (slant + slant.T)
    point_term = mm(moved_pair, split(slant))
    class_term = slope * pooled
    class_term = 0.5 * (class_term + class_term.T)

    symmetric = slant * inverse
    sym_pair = split(symmetric)
    center_pair = split(jnp.broadcast_to(center, (8, channels)))
    mean = dot(
        jnp.concatenate(center_pair, axis=1), jnp.concatenate([mixing, mixing], axis=0)
    )
    offset = -mm(split(mean), sym_pair)[0:1]

    row_id = iota((planes, LANES), 0)
    spots = []
    for dy_ in (-1, 0, 1):
        for dx_ in (-1, 0, 1):
            near_y, near_x = place[0] + dy_, place[1] + dx_
            inside = (near_y >= 0) & (near_y < grid_y) & (near_x >= 0) & (near_x < grid_x)
            spot = jnp.where(inside, near_y * grid_x + near_x, -1)
            near = jnp.sum(jnp.where(row_id == spot, counts, 0.0), axis=0, keepdims=True)
            spots.append(near[:, 0:1])

    both = dot(mapped[...], sym_pair[0]) + dot(mapped[...], sym_pair[1]) + offset
    lane_col = iota((wide, channels), 0) - LEFT
    inner_col = jnp.where(lane_col < 0, lane_col + width, jnp.where(lane_col >= width, lane_col - width, lane_col))
    seen = (lane_col >= -1) & (lane_col <= width)
    limits = []
    for k in range(3):
        limit = jnp.where(
            lane_col < 0, spots[3 * k], jnp.where(lane_col >= width, spots[3 * k + 2], spots[3 * k + 1])
        )
        limits.append(jnp.where(seen, limit, -1.0))
    pieces = []
    for r in range(height + 2):
        tile_row = (r - 1) % height
        limit = limits[0 if r == 0 else (2 if r == height + 1 else 1)]
        raster = (tile_row * width + inner_col).astype(F32)
        pieces.append(jnp.where(raster < limit, both[r * wide : (r + 1) * wide], 0.0).astype(BF16))
    back_mapped = jnp.concatenate(pieces, axis=0)
    back[...] = dot(back_mapped, mixing_turned).astype(BF16)
    copy = pltpu.make_async_copy(back, back_out, sem)
    copy.start()

    depth = []
    for lane in range(0, channels, LANES):
        part = slice(lane, lane + LANES)
        column = iota((wide, LANES), 0)
        within = (column >= LEFT) & (column < LEFT + width)

        def body(i, sums, part=part, within=within):
            start = pl.multiple_of((i + 1) * wide, 16)
            own = jnp.where(within, back[pl.ds(start, wide), part].astype(F32), 0.0)
            moved_own = [shifted(own, -1), own, shifted(own, 1)]
            feats = [ext[i + 1 + a, :, part] for a in range(3)]
            out = []
            for a in range(3):
                for b in range(3):
                    product = (feats[a] * moved_own[b]).reshape(wide // 8, 8, LANES)
                    out.append(sums[3 * a + b] + jnp.sum(product, axis=0))
            return tuple(out)

        sums = lax.fori_loop(
            0, height, body, tuple(jnp.zeros((8, LANES), F32) for _ in range(9))
        )
        depth.append(
            jnp.concatenate([jnp.sum(s, axis=0, keepdims=True) for s in sums], axis=0)
        )
    depth = jnp.concatenate(depth, axis=1)

    upper, tri, diag = tri_pack(class_term)
    class_flat = jnp.concatenate([upper, tri], axis=0)
    scale = 1.0 / planes
    extra = jnp.concatenate([diag, jnp.broadcast_to(loss, (1, half))], axis=1) * scale
    small = jnp.concatenate([depth, extra, jnp.zeros((6, channels), F32)], axis=0)
    rp, rc, rd = channels // slides, channels // slides // 2, 16 // slides
    pad = [jnp.zeros((8 - rd, channels), F32)] if rd < 8 else []
    for k in range(slides):
        sent[k, 0:rp, :] = point_term[k * rp : (k + 1) * rp]
        sent[k, rp : rp + rc, 0:half] = class_flat[k * rp : k * rp + rc]
        sent[k, rp : rp + rc, half:channels] = class_flat[k * rp + rc : (k + 1) * rp]
        sent[k, rp + rc : rp + rc + 8, :] = jnp.concatenate(
            [small[k * rd : (k + 1) * rd]] + pad, axis=0
        )
    copy.wait()


def spread_kernel(back, weights, gradient):
    height, width, channels = gradient.shape
    wide = width + 2 * LEFT
    for lane in range(0, channels, LANES):
        part = slice(lane, lane + LANES)
        taps = [weights[k : k + 1, part] for k in range(9)]

        def body(i, carry, part=part, taps=taps):
            rows = [
                back[pl.ds(pl.multiple_of((i + a) * wide, 16), wide), part].astype(F32)
                for a in range(3)
            ]
            cols = [sum(rows[2 - a] * taps[3 * a + b] for a in range(3)) for b in range(3)]
            value = cols[1] + shifted(cols[0], -1) + shifted(cols[2], 1)
            gradient[i, :, part] = value[LEFT : LEFT + width].astype(BF16)
            return carry

        lax.fori_loop(0, height, body, 0)


def slide_sum_kernel(rd, terms, shares, spread):
    slides, rows, channels = terms.shape
    main = rows - 8
    summed = terms[0]
    for k in range(1, slides):
        summed = summed + terms[k]
    shares[...] = summed[:main].astype(BF16)
    tail = summed[main : main + rd]
    lines = jnp.concatenate(
        [tail[q : q + 1, p : p + LANES] for q in range(rd) for p in range(0, channels, LANES)],
        axis=0,
    )
    spread[...] = jnp.broadcast_to(lines[None], spread.shape)


def join_kernel(shares, spread, out):
    slides, rows, channels = out.shape
    summed = jnp.sum(spread[...], axis=0)
    per = channels // LANES
    rd = summed.shape[0] // per
    tail = jnp.concatenate(
        [
            jnp.concatenate([summed[per * q + p : per * q + p + 1] for p in range(per)], axis=1)
            for q in range(rd)
        ],
        axis=0,
    )
    high, low = split(tail)
    tail = jnp.concatenate([high, low, jnp.zeros((16 - 2 * rd, channels), BF16)], axis=0)
    for k in range(slides):
        out[k, 0 : rows - 16, :] = shares[...]
        out[k, rows - 16 : rows, :] = tail


def finish_kernel(terms, loss, depth, point, classes):
    slides, rows, channels = terms.shape
    half = channels // 2
    rp, rc, rd = channels // slides, channels // slides // 2, 16 // slides
    flat, small = [], []
    for k in range(slides):
        piece = terms[k].astype(F32)
        point[k * rp : (k + 1) * rp, :] = piece[:rp]
        flat += [piece[rp : rp + rc, :half], piece[rp : rp + rc, half:]]
        tail = piece[rp + rc :]
        small.append(tail[:rd] + tail[rd : 2 * rd])
    flat = jnp.concatenate(flat, axis=0)
    small = jnp.concatenate(small, axis=0)
    full = tri_unpack(flat[:half], flat[half:], small[9:10, :half])
    classes[0] = full
    classes[1] = -full
    for a in range(3):
        depth[a] = small[3 * a : 3 * a + 3]
    loss[...] = small[9:10, half : half + 1]


def per_device(features, depth_weight, point_weight, classifier, valid_count, labels):
    slides, grid_y, grid_x = (lax.axis_size(axis) for axis in ("slide", "gy", "gx"))
    planes = grid_y * grid_x
    tile = features[0]
    height, width, channels = tile.shape
    wide = width + 2 * LEFT

    def edges(low_part, high_part, axis):
        forward = [(i, i + 1) for i in range(lax.axis_size(axis) - 1)]
        backward = [(target, source) for source, target in forward]
        return lax.ppermute(high_part, axis, forward), lax.ppermute(low_part, axis, backward)

    up, down = edges(tile[:RIM], tile[height - RIM :], "gy")

    tile, low, high, weights, point_turned, toward = pl.pallas_call(
        load_kernel,
        out_shape=(
            jax.ShapeDtypeStruct(tile.shape, BF16),
            jax.ShapeDtypeStruct((height, RIM, channels), BF16),
            jax.ShapeDtypeStruct((height, RIM, channels), BF16),
            jax.ShapeDtypeStruct((9, channels), F32),
            jax.ShapeDtypeStruct((channels, channels), BF16),
            jax.ShapeDtypeStruct((channels, channels), F32),
        ),
        in_specs=[VMEM] * 4,
        out_specs=(VMEM,) * 6,
        compiler_params=SMALL,
        name="load",
    )(tile, depth_weight, point_weight, classifier)

    def strip(own, start):
        ends = [part[:, start : start + RIM] for part in (up, down)]
        return jnp.concatenate([ends[0], own, ends[1]], axis=0)

    left, right = edges(strip(low, 0), strip(high, width - RIM), "gx")

    count = valid_count.reshape(1)
    place = jnp.stack([lax.axis_index("gy"), lax.axis_index("gx")]).astype(jnp.int32)
    halo = (tile, up, down, left, right)
    chunks = -(-(channels + 3) // planes)
    pixels = (height + 2) * wide
    ext_shape = (height + 2 * RIM, wide, channels)

    mapped, packed, ext = pl.pallas_call(
        functools.partial(forward_kernel, planes),
        out_shape=(
            jax.ShapeDtypeStruct((pixels, channels), BF16),
            jax.ShapeDtypeStruct((planes, chunks + 1, LANES), F32),
            jax.ShapeDtypeStruct(ext_shape, F32),
        ),
        in_specs=[SMEM] + [VMEM] * 7,
        out_specs=(VMEM, VMEM, VMEM),
        scratch_shapes=[
            pltpu.VMEM((pixels, channels), BF16),
            pltpu.VMEM((height * width, channels), BF16),
        ],
        compiler_params=PARAMS,
        name="forward",
    )(count, *halo, weights, point_weight)
    packed, place, labels = lax.optimization_barrier((packed, place, labels))

    packed = lax.all_to_all(packed, ("gy", "gx"), 0, 0)

    packed = pl.pallas_call(
        plane_sum_kernel,
        out_shape=jax.ShapeDtypeStruct((planes, chunks + 1, LANES), F32),
        in_specs=[SMEM, VMEM],
        out_specs=VMEM,
        compiler_params=SMALL,
        name="plane_sum",
    )(count, packed)
    gathered = lax.all_to_all(packed, ("gy", "gx"), 0, 0)

    rp, rd = channels // slides, 16 // slides
    main = rp + rp // 2
    back, sent = pl.pallas_call(
        functools.partial(cov_kernel, grid_y, grid_x, slides),
        out_shape=(
            jax.ShapeDtypeStruct((pixels, channels), BF16),
            jax.ShapeDtypeStruct((slides, main + 8, channels), F32),
        ),
        in_specs=[SMEM, SMEM] + [VMEM] * 7,
        out_specs=(pl.BlockSpec(memory_space=pltpu.HBM), VMEM),
        scratch_shapes=[pltpu.VMEM((pixels, channels), BF16), pltpu.SemaphoreType.DMA],
        compiler_params=PARAMS,
        name="covariance",
    )(place, labels, gathered, ext, mapped, toward, point_weight, point_turned, classifier)

    received = lax.all_to_all(sent, "slide", 0, 0)
    gradient = pl.pallas_call(
        spread_kernel,
        out_shape=jax.ShapeDtypeStruct((height, width, channels), BF16),
        in_specs=[VMEM, VMEM],
        out_specs=VMEM,
        compiler_params=PARAMS,
        cost_estimate=pl.CostEstimate(
            flops=20 * pixels * channels, bytes_accessed=4 << 20, transcendentals=0
        ),
        name="spread",
    )(back, weights)
    shares, spread = pl.pallas_call(
        functools.partial(slide_sum_kernel, rd),
        out_shape=(
            jax.ShapeDtypeStruct((main, channels), BF16),
            jax.ShapeDtypeStruct((planes, rd * channels // LANES, LANES), F32),
        ),
        in_specs=[VMEM],
        out_specs=(VMEM, VMEM),
        compiler_params=SMALL,
        name="slide_sum",
    )(received)
    spread = lax.all_to_all(spread, ("gy", "gx"), 0, 0)
    joined = pl.pallas_call(
        join_kernel,
        out_shape=jax.ShapeDtypeStruct((slides, main + 16, channels), BF16),
        in_specs=[VMEM, VMEM],
        out_specs=VMEM,
        compiler_params=SMALL,
        name="join",
    )(shares, spread)
    joined = lax.all_to_all(joined, "slide", 0, 0)
    loss, depth, point, classes = pl.pallas_call(
        finish_kernel,
        out_shape=(
            jax.ShapeDtypeStruct((1, 1), F32),
            jax.ShapeDtypeStruct((3, 3, channels), F32),
            jax.ShapeDtypeStruct((channels, channels), F32),
            jax.ShapeDtypeStruct(classifier.shape, F32),
        ),
        in_specs=[VMEM],
        out_specs=(VMEM, VMEM, VMEM, VMEM),
        compiler_params=SMALL,
        name="finish",
    )(joined)
    return loss.reshape(()), depth, point, classes, gradient[None]


def solution(mesh):
    placed = (P("slide", "gy", "gx", None), P(), P(), P(), P("slide", "gy", "gx"), P("slide"))
    return jax.shard_map(
        per_device,
        mesh=mesh,
        in_specs=placed,
        out_specs=(P(), P(), P(), P(), P("slide", "gy", "gx", None)),
        check_vma=False,
    )
```

```python
import functools

import jax
import jax.numpy as jnp
from jax import lax
from jax.experimental import pallas as pl
from jax.experimental.pallas import tpu as pltpu
from jax.sharding import PartitionSpec as P

ITERS = 5
RIM = 2
LEFT = 8
LANES = 128
F32 = jnp.float32
BF16 = jnp.bfloat16
VMEM = pl.BlockSpec(memory_space=pltpu.VMEM)
HBM = pl.BlockSpec(memory_space=pltpu.HBM)
SMEM = pl.BlockSpec(memory_space=pltpu.SMEM)
PARAMS = pltpu.CompilerParams(vmem_limit_bytes=16 * 1024 * 1024)
SMALL = pltpu.CompilerParams(vmem_limit_bytes=4 * 1024 * 1024)


def iota(shape, dim):
    return lax.broadcasted_iota(jnp.int32, shape, dim)


def total(x):
    return jnp.sum(jnp.sum(x, axis=1, keepdims=True), axis=0, keepdims=True)


def dot(left, right):
    return jnp.dot(left, right, preferred_element_type=F32)


def split(x):
    high = x.astype(BF16)
    return high, (x - high.astype(F32)).astype(BF16)


def mm(left, right):
    lhs = jnp.concatenate([left[0], left[1], left[0]], axis=1)
    rhs = jnp.concatenate([right[0], right[0], right[1]], axis=0)
    return dot(lhs, rhs)


def stack(*pairs):
    return tuple(jnp.concatenate([pair[i] for pair in pairs], axis=0) for i in range(2))


def beside(*pairs):
    return tuple(jnp.concatenate([pair[i] for pair in pairs], axis=1) for i in range(2))


def shifted(x, step):
    return pltpu.roll(x, step % x.shape[0], 0)


def tri_pack(full):
    half = full.shape[0] // 2
    row, col = iota((half, half), 0), iota((half, half), 1)
    first, upper, second = full[:half, :half], full[:half, half:], full[half:, half:]
    both = jnp.where(row <= col, first, second)
    diag = jnp.sum(jnp.where(row == col, second, 0.0), axis=0, keepdims=True)
    return upper, both, diag


def tri_unpack(upper, both, diag):
    half = both.shape[0]
    row, col = iota((half, half), 0), iota((half, half), 1)
    turned = both.T
    first = jnp.where(row <= col, both, turned)
    second = jnp.where(row > col, both, jnp.where(row == col, diag, turned))
    return jnp.concatenate(
        [jnp.concatenate([first, upper], axis=1), jnp.concatenate([upper.T, second], axis=1)],
        axis=0,
    )


def assemble(ext, tile, up, down, left, right):
    height, width, channels = tile.shape
    rows = height + 2 * RIM
    ext[:, 0:LEFT, :] = jnp.zeros((rows, LEFT, channels), F32)
    ext[:, LEFT + width : 2 * LEFT + width, :] = jnp.zeros((rows, LEFT, channels), F32)
    ext[RIM : RIM + height, LEFT : LEFT + width, :] = tile[...].astype(F32)
    ext[0:RIM, LEFT : LEFT + width, :] = up[...].astype(F32)
    ext[RIM + height : rows, LEFT : LEFT + width, :] = down[...].astype(F32)
    ext[:, LEFT - RIM : LEFT, :] = left[...].astype(F32)
    ext[:, LEFT + width : LEFT + width + RIM, :] = right[...].astype(F32)


def load_kernel(scalars, tile_in, tile, low, high, info):
    width = tile.shape[1]
    tile[...] = tile_in[...]
    low[...] = tile_in[:, :RIM, :]
    high[...] = tile_in[:, width - RIM :, :]
    row = iota(info.shape, 0)
    value = jnp.zeros(info.shape, F32)
    for k in range(4):
        value = jnp.where(row == k, scalars[k].astype(F32), value)
    info[...] = value


def weights_kernel(edge, weights, point, classifier, taps, mixing, turned, classes, toward):
    taps[...] = jnp.concatenate([weights[a].astype(F32) for a in range(3)], axis=0)
    mixing[...] = point[...]
    turned[...] = point[...].astype(F32).T.astype(BF16)
    classes[...] = classifier[...]
    gap = classifier[0] - classifier[1]
    toward[...] = gap + gap.T


def forward_kernel(
    planes, info, tile, up, down, left, right, weights, point, mapped, packed, ext, hidden, inner
):
    height, width, channels = tile.shape
    wide = ext.shape[1]
    assemble(ext, tile, up, down, left, right)
    valid = jnp.broadcast_to(info[0:1, :].astype(jnp.int32), (width, LANES))
    order = iota((width, LANES), 0)

    for lane in range(0, channels, LANES):
        part = slice(lane, lane + LANES)
        taps = [weights[k : k + 1, part] for k in range(9)]

        def body(r, carry, part=part, taps=taps):
            rows = [ext[r + a, :, part] for a in range(3)]
            cols = [sum(rows[a] * taps[3 * a + b] for a in range(3)) for b in range(3)]
            value = cols[1] + shifted(cols[0], 1) + shifted(cols[2], -1)
            hidden[pl.ds(pl.multiple_of(r * wide, 16), wide), part] = value.astype(BF16)

            @pl.when((r >= 1) & (r <= height))
            def _():
                kept = jnp.where(order < valid - (r - 1) * width, value[LEFT : LEFT + width], 0.0)
                start = pl.multiple_of((r - 1) * width, 16)
                inner[pl.ds(start, width), part] = kept.astype(BF16)

            return carry

        lax.fori_loop(0, height + 2, body, 0)

    kept = inner[...]
    gram = lax.dot_general(kept, kept, (((0,), (0,)), ((), ())), preferred_element_type=F32)
    mapped[...] = dot(hidden[...], point[...]).astype(BF16)
    sums = jnp.sum(kept.astype(F32), axis=0, keepdims=True)
    upper, both, diag = tri_pack(gram)
    chunks = packed.shape[1] - 1
    spare = chunks * planes - 2 * LANES - 3
    flat = jnp.concatenate(
        [upper, both, diag, sums[:, :LANES], sums[:, LANES:], jnp.zeros((spare, LANES), F32)],
        axis=0,
    )
    for q in range(chunks):
        packed[:, q, :] = flat[q * planes : (q + 1) * planes]
    packed[:, chunks, :] = jnp.zeros((planes, LANES), F32)


def plane_sum_kernel(info, terms, out):
    planes, rows, lanes = terms.shape
    summed = jnp.sum(terms[...], axis=0)
    summed = jnp.where(iota((rows, lanes), 0) == rows - 1, info[0:1, 0:1], summed)
    out[...] = jnp.broadcast_to(summed[None], out.shape)


def cov_kernel(
    grid_y, grid_x, slides, info, gathered, ext, mapped, toward_ref, point, point_turned,
    classifier, back_out, sent, back, sem,
):
    planes = grid_y * grid_x
    wide, channels = ext.shape[1:]
    height, width = ext.shape[0] - 2 * RIM, wide - 2 * LEFT
    half = channels // 2
    chunks = gathered.shape[1] - 1

    flat = jnp.concatenate([gathered[:, q, :] for q in range(chunks)], axis=0)
    counts = gathered[:, chunks, :]
    inverse = 1.0 / jnp.sum(counts, axis=0, keepdims=True)[:, 0:1]
    gram = tri_unpack(flat[:half], flat[half : 2 * half], flat[2 * half : 2 * half + 1])
    sums = jnp.concatenate(
        [flat[2 * half + 1 : 2 * half + 2], flat[2 * half + 2 : 2 * half + 3]], axis=1
    )
    center = sums * inverse
    spread = jnp.broadcast_to(center, (channels, channels))
    moment = gram * inverse - spread * spread.T

    mixing, mixing_turned = point[...], point_turned[...]
    high, low = split(moment)
    moved = dot(
        jnp.concatenate([high, low], axis=1), jnp.concatenate([mixing, mixing], axis=0)
    )
    moved_pair = split(moved)
    sigma = dot(
        jnp.concatenate([mixing_turned, mixing_turned], axis=1),
        jnp.concatenate(moved_pair, axis=0),
    )
    sigma = 0.5 * (sigma + sigma.T)
    eye = iota((channels, channels), 0) == iota((channels, channels), 1)
    trace = total(jnp.where(eye, sigma, 0.0))
    start = sigma * (1.0 / trace)

    toward = toward_ref[...]
    wmat, ymat, dw, dy = start, start, toward, toward
    for step in range(ITERS):
        w_pair, dw_pair = split(wmat), split(dw)
        both = beside(w_pair, dw_pair)
        if step == 0:
            first = mm(w_pair, both)
            square, cross = first[:, :channels], first[:, channels:]
            yw, dyw = square, cross + cross.T
        elif step + 1 < ITERS:
            first = mm(stack(w_pair, split(ymat)), both)
            square, cross = first[:channels, :channels], first[:channels, channels:]
            yw = first[channels:, :channels]
            dyw = first[channels:, channels:] + mm(split(dy), w_pair)
        else:
            first = mm(split(ymat), both)
            yw = first[:, :channels]
            dyw = first[:, channels:] + mm(split(dy), w_pair)
        ymat = 1.5 * ymat - 0.5 * yw
        dy = 1.5 * dy - 0.5 * dyw
        if step + 1 < ITERS:
            dsquare = cross + cross.T
            third = mm(split(square), both)
            dcube = third[:, channels:] + mm(split(dsquare), w_pair)
            wmat = 2.25 * wmat - 1.5 * square + 0.25 * third[:, :channels]
            dw = 2.25 * dw - 1.5 * dsquare + 0.25 * dcube

    root = jnp.sqrt(trace)
    pooled = root * ymat
    logit0 = total(classifier[0] * pooled)
    logit1 = total(classifier[1] * pooled)
    peak = jnp.maximum(logit0, logit1)
    lse = peak + jnp.log(jnp.exp(logit0 - peak) + jnp.exp(logit1 - peak))
    is_zero = info[1:2, 0:1] == 0.0
    slope = jnp.where(is_zero, -jnp.exp(logit1 - lse), jnp.exp(logit0 - lse)) * (1.0 / slides)
    loss = (lse - jnp.where(is_zero, logit0, logit1)) * (1.0 / slides)

    level = 0.5 * total(toward * ymat) - total(dy * start)
    slant = (dy + jnp.where(eye, level, 0.0)) * (slope / root)
    slant = 0.5 * (slant + slant.T)
    point_term = mm(moved_pair, split(slant))
    class_term = slope * pooled
    class_term = 0.5 * (class_term + class_term.T)

    symmetric = slant * inverse
    sym_pair = split(symmetric)
    center_pair = split(jnp.broadcast_to(center, (8, channels)))
    mean = dot(
        jnp.concatenate(center_pair, axis=1), jnp.concatenate([mixing, mixing], axis=0)
    )
    offset = -mm(split(mean), sym_pair)[0:1]

    row_id = iota((planes, LANES), 0).astype(F32)
    spots = []
    for dy_ in (-1, 0, 1):
        for dx_ in (-1, 0, 1):
            near_y, near_x = info[2:3, 0:1] + dy_, info[3:4, 0:1] + dx_
            inside = (near_y >= 0) & (near_y < grid_y) & (near_x >= 0) & (near_x < grid_x)
            spot = jnp.where(inside, near_y * grid_x + near_x, -1.0)
            near = jnp.sum(jnp.where(row_id == spot, counts, 0.0), axis=0, keepdims=True)
            spots.append(near[:, 0:1])

    both = dot(mapped[...], sym_pair[0]) + dot(mapped[...], sym_pair[1]) + offset
    lane_col = iota((wide, channels), 0) - LEFT
    inner_col = jnp.where(lane_col < 0, lane_col + width, jnp.where(lane_col >= width, lane_col - width, lane_col))
    seen = (lane_col >= -1) & (lane_col <= width)
    limits = []
    for k in range(3):
        limit = jnp.where(
            lane_col < 0, spots[3 * k], jnp.where(lane_col >= width, spots[3 * k + 2], spots[3 * k + 1])
        )
        limits.append(jnp.where(seen, limit, -1.0))
    pieces = []
    for r in range(height + 2):
        tile_row = (r - 1) % height
        limit = limits[0 if r == 0 else (2 if r == height + 1 else 1)]
        raster = (tile_row * width + inner_col).astype(F32)
        pieces.append(jnp.where(raster < limit, both[r * wide : (r + 1) * wide], 0.0).astype(BF16))
    back_mapped = jnp.concatenate(pieces, axis=0)
    back[...] = dot(back_mapped, mixing_turned).astype(BF16)
    copy = pltpu.make_async_copy(back, back_out, sem)
    copy.start()

    depth = []
    for lane in range(0, channels, LANES):
        part = slice(lane, lane + LANES)
        column = iota((wide, LANES), 0)
        within = (column >= LEFT) & (column < LEFT + width)

        def body(i, sums, part=part, within=within):
            start = pl.multiple_of((i + 1) * wide, 16)
            own = jnp.where(within, back[pl.ds(start, wide), part].astype(F32), 0.0)
            moved_own = [shifted(own, -1), own, shifted(own, 1)]
            feats = [ext[i + 1 + a, :, part] for a in range(3)]
            out = []
            for a in range(3):
                for b in range(3):
                    product = (feats[a] * moved_own[b]).reshape(wide // 8, 8, LANES)
                    out.append(sums[3 * a + b] + jnp.sum(product, axis=0))
            return tuple(out)

        sums = lax.fori_loop(
            0, height, body, tuple(jnp.zeros((8, LANES), F32) for _ in range(9))
        )
        depth.append(
            jnp.concatenate([jnp.sum(s, axis=0, keepdims=True) for s in sums], axis=0)
        )
    depth = jnp.concatenate(depth, axis=1)

    upper, tri, diag = tri_pack(class_term)
    class_flat = jnp.concatenate([upper, tri], axis=0)
    scale = 1.0 / planes
    extra = jnp.concatenate([diag, jnp.broadcast_to(loss, (1, half))], axis=1) * scale
    small = jnp.concatenate([depth, extra, jnp.zeros((6, channels), F32)], axis=0)
    rp, rc, rd = channels // slides, channels // slides // 2, 16 // slides
    pad = [jnp.zeros((8 - rd, channels), F32)] if rd < 8 else []
    for k in range(slides):
        sent[k, 0:rp, :] = point_term[k * rp : (k + 1) * rp]
        sent[k, rp : rp + rc, 0:half] = class_flat[k * rp : k * rp + rc]
        sent[k, rp : rp + rc, half:channels] = class_flat[k * rp + rc : (k + 1) * rp]
        sent[k, rp + rc : rp + rc + 8, :] = jnp.concatenate(
            [small[k * rd : (k + 1) * rd]] + pad, axis=0
        )
    copy.wait()


def spread_kernel(back, weights, gradient):
    height, width, channels = gradient.shape
    wide = width + 2 * LEFT
    for lane in range(0, channels, LANES):
        part = slice(lane, lane + LANES)
        taps = [weights[k : k + 1, part] for k in range(9)]

        def body(i, carry, part=part, taps=taps):
            rows = [
                back[pl.ds(pl.multiple_of((i + a) * wide, 16), wide), part].astype(F32)
                for a in range(3)
            ]
            cols = [sum(rows[2 - a] * taps[3 * a + b] for a in range(3)) for b in range(3)]
            value = cols[1] + shifted(cols[0], -1) + shifted(cols[2], 1)
            gradient[i, :, part] = value[LEFT : LEFT + width].astype(BF16)
            return carry

        lax.fori_loop(0, height, body, 0)


def slide_sum_kernel(rd, terms, shares, spread):
    slides, rows, channels = terms.shape
    main = rows - 8
    summed = terms[0]
    for k in range(1, slides):
        summed = summed + terms[k]
    shares[...] = summed[:main].astype(BF16)
    tail = summed[main : main + rd]
    lines = jnp.concatenate(
        [tail[q : q + 1, p : p + LANES] for q in range(rd) for p in range(0, channels, LANES)],
        axis=0,
    )
    spread[...] = jnp.broadcast_to(lines[None], spread.shape)


def join_kernel(shares, spread, out):
    slides, rows, channels = out.shape
    summed = jnp.sum(spread[...], axis=0)
    per = channels // LANES
    rd = summed.shape[0] // per
    tail = jnp.concatenate(
        [
            jnp.concatenate([summed[per * q + p : per * q + p + 1] for p in range(per)], axis=1)
            for q in range(rd)
        ],
        axis=0,
    )
    high, low = split(tail)
    tail = jnp.concatenate([high, low, jnp.zeros((16 - 2 * rd, channels), BF16)], axis=0)
    for k in range(slides):
        out[k, 0 : rows - 16, :] = shares[...]
        out[k, rows - 16 : rows, :] = tail


def finish_kernel(terms, loss, depth, point, classes):
    slides, rows, channels = terms.shape
    half = channels // 2
    rp, rc, rd = channels // slides, channels // slides // 2, 16 // slides
    flat, small = [], []
    for k in range(slides):
        piece = terms[k].astype(F32)
        point[k * rp : (k + 1) * rp, :] = piece[:rp]
        flat += [piece[rp : rp + rc, :half], piece[rp : rp + rc, half:]]
        tail = piece[rp + rc :]
        small.append(tail[:rd] + tail[rd : 2 * rd])
    flat = jnp.concatenate(flat, axis=0)
    small = jnp.concatenate(small, axis=0)
    full = tri_unpack(flat[:half], flat[half:], small[9:10, :half])
    classes[0] = full
    classes[1] = -full
    for a in range(3):
        depth[a] = small[3 * a : 3 * a + 3]
    loss[...] = small[9:10, half : half + 1]


def per_device(features, depth_weight, point_weight, classifier, valid_count, labels):
    slides, grid_y, grid_x = (lax.axis_size(axis) for axis in ("slide", "gy", "gx"))
    planes = grid_y * grid_x
    tile = features[0]
    height, width, channels = tile.shape
    wide = width + 2 * LEFT

    def edges(low_part, high_part, axis):
        forward = [(i, i + 1) for i in range(lax.axis_size(axis) - 1)]
        backward = [(target, source) for source, target in forward]
        return lax.ppermute(high_part, axis, forward), lax.ppermute(low_part, axis, backward)

    up, down = edges(tile[:RIM], tile[height - RIM :], "gy")
    strip_shape = jax.ShapeDtypeStruct((height, RIM, channels), BF16)
    scalars = jnp.stack(
        [
            valid_count[0, 0, 0],
            labels[0],
            lax.axis_index("gy").astype(jnp.int32),
            lax.axis_index("gx").astype(jnp.int32),
        ]
    )
    tile, low, high, info = pl.pallas_call(
        load_kernel,
        out_shape=(
            jax.ShapeDtypeStruct(tile.shape, BF16),
            strip_shape,
            strip_shape,
            jax.ShapeDtypeStruct((8, LANES), F32),
        ),
        in_specs=[SMEM, VMEM],
        out_specs=(VMEM,) * 4,
        compiler_params=SMALL,
        name="load",
    )(scalars, tile)
    def strip(own, start):
        ends = [part[:, start : start + RIM] for part in (up, down)]
        return jnp.concatenate([ends[0], own, ends[1]], axis=0)

    low_strip, high_strip = strip(low, 0), strip(high, width - RIM)
    left, right = edges(low_strip, high_strip, "gx")
    square = (channels, channels)
    weights, point, point_turned, classes, toward = pl.pallas_call(
        weights_kernel,
        out_shape=(
            jax.ShapeDtypeStruct((9, channels), F32),
            jax.ShapeDtypeStruct(square, BF16),
            jax.ShapeDtypeStruct(square, BF16),
            jax.ShapeDtypeStruct(classifier.shape, F32),
            jax.ShapeDtypeStruct(square, F32),
        ),
        in_specs=[VMEM] * 4,
        out_specs=(VMEM,) * 5,
        compiler_params=SMALL,
        name="weights",
    )(low_strip, depth_weight, point_weight, classifier)

    halo = (tile, up, down, left, right)
    chunks = -(-(channels + 3) // planes)
    pixels = (height + 2) * wide
    ext_shape = (height + 2 * RIM, wide, channels)

    mapped, packed, ext = pl.pallas_call(
        functools.partial(forward_kernel, planes),
        out_shape=(
            jax.ShapeDtypeStruct((pixels, channels), BF16),
            jax.ShapeDtypeStruct((planes, chunks + 1, LANES), F32),
            jax.ShapeDtypeStruct(ext_shape, F32),
        ),
        in_specs=[VMEM] * 8,
        out_specs=(VMEM,) * 3,
        scratch_shapes=[
            pltpu.VMEM((pixels, channels), BF16),
            pltpu.VMEM((height * width, channels), BF16),
        ],
        compiler_params=PARAMS,
        name="forward",
    )(info, *halo, weights, point)

    packed = lax.all_to_all(packed, ("gy", "gx"), 0, 0)

    packed = pl.pallas_call(
        plane_sum_kernel,
        out_shape=jax.ShapeDtypeStruct((planes, chunks + 1, LANES), F32),
        in_specs=[VMEM, VMEM],
        out_specs=VMEM,
        compiler_params=SMALL,
        name="plane_sum",
    )(info, packed)
    gathered = lax.all_to_all(packed, ("gy", "gx"), 0, 0)

    rp, rd = channels // slides, 16 // slides
    main = rp + rp // 2
    back, sent = pl.pallas_call(
        functools.partial(cov_kernel, grid_y, grid_x, slides),
        out_shape=(
            jax.ShapeDtypeStruct((pixels, channels), BF16),
            jax.ShapeDtypeStruct((slides, main + 8, channels), F32),
        ),
        in_specs=[VMEM] * 8,
        out_specs=(HBM, VMEM),
        scratch_shapes=[pltpu.VMEM((pixels, channels), BF16), pltpu.SemaphoreType.DMA],
        compiler_params=PARAMS,
        name="covariance",
    )(info, gathered, ext, mapped, toward, point, point_turned, classes)

    received = lax.all_to_all(sent, "slide", 0, 0)
    gradient = pl.pallas_call(
        spread_kernel,
        out_shape=jax.ShapeDtypeStruct((height, width, channels), BF16),
        in_specs=[VMEM, VMEM],
        out_specs=VMEM,
        compiler_params=PARAMS,
        cost_estimate=pl.CostEstimate(
            flops=20 * pixels * channels, bytes_accessed=4 << 20, transcendentals=0
        ),
        name="spread",
    )(back, weights)
    shares, spread = pl.pallas_call(
        functools.partial(slide_sum_kernel, rd),
        out_shape=(
            jax.ShapeDtypeStruct((main, channels), BF16),
            jax.ShapeDtypeStruct((planes, rd * channels // LANES, LANES), F32),
        ),
        in_specs=[VMEM],
        out_specs=(VMEM, VMEM),
        compiler_params=SMALL,
        name="slide_sum",
    )(received)
    spread = lax.all_to_all(spread, ("gy", "gx"), 0, 0)
    joined = pl.pallas_call(
        join_kernel,
        out_shape=jax.ShapeDtypeStruct((slides, main + 16, channels), BF16),
        in_specs=[VMEM, VMEM],
        out_specs=VMEM,
        compiler_params=SMALL,
        name="join",
    )(shares, spread)
    joined = lax.all_to_all(joined, "slide", 0, 0)
    loss, depth, point_total, class_total = pl.pallas_call(
        finish_kernel,
        out_shape=(
            jax.ShapeDtypeStruct((1, 1), F32),
            jax.ShapeDtypeStruct((3, 3, channels), F32),
            jax.ShapeDtypeStruct((channels, channels), F32),
            jax.ShapeDtypeStruct(classifier.shape, F32),
        ),
        in_specs=[VMEM],
        out_specs=(VMEM, VMEM, VMEM, VMEM),
        compiler_params=SMALL,
        name="finish",
    )(joined)
    return loss.reshape(()), depth, point_total, class_total, gradient[None]


def solution(mesh):
    placed = (P("slide", "gy", "gx", None), P(), P(), P(), P("slide", "gy", "gx"), P("slide"))
    return jax.shard_map(
        per_device,
        mesh=mesh,
        in_specs=placed,
        out_specs=(P(), P(), P(), P(), P("slide", "gy", "gx", None)),
        check_vma=False,
    )
```

```python
import functools

import jax
import jax.numpy as jnp
from jax import lax
from jax.experimental import pallas as pl
from jax.experimental.pallas import tpu as pltpu
from jax.sharding import PartitionSpec as P

ITERS = 5
RIM = 2
LEFT = 8
LANES = 128
F32 = jnp.float32
BF16 = jnp.bfloat16
VMEM = pl.BlockSpec(memory_space=pltpu.VMEM)
HBM = pl.BlockSpec(memory_space=pltpu.HBM)
SMEM = pl.BlockSpec(memory_space=pltpu.SMEM)
PARAMS = pltpu.CompilerParams(vmem_limit_bytes=16 * 1024 * 1024)
SMALL = pltpu.CompilerParams(vmem_limit_bytes=4 * 1024 * 1024)


def iota(shape, dim):
    return lax.broadcasted_iota(jnp.int32, shape, dim)


def total(x):
    return jnp.sum(jnp.sum(x, axis=1, keepdims=True), axis=0, keepdims=True)


def dot(left, right):
    return jnp.dot(left, right, preferred_element_type=F32)


def split(x):
    high = x.astype(BF16)
    return high, (x - high.astype(F32)).astype(BF16)


def mm(left, right):
    lhs = jnp.concatenate([left[0], left[1], left[0]], axis=1)
    rhs = jnp.concatenate([right[0], right[0], right[1]], axis=0)
    return dot(lhs, rhs)


def stack(*pairs):
    return tuple(jnp.concatenate([pair[i] for pair in pairs], axis=0) for i in range(2))


def beside(*pairs):
    return tuple(jnp.concatenate([pair[i] for pair in pairs], axis=1) for i in range(2))


def shifted(x, step):
    return pltpu.roll(x, step % x.shape[0], 0)


def tri_pack(full):
    half = full.shape[0] // 2
    row, col = iota((half, half), 0), iota((half, half), 1)
    first, upper, second = full[:half, :half], full[:half, half:], full[half:, half:]
    both = jnp.where(row <= col, first, second)
    diag = jnp.sum(jnp.where(row == col, second, 0.0), axis=0, keepdims=True)
    return upper, both, diag


def tri_unpack(upper, both, diag):
    half = both.shape[0]
    row, col = iota((half, half), 0), iota((half, half), 1)
    turned = both.T
    first = jnp.where(row <= col, both, turned)
    second = jnp.where(row > col, both, jnp.where(row == col, diag, turned))
    return jnp.concatenate(
        [jnp.concatenate([first, upper], axis=1), jnp.concatenate([upper.T, second], axis=1)],
        axis=0,
    )


def assemble(ext, tile, up, down, left, right):
    height, width, channels = tile.shape
    rows = height + 2 * RIM
    ext[:, 0:LEFT, :] = jnp.zeros((rows, LEFT, channels), F32)
    ext[:, LEFT + width : 2 * LEFT + width, :] = jnp.zeros((rows, LEFT, channels), F32)
    ext[RIM : RIM + height, LEFT : LEFT + width, :] = tile[...].astype(F32)
    ext[0:RIM, LEFT : LEFT + width, :] = up[...].astype(F32)
    ext[RIM + height : rows, LEFT : LEFT + width, :] = down[...].astype(F32)
    ext[:, LEFT - RIM : LEFT, :] = left[...].astype(F32)
    ext[:, LEFT + width : LEFT + width + RIM, :] = right[...].astype(F32)


def load_kernel(count, label, tile_in, tile, bottom, low, high, info):
    height, width, _ = tile.shape
    tile[...] = tile_in[...]
    bottom[...] = tile_in[height - RIM :]
    low[...] = tile_in[:, :RIM, :]
    high[...] = tile_in[:, width - RIM :, :]
    row = iota(info.shape, 0)
    value = jnp.zeros(info.shape, F32)
    for k, scalar in enumerate(
        (count[0], label[0], lax.axis_index("gy"), lax.axis_index("gx"), lax.axis_index("slide"))
    ):
        value = jnp.where(row == k, scalar.astype(jnp.int32).astype(F32), value)
    info[...] = value


def weights_kernel(
    up, own, down, weights, point, classifier, strip, taps, mixing, turned, classes, toward
):
    height, width = own.shape[0], up.shape[1]
    strip[0:RIM] = up[:, width - RIM :, :]
    strip[RIM : RIM + height] = own[...]
    strip[RIM + height :] = down[:, width - RIM :, :]
    taps[...] = jnp.concatenate([weights[a].astype(F32) for a in range(3)], axis=0)
    mixing[...] = point[...]
    turned[...] = point[...].astype(F32).T.astype(BF16)
    classes[...] = classifier[...]
    gap = classifier[0] - classifier[1]
    toward[...] = gap + gap.T


def forward_kernel(
    planes, info, tile, up, down, left, right, weights, point, mapped, packed, ext, hidden, inner
):
    height, width, channels = tile.shape
    wide = ext.shape[1]
    assemble(ext, tile, up, down, left, right)
    valid = jnp.broadcast_to(info[0:1, :].astype(jnp.int32), (width, LANES))
    order = iota((width, LANES), 0)

    for lane in range(0, channels, LANES):
        part = slice(lane, lane + LANES)
        taps = [weights[k : k + 1, part] for k in range(9)]

        def body(r, carry, part=part, taps=taps):
            rows = [ext[r + a, :, part] for a in range(3)]
            cols = [sum(rows[a] * taps[3 * a + b] for a in range(3)) for b in range(3)]
            value = cols[1] + shifted(cols[0], 1) + shifted(cols[2], -1)
            hidden[pl.ds(pl.multiple_of(r * wide, 16), wide), part] = value.astype(BF16)

            @pl.when((r >= 1) & (r <= height))
            def _():
                kept = jnp.where(order < valid - (r - 1) * width, value[LEFT : LEFT + width], 0.0)
                start = pl.multiple_of((r - 1) * width, 16)
                inner[pl.ds(start, width), part] = kept.astype(BF16)

            return carry

        lax.fori_loop(0, height + 2, body, 0)

    kept = inner[...]
    gram = lax.dot_general(kept, kept, (((0,), (0,)), ((), ())), preferred_element_type=F32)
    mapped[...] = dot(hidden[...], point[...]).astype(BF16)
    sums = jnp.sum(kept.astype(F32), axis=0, keepdims=True)
    upper, both, diag = tri_pack(gram)
    chunks = packed.shape[1] - 1
    spare = chunks * planes - 2 * LANES - 3
    flat = jnp.concatenate(
        [upper, both, diag, sums[:, :LANES], sums[:, LANES:], jnp.zeros((spare, LANES), F32)],
        axis=0,
    )
    for q in range(chunks):
        packed[:, q, :] = flat[q * planes : (q + 1) * planes]
    packed[:, chunks, :] = jnp.zeros((planes, LANES), F32)


def plane_sum_kernel(info, terms, out):
    planes, rows, lanes = terms.shape
    summed = jnp.sum(terms[...], axis=0)
    summed = jnp.where(iota((rows, lanes), 0) == rows - 1, info[0:1, 0:1], summed)
    out[...] = jnp.broadcast_to(summed[None], out.shape)


def cov_kernel(
    grid_y, grid_x, slides, info, gathered, ext, mapped, toward_ref, point, point_turned,
    classifier, back_out, sent, back, sem,
):
    planes = grid_y * grid_x
    wide, channels = ext.shape[1:]
    height, width = ext.shape[0] - 2 * RIM, wide - 2 * LEFT
    half = channels // 2
    chunks = gathered.shape[1] - 1

    flat = jnp.concatenate([gathered[:, q, :] for q in range(chunks)], axis=0)
    counts = gathered[:, chunks, :]
    inverse = 1.0 / jnp.sum(counts, axis=0, keepdims=True)[:, 0:1]
    gram = tri_unpack(flat[:half], flat[half : 2 * half], flat[2 * half : 2 * half + 1])
    sums = jnp.concatenate(
        [flat[2 * half + 1 : 2 * half + 2], flat[2 * half + 2 : 2 * half + 3]], axis=1
    )
    center = sums * inverse
    spread = jnp.broadcast_to(center, (channels, channels))
    moment = gram * inverse - spread * spread.T

    mixing, mixing_turned = point[...], point_turned[...]
    high, low = split(moment)
    moved = dot(
        jnp.concatenate([high, low], axis=1), jnp.concatenate([mixing, mixing], axis=0)
    )
    moved_pair = split(moved)
    sigma = dot(
        jnp.concatenate([mixing_turned, mixing_turned], axis=1),
        jnp.concatenate(moved_pair, axis=0),
    )
    sigma = 0.5 * (sigma + sigma.T)
    eye = iota((channels, channels), 0) == iota((channels, channels), 1)
    trace = total(jnp.where(eye, sigma, 0.0))
    start = sigma * (1.0 / trace)

    toward = toward_ref[...]
    wmat, ymat, dw, dy = start, start, toward, toward
    for step in range(ITERS):
        w_pair, dw_pair = split(wmat), split(dw)
        both = beside(w_pair, dw_pair)
        if step == 0:
            first = mm(w_pair, both)
            square, cross = first[:, :channels], first[:, channels:]
            yw, dyw = square, cross + cross.T
        elif step + 1 < ITERS:
            first = mm(stack(w_pair, split(ymat)), both)
            square, cross = first[:channels, :channels], first[:channels, channels:]
            yw = first[channels:, :channels]
            dyw = first[channels:, channels:] + mm(split(dy), w_pair)
        else:
            first = mm(split(ymat), both)
            yw = first[:, :channels]
            dyw = first[:, channels:] + mm(split(dy), w_pair)
        ymat = 1.5 * ymat - 0.5 * yw
        dy = 1.5 * dy - 0.5 * dyw
        if step + 1 < ITERS:
            dsquare = cross + cross.T
            third = mm(split(square), both)
            dcube = third[:, channels:] + mm(split(dsquare), w_pair)
            wmat = 2.25 * wmat - 1.5 * square + 0.25 * third[:, :channels]
            dw = 2.25 * dw - 1.5 * dsquare + 0.25 * dcube

    root = jnp.sqrt(trace)
    pooled = root * ymat
    logit0 = total(classifier[0] * pooled)
    logit1 = total(classifier[1] * pooled)
    peak = jnp.maximum(logit0, logit1)
    lse = peak + jnp.log(jnp.exp(logit0 - peak) + jnp.exp(logit1 - peak))
    is_zero = info[1:2, 0:1] == 0.0
    slope = jnp.where(is_zero, -jnp.exp(logit1 - lse), jnp.exp(logit0 - lse)) * (1.0 / slides)
    loss = (lse - jnp.where(is_zero, logit0, logit1)) * (1.0 / slides)

    level = 0.5 * total(toward * ymat) - total(dy * start)
    slant = (dy + jnp.where(eye, level, 0.0)) * (slope / root)
    slant = 0.5 * (slant + slant.T)
    point_term = mm(moved_pair, split(slant))
    class_term = slope * pooled
    class_term = 0.5 * (class_term + class_term.T)

    symmetric = slant * inverse
    sym_pair = split(symmetric)
    center_pair = split(jnp.broadcast_to(center, (8, channels)))
    mean = dot(
        jnp.concatenate(center_pair, axis=1), jnp.concatenate([mixing, mixing], axis=0)
    )
    offset = -mm(split(mean), sym_pair)[0:1]

    row_id = iota((planes, LANES), 0).astype(F32)
    spots = []
    for dy_ in (-1, 0, 1):
        for dx_ in (-1, 0, 1):
            near_y, near_x = info[2:3, 0:1] + dy_, info[3:4, 0:1] + dx_
            inside = (near_y >= 0) & (near_y < grid_y) & (near_x >= 0) & (near_x < grid_x)
            spot = jnp.where(inside, near_y * grid_x + near_x, -1.0)
            near = jnp.sum(jnp.where(row_id == spot, counts, 0.0), axis=0, keepdims=True)
            spots.append(near[:, 0:1])

    both = dot(mapped[...], sym_pair[0]) + dot(mapped[...], sym_pair[1]) + offset
    lane_col = iota((wide, channels), 0) - LEFT
    inner_col = jnp.where(lane_col < 0, lane_col + width, jnp.where(lane_col >= width, lane_col - width, lane_col))
    seen = (lane_col >= -1) & (lane_col <= width)
    limits = []
    for k in range(3):
        limit = jnp.where(
            lane_col < 0, spots[3 * k], jnp.where(lane_col >= width, spots[3 * k + 2], spots[3 * k + 1])
        )
        limits.append(jnp.where(seen, limit, -1.0))
    pieces = []
    for r in range(height + 2):
        tile_row = (r - 1) % height
        limit = limits[0 if r == 0 else (2 if r == height + 1 else 1)]
        raster = (tile_row * width + inner_col).astype(F32)
        pieces.append(jnp.where(raster < limit, both[r * wide : (r + 1) * wide], 0.0).astype(BF16))
    back_mapped = jnp.concatenate(pieces, axis=0)
    back[...] = dot(back_mapped, mixing_turned).astype(BF16)
    copy = pltpu.make_async_copy(back, back_out, sem)
    copy.start()

    depth = []
    for lane in range(0, channels, LANES):
        part = slice(lane, lane + LANES)
        column = iota((wide, LANES), 0)
        within = (column >= LEFT) & (column < LEFT + width)

        def body(i, sums, part=part, within=within):
            start = pl.multiple_of((i + 1) * wide, 16)
            own = jnp.where(within, back[pl.ds(start, wide), part].astype(F32), 0.0)
            moved_own = [shifted(own, -1), own, shifted(own, 1)]
            feats = [ext[i + 1 + a, :, part] for a in range(3)]
            out = []
            for a in range(3):
                for b in range(3):
                    product = (feats[a] * moved_own[b]).reshape(wide // 8, 8, LANES)
                    out.append(sums[3 * a + b] + jnp.sum(product, axis=0))
            return tuple(out)

        sums = lax.fori_loop(
            0, height, body, tuple(jnp.zeros((8, LANES), F32) for _ in range(9))
        )
        depth.append(
            jnp.concatenate([jnp.sum(s, axis=0, keepdims=True) for s in sums], axis=0)
        )
    depth = jnp.concatenate(depth, axis=1)

    upper, tri, diag = tri_pack(class_term)
    class_flat = jnp.concatenate([upper, tri], axis=0)
    extra = jnp.concatenate([diag, jnp.broadcast_to(loss, (1, half))], axis=1)
    small = jnp.concatenate([depth, extra, jnp.zeros((6, channels), F32)], axis=0)
    rp, rc, rd = channels // slides, channels // slides // 2, 16 // slides
    pad = [jnp.zeros((8 - rd, channels), F32)] if rd < 8 else []
    for k in range(slides):
        sent[k, 0:rp, :] = point_term[k * rp : (k + 1) * rp]
        sent[k, rp : rp + rc, 0:half] = class_flat[k * rp : k * rp + rc]
        sent[k, rp : rp + rc, half:channels] = class_flat[k * rp + rc : (k + 1) * rp]
        sent[k, rp + rc : rp + rc + 8, :] = jnp.concatenate(
            [small[k * rd : (k + 1) * rd]] + pad, axis=0
        )
    copy.wait()


def spread_kernel(back, weights, gradient):
    height, width, channels = gradient.shape
    wide = width + 2 * LEFT
    for lane in range(0, channels, LANES):
        part = slice(lane, lane + LANES)
        taps = [weights[k : k + 1, part] for k in range(9)]

        def body(i, carry, part=part, taps=taps):
            rows = [
                back[pl.ds(pl.multiple_of((i + a) * wide, 16), wide), part].astype(F32)
                for a in range(3)
            ]
            cols = [sum(rows[2 - a] * taps[3 * a + b] for a in range(3)) for b in range(3)]
            value = cols[1] + shifted(cols[0], -1) + shifted(cols[2], 1)
            gradient[i, :, part] = value[LEFT : LEFT + width].astype(BF16)
            return carry

        lax.fori_loop(0, height, body, 0)


def slide_sum_kernel(rd, terms, shares, small, spread):
    slides, rows, channels = terms.shape
    main = rows - 8
    summed = terms[0]
    for k in range(1, slides):
        summed = summed + terms[k]
    shares[...] = summed[:main].astype(BF16)
    tail = summed[main:]
    small[...] = tail
    lines = jnp.concatenate(
        [tail[q : q + 1, p : p + LANES] for q in range(rd) for p in range(0, channels, LANES)],
        axis=0,
    )
    spread[...] = jnp.broadcast_to(lines.astype(BF16)[None], spread.shape)


def join_kernel(rd, info, shares, small, spread, out):
    slides, rows, channels = out.shape
    summed = jnp.sum(spread[...].astype(F32), axis=0)
    per = channels // LANES
    tail = jnp.concatenate(
        [
            jnp.concatenate([summed[per * q + p : per * q + p + 1] for p in range(per)], axis=1)
            for q in range(rd)
        ],
        axis=0,
    )
    line = info[4:5, 0:1] * rd + iota((rd, channels), 0).astype(F32)
    tail = jnp.where(line < 9, tail, small[:rd])
    high, low = split(tail)
    tail = jnp.concatenate([high, low, jnp.zeros((16 - 2 * rd, channels), BF16)], axis=0)
    for k in range(slides):
        out[k, 0 : rows - 16, :] = shares[...]
        out[k, rows - 16 : rows, :] = tail


def finish_kernel(terms, loss, depth, point, classes):
    slides, rows, channels = terms.shape
    half = channels // 2
    rp, rc, rd = channels // slides, channels // slides // 2, 16 // slides
    flat, small = [], []
    for k in range(slides):
        piece = terms[k].astype(F32)
        point[k * rp : (k + 1) * rp, :] = piece[:rp]
        flat += [piece[rp : rp + rc, :half], piece[rp : rp + rc, half:]]
        tail = piece[rp + rc :]
        small.append(tail[:rd] + tail[rd : 2 * rd])
    flat = jnp.concatenate(flat, axis=0)
    small = jnp.concatenate(small, axis=0)
    full = tri_unpack(flat[:half], flat[half:], small[9:10, :half])
    classes[0] = full
    classes[1] = -full
    for a in range(3):
        depth[a] = small[3 * a : 3 * a + 3]
    loss[...] = small[9:10, half : half + 1]


def per_device(features, depth_weight, point_weight, classifier, valid_count, labels):
    slides, grid_y, grid_x = (lax.axis_size(axis) for axis in ("slide", "gy", "gx"))
    planes = grid_y * grid_x
    tile = features[0]
    height, width, channels = tile.shape
    wide = width + 2 * LEFT

    def upward(part, axis):
        pairs = [(i, i + 1) for i in range(lax.axis_size(axis) - 1)]
        return lax.ppermute(part, axis, pairs)

    def downward(part, axis):
        pairs = [(i + 1, i) for i in range(lax.axis_size(axis) - 1)]
        return lax.ppermute(part, axis, pairs)

    square = jax.ShapeDtypeStruct((channels, channels), BF16)
    strip = jax.ShapeDtypeStruct((height, RIM, channels), BF16)
    down = downward(tile[:RIM], "gy")
    tile, bottom, low, high, info = pl.pallas_call(
        load_kernel,
        out_shape=(
            jax.ShapeDtypeStruct(tile.shape, BF16),
            jax.ShapeDtypeStruct((RIM, width, channels), BF16),
            strip,
            strip,
            jax.ShapeDtypeStruct((8, LANES), F32),
        ),
        in_specs=[SMEM, SMEM, VMEM],
        out_specs=(VMEM,) * 5,
        compiler_params=SMALL,
        name="load",
    )(valid_count.reshape(1), labels, tile)
    up = upward(bottom, "gy")

    right = downward(
        jnp.concatenate([up[:, :RIM], low, down[:, :RIM]], axis=0), "gx"
    )
    strip, weights, point, point_turned, classes, toward = pl.pallas_call(
        weights_kernel,
        out_shape=(
            jax.ShapeDtypeStruct((height + 2 * RIM, RIM, channels), BF16),
            jax.ShapeDtypeStruct((9, channels), F32),
            square,
            square,
            jax.ShapeDtypeStruct(classifier.shape, F32),
            jax.ShapeDtypeStruct((channels, channels), F32),
        ),
        in_specs=[VMEM] * 6,
        out_specs=(VMEM,) * 6,
        compiler_params=SMALL,
        name="weights",
    )(up, high, down, depth_weight, point_weight, classifier)
    left = upward(strip, "gx")

    halo = (tile, up, down, left, right)
    chunks = -(-(channels + 3) // planes)
    pixels = (height + 2) * wide
    ext_shape = (height + 2 * RIM, wide, channels)

    mapped, packed, ext = pl.pallas_call(
        functools.partial(forward_kernel, planes),
        out_shape=(
            jax.ShapeDtypeStruct((pixels, channels), BF16),
            jax.ShapeDtypeStruct((planes, chunks + 1, LANES), F32),
            jax.ShapeDtypeStruct(ext_shape, F32),
        ),
        in_specs=[VMEM] * 8,
        out_specs=(VMEM,) * 3,
        scratch_shapes=[
            pltpu.VMEM((pixels, channels), BF16),
            pltpu.VMEM((height * width, channels), BF16),
        ],
        compiler_params=PARAMS,
        name="forward",
    )(info, *halo, weights, point)

    packed = lax.all_to_all(packed, ("gy", "gx"), 0, 0)

    packed = pl.pallas_call(
        plane_sum_kernel,
        out_shape=jax.ShapeDtypeStruct((planes, chunks + 1, LANES), F32),
        in_specs=[VMEM, VMEM],
        out_specs=VMEM,
        compiler_params=SMALL,
        name="plane_sum",
    )(info, packed)
    gathered = lax.all_to_all(packed, ("gy", "gx"), 0, 0)

    rp, rd = channels // slides, 16 // slides
    main = rp + rp // 2
    back, sent = pl.pallas_call(
        functools.partial(cov_kernel, grid_y, grid_x, slides),
        out_shape=(
            jax.ShapeDtypeStruct((pixels, channels), BF16),
            jax.ShapeDtypeStruct((slides, main + 8, channels), F32),
        ),
        in_specs=[VMEM] * 8,
        out_specs=(HBM, VMEM),
        scratch_shapes=[pltpu.VMEM((pixels, channels), BF16), pltpu.SemaphoreType.DMA],
        compiler_params=PARAMS,
        name="covariance",
    )(info, gathered, ext, mapped, toward, point, point_turned, classes)

    received = lax.all_to_all(sent, "slide", 0, 0)
    gradient = pl.pallas_call(
        spread_kernel,
        out_shape=jax.ShapeDtypeStruct((height, width, channels), BF16),
        in_specs=[VMEM, VMEM],
        out_specs=VMEM,
        compiler_params=PARAMS,
        cost_estimate=pl.CostEstimate(
            flops=20 * pixels * channels, bytes_accessed=4 << 20, transcendentals=0
        ),
        name="spread",
    )(back, weights)
    shares, small, spread = pl.pallas_call(
        functools.partial(slide_sum_kernel, rd),
        out_shape=(
            jax.ShapeDtypeStruct((main, channels), BF16),
            jax.ShapeDtypeStruct((8, channels), F32),
            jax.ShapeDtypeStruct((planes, rd * channels // LANES, LANES), BF16),
        ),
        in_specs=[VMEM],
        out_specs=(VMEM, VMEM, VMEM),
        compiler_params=SMALL,
        name="slide_sum",
    )(received)
    spread = lax.all_to_all(spread, ("gy", "gx"), 0, 0)
    spread, gradient = lax.optimization_barrier((spread, gradient))
    joined = pl.pallas_call(
        functools.partial(join_kernel, rd),
        out_shape=jax.ShapeDtypeStruct((slides, main + 16, channels), BF16),
        in_specs=[VMEM] * 4,
        out_specs=VMEM,
        compiler_params=SMALL,
        name="join",
    )(info, shares, small, spread)
    joined = lax.all_to_all(joined, "slide", 0, 0)
    loss, depth, point_total, class_total = pl.pallas_call(
        finish_kernel,
        out_shape=(
            jax.ShapeDtypeStruct((1, 1), F32),
            jax.ShapeDtypeStruct((3, 3, channels), F32),
            jax.ShapeDtypeStruct((channels, channels), F32),
            jax.ShapeDtypeStruct(classifier.shape, F32),
        ),
        in_specs=[VMEM],
        out_specs=(VMEM, VMEM, VMEM, VMEM),
        compiler_params=SMALL,
        name="finish",
    )(joined)
    return loss.reshape(()), depth, point_total, class_total, gradient[None]


def solution(mesh):
    placed = (P("slide", "gy", "gx", None), P(), P(), P(), P("slide", "gy", "gx"), P("slide"))
    return jax.shard_map(
        per_device,
        mesh=mesh,
        in_specs=placed,
        out_specs=(P(), P(), P(), P(), P("slide", "gy", "gx", None)),
        check_vma=False,
    )
```

```python
import functools

import jax
import jax.numpy as jnp
from jax import lax
from jax.experimental import pallas as pl
from jax.experimental.pallas import tpu as pltpu
from jax.sharding import PartitionSpec as P

ITERS = 5
RIM = 2
LEFT = 8
LANES = 128
F32 = jnp.float32
BF16 = jnp.bfloat16
VMEM = pl.BlockSpec(memory_space=pltpu.VMEM)
HBM = pl.BlockSpec(memory_space=pltpu.HBM)
SMEM = pl.BlockSpec(memory_space=pltpu.SMEM)
PARAMS = pltpu.CompilerParams(vmem_limit_bytes=16 * 1024 * 1024)
SMALL = pltpu.CompilerParams(vmem_limit_bytes=4 * 1024 * 1024)


def iota(shape, dim):
    return lax.broadcasted_iota(jnp.int32, shape, dim)


def total(x):
    return jnp.sum(jnp.sum(x, axis=1, keepdims=True), axis=0, keepdims=True)


def dot(left, right):
    return jnp.dot(left, right, preferred_element_type=F32)


def split(x):
    high = x.astype(BF16)
    return high, (x - high.astype(F32)).astype(BF16)


def mm(left, right):
    lhs = jnp.concatenate([left[0], left[1], left[0]], axis=1)
    rhs = jnp.concatenate([right[0], right[0], right[1]], axis=0)
    return dot(lhs, rhs)


def stack(*pairs):
    return tuple(jnp.concatenate([pair[i] for pair in pairs], axis=0) for i in range(2))


def beside(*pairs):
    return tuple(jnp.concatenate([pair[i] for pair in pairs], axis=1) for i in range(2))


def shifted(x, step):
    return pltpu.roll(x, step % x.shape[0], 0)


def tri_pack(full):
    half = full.shape[0] // 2
    row, col = iota((half, half), 0), iota((half, half), 1)
    first, upper, second = full[:half, :half], full[:half, half:], full[half:, half:]
    both = jnp.where(row <= col, first, second)
    diag = jnp.sum(jnp.where(row == col, second, 0.0), axis=0, keepdims=True)
    return upper, both, diag


def tri_unpack(upper, both, diag):
    half = both.shape[0]
    row, col = iota((half, half), 0), iota((half, half), 1)
    turned = both.T
    first = jnp.where(row <= col, both, turned)
    second = jnp.where(row > col, both, jnp.where(row == col, diag, turned))
    return jnp.concatenate(
        [jnp.concatenate([first, upper], axis=1), jnp.concatenate([upper.T, second], axis=1)],
        axis=0,
    )


def assemble(ext, tile, up, down, left, right):
    height, width, channels = tile.shape
    rows = height + 2 * RIM
    ext[:, 0:LEFT, :] = jnp.zeros((rows, LEFT, channels), F32)
    ext[:, LEFT + width : 2 * LEFT + width, :] = jnp.zeros((rows, LEFT, channels), F32)
    ext[RIM : RIM + height, LEFT : LEFT + width, :] = tile[...].astype(F32)
    ext[0:RIM, LEFT : LEFT + width, :] = up[...].astype(F32)
    ext[RIM + height : rows, LEFT : LEFT + width, :] = down[...].astype(F32)
    ext[:, LEFT - RIM : LEFT, :] = left[...].astype(F32)
    ext[:, LEFT + width : LEFT + width + RIM, :] = right[...].astype(F32)


def load_kernel(tile_in, tile, low, high):
    width = tile.shape[1]
    tile[...] = tile_in[...]
    low[...] = tile_in[:, :RIM, :]
    high[...] = tile_in[:, width - RIM :, :]


def weights_kernel(count, label, strip, weights, point, taps, mixing, turned, info):
    taps[...] = jnp.concatenate([weights[a].astype(F32) for a in range(3)], axis=0)
    mixing[...] = point[...]
    turned[...] = point[...].astype(F32).T.astype(BF16)
    row = iota(info.shape, 0)
    value = jnp.zeros(info.shape, F32)
    scalars = [count[0], label[0]] + [lax.axis_index(axis) for axis in ("gy", "gx", "slide")]
    for k, scalar in enumerate(scalars):
        value = jnp.where(row == k, scalar.astype(jnp.int32).astype(F32), value)
    info[...] = value


def forward_kernel(
    planes, info, tile, up, down, left, right, weights, point, mapped, packed, ext, hidden, inner
):
    height, width, channels = tile.shape
    wide = ext.shape[1]
    assemble(ext, tile, up, down, left, right)
    valid = jnp.broadcast_to(info[0:1, :].astype(jnp.int32), (width, LANES))
    order = iota((width, LANES), 0)

    for lane in range(0, channels, LANES):
        part = slice(lane, lane + LANES)
        taps = [weights[k : k + 1, part] for k in range(9)]

        def body(r, carry, part=part, taps=taps):
            rows = [ext[r + a, :, part] for a in range(3)]
            cols = [sum(rows[a] * taps[3 * a + b] for a in range(3)) for b in range(3)]
            value = cols[1] + shifted(cols[0], 1) + shifted(cols[2], -1)
            hidden[pl.ds(pl.multiple_of(r * wide, 16), wide), part] = value.astype(BF16)

            @pl.when((r >= 1) & (r <= height))
            def _():
                kept = jnp.where(order < valid - (r - 1) * width, value[LEFT : LEFT + width], 0.0)
                start = pl.multiple_of((r - 1) * width, 16)
                inner[pl.ds(start, width), part] = kept.astype(BF16)

            return carry

        lax.fori_loop(0, height + 2, body, 0)

    kept = inner[...]
    gram = lax.dot_general(kept, kept, (((0,), (0,)), ((), ())), preferred_element_type=F32)
    mapped[...] = dot(hidden[...], point[...]).astype(BF16)
    ones = jnp.ones((16, height * width), BF16)
    sums = dot(ones, kept)[0:1]
    first = dot(ones, dot(kept, point[...]).astype(BF16))[0:1]
    upper, both, diag = tri_pack(gram)
    chunks = packed.shape[1] - 1
    lines = [line[:, p : p + LANES] for line in (sums, first) for p in range(0, channels, LANES)]
    spare = chunks * planes - 2 * LANES - 1 - len(lines)
    flat = jnp.concatenate(
        [upper, both, diag] + lines + [jnp.zeros((spare, LANES), F32)], axis=0
    )
    for q in range(chunks):
        packed[:, q, :] = flat[q * planes : (q + 1) * planes]
    packed[:, chunks, :] = jnp.zeros((planes, LANES), F32)


def plane_sum_kernel(info, terms, out):
    planes, rows, lanes = terms.shape
    summed = jnp.sum(terms[...], axis=0)
    summed = jnp.where(iota((rows, lanes), 0) == rows - 1, info[0:1, 0:1], summed)
    out[...] = jnp.broadcast_to(summed[None], out.shape)


def cov_kernel(
    grid_y, grid_x, slides, info, gathered, ext, mapped, point, point_turned, classes,
    back_out, sent, back, classifier, sems,
):
    planes = grid_y * grid_x
    wide, channels = ext.shape[1:]
    height, width = ext.shape[0] - 2 * RIM, wide - 2 * LEFT
    half = channels // 2
    chunks = gathered.shape[1] - 1

    fetch = pltpu.make_async_copy(classes, classifier, sems.at[0])
    fetch.start()
    flat = jnp.concatenate([gathered[:, q, :] for q in range(chunks)], axis=0)
    counts = gathered[:, chunks, :]
    inverse = 1.0 / jnp.sum(counts, axis=0, keepdims=True)[:, 0:1]
    gram = tri_unpack(flat[:half], flat[half : 2 * half], flat[2 * half : 2 * half + 1])
    sums = jnp.concatenate(
        [flat[2 * half + 1 : 2 * half + 2], flat[2 * half + 2 : 2 * half + 3]], axis=1
    )
    mapped_sum = jnp.concatenate(
        [flat[2 * half + 3 : 2 * half + 4], flat[2 * half + 4 : 2 * half + 5]], axis=1
    )
    center = sums * inverse
    spread = jnp.broadcast_to(center, (channels, channels))
    moment = gram * inverse - spread * spread.T

    mixing, mixing_turned = point[...], point_turned[...]
    high, low = split(moment)
    moved = dot(
        jnp.concatenate([high, low], axis=1), jnp.concatenate([mixing, mixing], axis=0)
    )
    moved_pair = split(moved)
    sigma = dot(
        jnp.concatenate([mixing_turned, mixing_turned], axis=1),
        jnp.concatenate(moved_pair, axis=0),
    )
    sigma = 0.5 * (sigma + sigma.T)
    eye = iota((channels, channels), 0) == iota((channels, channels), 1)
    trace = total(jnp.where(eye, sigma, 0.0))
    start = sigma * (1.0 / trace)

    fetch.wait()
    toward = classifier[0] - classifier[1]
    toward = toward + toward.T
    wmat, ymat, dw, dy = start, start, toward, toward
    for step in range(ITERS):
        w_pair, dw_pair = split(wmat), split(dw)
        both = beside(w_pair, dw_pair)
        if step == 0:
            first = mm(w_pair, both)
            square, cross = first[:, :channels], first[:, channels:]
            yw, dyw = square, cross + cross.T
        elif step + 1 < ITERS:
            first = mm(stack(w_pair, split(ymat)), both)
            square, cross = first[:channels, :channels], first[:channels, channels:]
            yw = first[channels:, :channels]
            dyw = first[channels:, channels:] + mm(split(dy), w_pair)
        else:
            first = mm(split(ymat), both)
            yw = first[:, :channels]
            dyw = first[:, channels:] + mm(split(dy), w_pair)
        ymat = 1.5 * ymat - 0.5 * yw
        dy = 1.5 * dy - 0.5 * dyw
        if step + 1 < ITERS:
            dsquare = cross + cross.T
            third = mm(split(square), both)
            dcube = third[:, channels:] + mm(split(dsquare), w_pair)
            wmat = 2.25 * wmat - 1.5 * square + 0.25 * third[:, :channels]
            dw = 2.25 * dw - 1.5 * dsquare + 0.25 * dcube

    root = jnp.sqrt(trace)
    pooled = root * ymat
    logit0 = total(classifier[0] * pooled)
    logit1 = total(classifier[1] * pooled)
    peak = jnp.maximum(logit0, logit1)
    lse = peak + jnp.log(jnp.exp(logit0 - peak) + jnp.exp(logit1 - peak))
    is_zero = info[1:2, 0:1] == 0.0
    slope = jnp.where(is_zero, -jnp.exp(logit1 - lse), jnp.exp(logit0 - lse)) * (1.0 / slides)
    loss = (lse - jnp.where(is_zero, logit0, logit1)) * (1.0 / slides)

    level = 0.5 * total(toward * ymat) - total(dy * start)
    slant = (dy + jnp.where(eye, level, 0.0)) * (slope / root)
    slant = 0.5 * (slant + slant.T)
    point_term = mm(moved_pair, split(slant))
    class_term = slope * pooled
    class_term = 0.5 * (class_term + class_term.T)

    symmetric = slant * inverse
    sym_pair = split(symmetric)
    mean = jnp.broadcast_to(mapped_sum * inverse, (8, channels))
    offset = -mm(split(mean), sym_pair)[0:1]

    row_id = iota((planes, LANES), 0).astype(F32)
    spots = []
    for dy_ in (-1, 0, 1):
        for dx_ in (-1, 0, 1):
            near_y, near_x = info[2:3, 0:1] + dy_, info[3:4, 0:1] + dx_
            inside = (near_y >= 0) & (near_y < grid_y) & (near_x >= 0) & (near_x < grid_x)
            spot = jnp.where(inside, near_y * grid_x + near_x, -1.0)
            near = jnp.sum(jnp.where(row_id == spot, counts, 0.0), axis=0, keepdims=True)
            spots.append(near[:, 0:1])

    both = dot(mapped[...], sym_pair[0]) + dot(mapped[...], sym_pair[1]) + offset
    lane_col = iota((wide, channels), 0) - LEFT
    inner_col = jnp.where(lane_col < 0, lane_col + width, jnp.where(lane_col >= width, lane_col - width, lane_col))
    seen = (lane_col >= -1) & (lane_col <= width)
    limits = []
    for k in range(3):
        limit = jnp.where(
            lane_col < 0, spots[3 * k], jnp.where(lane_col >= width, spots[3 * k + 2], spots[3 * k + 1])
        )
        limits.append(jnp.where(seen, limit, -1.0))
    pieces = []
    for r in range(height + 2):
        tile_row = (r - 1) % height
        limit = limits[0 if r == 0 else (2 if r == height + 1 else 1)]
        raster = (tile_row * width + inner_col).astype(F32)
        pieces.append(jnp.where(raster < limit, both[r * wide : (r + 1) * wide], 0.0).astype(BF16))
    back_mapped = jnp.concatenate(pieces, axis=0)
    back[...] = dot(back_mapped, mixing_turned).astype(BF16)
    copy = pltpu.make_async_copy(back, back_out, sems.at[1])
    copy.start()

    depth = []
    for lane in range(0, channels, LANES):
        part = slice(lane, lane + LANES)
        column = iota((wide, LANES), 0)
        within = (column >= LEFT) & (column < LEFT + width)

        def body(i, sums, part=part, within=within):
            start = pl.multiple_of((i + 1) * wide, 16)
            own = jnp.where(within, back[pl.ds(start, wide), part].astype(F32), 0.0)
            moved_own = [shifted(own, -1), own, shifted(own, 1)]
            feats = [ext[i + 1 + a, :, part] for a in range(3)]
            out = []
            for a in range(3):
                for b in range(3):
                    product = (feats[a] * moved_own[b]).reshape(wide // 8, 8, LANES)
                    out.append(sums[3 * a + b] + jnp.sum(product, axis=0))
            return tuple(out)

        sums = lax.fori_loop(
            0, height, body, tuple(jnp.zeros((8, LANES), F32) for _ in range(9))
        )
        depth.append(
            jnp.concatenate([jnp.sum(s, axis=0, keepdims=True) for s in sums], axis=0)
        )
    depth = jnp.concatenate(depth, axis=1)

    upper, tri, diag = tri_pack(class_term)
    class_flat = jnp.concatenate([upper, tri], axis=0)
    extra = jnp.concatenate([diag, jnp.broadcast_to(loss, (1, half))], axis=1)
    small = jnp.concatenate([depth, extra, jnp.zeros((6, channels), F32)], axis=0)
    rp, rc, rd = channels // slides, channels // slides // 2, 16 // slides
    pad = [jnp.zeros((8 - rd, channels), F32)] if rd < 8 else []
    for k in range(slides):
        sent[k, 0:rp, :] = point_term[k * rp : (k + 1) * rp]
        sent[k, rp : rp + rc, 0:half] = class_flat[k * rp : k * rp + rc]
        sent[k, rp : rp + rc, half:channels] = class_flat[k * rp + rc : (k + 1) * rp]
        sent[k, rp + rc : rp + rc + 8, :] = jnp.concatenate(
            [small[k * rd : (k + 1) * rd]] + pad, axis=0
        )
    copy.wait()


def spread_kernel(back, weights, gradient):
    height, width, channels = gradient.shape
    wide = width + 2 * LEFT
    for lane in range(0, channels, LANES):
        part = slice(lane, lane + LANES)
        taps = [weights[k : k + 1, part] for k in range(9)]

        def body(i, carry, part=part, taps=taps):
            rows = [
                back[pl.ds(pl.multiple_of((i + a) * wide, 16), wide), part].astype(F32)
                for a in range(3)
            ]
            cols = [sum(rows[2 - a] * taps[3 * a + b] for a in range(3)) for b in range(3)]
            value = cols[1] + shifted(cols[0], -1) + shifted(cols[2], 1)
            gradient[i, :, part] = value[LEFT : LEFT + width].astype(BF16)
            return carry

        lax.fori_loop(0, height, body, 0)


def slide_sum_kernel(rd, terms, shares, small, spread):
    slides, rows, channels = terms.shape
    main = rows - 8
    summed = terms[0]
    for k in range(1, slides):
        summed = summed + terms[k]
    shares[...] = summed[:main].astype(BF16)
    tail = summed[main:]
    small[...] = tail
    lines = jnp.concatenate(
        [tail[q : q + 1, p : p + LANES] for q in range(rd) for p in range(0, channels, LANES)],
        axis=0,
    )
    spread[...] = jnp.broadcast_to(lines.astype(BF16)[None], spread.shape)


def join_kernel(rd, info, shares, small, spread, out):
    slides, rows, channels = out.shape
    summed = jnp.sum(spread[...].astype(F32), axis=0)
    per = channels // LANES
    tail = jnp.concatenate(
        [
            jnp.concatenate([summed[per * q + p : per * q + p + 1] for p in range(per)], axis=1)
            for q in range(rd)
        ],
        axis=0,
    )
    line = info[4:5, 0:1] * rd + iota((rd, channels), 0).astype(F32)
    tail = jnp.where(line < 9, tail, small[:rd])
    high, low = split(tail)
    tail = jnp.concatenate([high, low, jnp.zeros((16 - 2 * rd, channels), BF16)], axis=0)
    for k in range(slides):
        out[k, 0 : rows - 16, :] = shares[...]
        out[k, rows - 16 : rows, :] = tail


def finish_kernel(terms, loss, depth, point, classes):
    slides, rows, channels = terms.shape
    half = channels // 2
    rp, rc, rd = channels // slides, channels // slides // 2, 16 // slides
    flat, small = [], []
    for k in range(slides):
        piece = terms[k].astype(F32)
        point[k * rp : (k + 1) * rp, :] = piece[:rp]
        flat += [piece[rp : rp + rc, :half], piece[rp : rp + rc, half:]]
        tail = piece[rp + rc :]
        small.append(tail[:rd] + tail[rd : 2 * rd])
    flat = jnp.concatenate(flat, axis=0)
    small = jnp.concatenate(small, axis=0)
    full = tri_unpack(flat[:half], flat[half:], small[9:10, :half])
    classes[0] = full
    classes[1] = -full
    for a in range(3):
        depth[a] = small[3 * a : 3 * a + 3]
    loss[...] = small[9:10, half : half + 1]


def per_device(features, depth_weight, point_weight, classifier, valid_count, labels):
    slides, grid_y, grid_x = (lax.axis_size(axis) for axis in ("slide", "gy", "gx"))
    planes = grid_y * grid_x
    tile = features[0]
    height, width, channels = tile.shape
    wide = width + 2 * LEFT

    def upward(part, axis):
        pairs = [(i, i + 1) for i in range(lax.axis_size(axis) - 1)]
        return lax.ppermute(part, axis, pairs)

    def downward(part, axis):
        pairs = [(i + 1, i) for i in range(lax.axis_size(axis) - 1)]
        return lax.ppermute(part, axis, pairs)

    square = jax.ShapeDtypeStruct((channels, channels), BF16)
    strip = jax.ShapeDtypeStruct((height, RIM, channels), BF16)
    up, down = upward(tile[height - RIM :], "gy"), downward(tile[:RIM], "gy")
    tile, low, high = pl.pallas_call(
        load_kernel,
        out_shape=(jax.ShapeDtypeStruct(tile.shape, BF16), strip, strip),
        in_specs=[VMEM],
        out_specs=(VMEM,) * 3,
        compiler_params=SMALL,
        name="load",
    )(tile)

    low_strip = jnp.concatenate([up[:, :RIM], low, down[:, :RIM]], axis=0)
    high_strip = jnp.concatenate(
        [up[:, width - RIM :], high, down[:, width - RIM :]], axis=0
    )
    left, right = upward(high_strip, "gx"), downward(low_strip, "gx")
    weights, point, point_turned, info = pl.pallas_call(
        weights_kernel,
        out_shape=(
            jax.ShapeDtypeStruct((9, channels), F32),
            square,
            square,
            jax.ShapeDtypeStruct((8, LANES), F32),
        ),
        in_specs=[SMEM, SMEM] + [VMEM] * 3,
        out_specs=(VMEM,) * 4,
        compiler_params=SMALL,
        name="weights",
    )(valid_count.reshape(1), labels, low_strip, depth_weight, point_weight)

    halo = (tile, up, down, left, right)
    chunks = -(-(channels + 5) // planes)
    pixels = (height + 2) * wide
    ext_shape = (height + 2 * RIM, wide, channels)

    mapped, packed, ext = pl.pallas_call(
        functools.partial(forward_kernel, planes),
        out_shape=(
            jax.ShapeDtypeStruct((pixels, channels), BF16),
            jax.ShapeDtypeStruct((planes, chunks + 1, LANES), F32),
            jax.ShapeDtypeStruct(ext_shape, F32),
        ),
        in_specs=[VMEM] * 8,
        out_specs=(VMEM,) * 3,
        scratch_shapes=[
            pltpu.VMEM((pixels, channels), BF16),
            pltpu.VMEM((height * width, channels), BF16),
        ],
        compiler_params=PARAMS,
        name="forward",
    )(info, *halo, weights, point)

    packed = lax.all_to_all(packed, ("gy", "gx"), 0, 0)

    packed = pl.pallas_call(
        plane_sum_kernel,
        out_shape=jax.ShapeDtypeStruct((planes, chunks + 1, LANES), F32),
        in_specs=[VMEM, VMEM],
        out_specs=VMEM,
        compiler_params=SMALL,
        name="plane_sum",
    )(info, packed)
    gathered = lax.all_to_all(packed, ("gy", "gx"), 0, 0)

    rp, rd = channels // slides, 16 // slides
    main = rp + rp // 2
    back, sent = pl.pallas_call(
        functools.partial(cov_kernel, grid_y, grid_x, slides),
        out_shape=(
            jax.ShapeDtypeStruct((pixels, channels), BF16),
            jax.ShapeDtypeStruct((slides, main + 8, channels), F32),
        ),
        in_specs=[VMEM] * 6 + [HBM],
        out_specs=(HBM, VMEM),
        scratch_shapes=[
            pltpu.VMEM((pixels, channels), BF16),
            pltpu.VMEM(classifier.shape, F32),
            pltpu.SemaphoreType.DMA((2,)),
        ],
        compiler_params=PARAMS,
        name="covariance",
    )(info, gathered, ext, mapped, point, point_turned, classifier)

    received = lax.all_to_all(sent, "slide", 0, 0)
    gradient = pl.pallas_call(
        spread_kernel,
        out_shape=jax.ShapeDtypeStruct((height, width, channels), BF16),
        in_specs=[VMEM, VMEM],
        out_specs=VMEM,
        compiler_params=PARAMS,
        cost_estimate=pl.CostEstimate(
            flops=20 * pixels * channels, bytes_accessed=4 << 20, transcendentals=0
        ),
        name="spread",
    )(back, weights)
    shares, small, spread = pl.pallas_call(
        functools.partial(slide_sum_kernel, rd),
        out_shape=(
            jax.ShapeDtypeStruct((main, channels), BF16),
            jax.ShapeDtypeStruct((8, channels), F32),
            jax.ShapeDtypeStruct((planes, rd * channels // LANES, LANES), BF16),
        ),
        in_specs=[VMEM],
        out_specs=(VMEM, VMEM, VMEM),
        compiler_params=SMALL,
        name="slide_sum",
    )(received)
    spread = lax.all_to_all(spread, ("gy", "gx"), 0, 0)
    spread, gradient = lax.optimization_barrier((spread, gradient))
    joined = pl.pallas_call(
        functools.partial(join_kernel, rd),
        out_shape=jax.ShapeDtypeStruct((slides, main + 16, channels), BF16),
        in_specs=[VMEM] * 4,
        out_specs=VMEM,
        compiler_params=SMALL,
        name="join",
    )(info, shares, small, spread)
    joined = lax.all_to_all(joined, "slide", 0, 0)
    loss, depth, point_total, class_total = pl.pallas_call(
        finish_kernel,
        out_shape=(
            jax.ShapeDtypeStruct((1, 1), F32),
            jax.ShapeDtypeStruct((3, 3, channels), F32),
            jax.ShapeDtypeStruct((channels, channels), F32),
            jax.ShapeDtypeStruct(classifier.shape, F32),
        ),
        in_specs=[VMEM],
        out_specs=(VMEM, VMEM, VMEM, VMEM),
        compiler_params=SMALL,
        name="finish",
    )(joined)
    return loss.reshape(()), depth, point_total, class_total, gradient[None]


def solution(mesh):
    placed = (P("slide", "gy", "gx", None), P(), P(), P(), P("slide", "gy", "gx"), P("slide"))
    return jax.shard_map(
        per_device,
        mesh=mesh,
        in_specs=placed,
        out_specs=(P(), P(), P(), P(), P("slide", "gy", "gx", None)),
        check_vma=False,
    )
```

```python
import functools

import jax
import jax.numpy as jnp
from jax import lax
from jax.experimental import pallas as pl
from jax.experimental.pallas import tpu as pltpu
from jax.sharding import PartitionSpec as P

ITERS = 5
RIM = 2
LEFT = 8
LANES = 128
F32 = jnp.float32
BF16 = jnp.bfloat16
VMEM = pl.BlockSpec(memory_space=pltpu.VMEM)
HBM = pl.BlockSpec(memory_space=pltpu.HBM)
PARAMS = pltpu.CompilerParams(vmem_limit_bytes=16 * 1024 * 1024)
SMALL = pltpu.CompilerParams(vmem_limit_bytes=4 * 1024 * 1024)


def iota(shape, dim):
    return lax.broadcasted_iota(jnp.int32, shape, dim)


def total(x):
    return jnp.sum(jnp.sum(x, axis=1, keepdims=True), axis=0, keepdims=True)


def dot(left, right):
    return jnp.dot(left, right, preferred_element_type=F32)


def split(x):
    high = x.astype(BF16)
    return high, (x - high.astype(F32)).astype(BF16)


def mm(left, right):
    lhs = jnp.concatenate([left[0], left[1], left[0]], axis=1)
    rhs = jnp.concatenate([right[0], right[0], right[1]], axis=0)
    return dot(lhs, rhs)


def stack(*pairs):
    return tuple(jnp.concatenate([pair[i] for pair in pairs], axis=0) for i in range(2))


def beside(*pairs):
    return tuple(jnp.concatenate([pair[i] for pair in pairs], axis=1) for i in range(2))


def shifted(x, step):
    return pltpu.roll(x, step % x.shape[0], 0)


def tri_pack(full):
    half = full.shape[0] // 2
    row, col = iota((half, half), 0), iota((half, half), 1)
    first, upper, second = full[:half, :half], full[:half, half:], full[half:, half:]
    both = jnp.where(row <= col, first, second)
    diag = jnp.sum(jnp.where(row == col, second, 0.0), axis=0, keepdims=True)
    return upper, both, diag


def tri_unpack(upper, both, diag):
    half = both.shape[0]
    row, col = iota((half, half), 0), iota((half, half), 1)
    turned = both.T
    first = jnp.where(row <= col, both, turned)
    second = jnp.where(row > col, both, jnp.where(row == col, diag, turned))
    return jnp.concatenate(
        [jnp.concatenate([first, upper], axis=1), jnp.concatenate([upper.T, second], axis=1)],
        axis=0,
    )


def assemble(ext, tile, up, down, left, right):
    height, width, channels = tile.shape
    rows = height + 2 * RIM
    ext[:, 0:LEFT, :] = jnp.zeros((rows, LEFT, channels), F32)
    ext[:, LEFT + width : 2 * LEFT + width, :] = jnp.zeros((rows, LEFT, channels), F32)
    ext[RIM : RIM + height, LEFT : LEFT + width, :] = tile[...].astype(F32)
    ext[0:RIM, LEFT : LEFT + width, :] = up[...].astype(F32)
    ext[RIM + height : rows, LEFT : LEFT + width, :] = down[...].astype(F32)
    ext[:, LEFT - RIM : LEFT, :] = left[...].astype(F32)
    ext[:, LEFT + width : LEFT + width + RIM, :] = right[...].astype(F32)


def load_kernel(tile_in, tile, low, high):
    width = tile.shape[1]
    tile[...] = tile_in[...]
    low[...] = tile_in[:, :RIM, :]
    high[...] = tile_in[:, width - RIM :, :]


def weights_kernel(scalars, strip, weights, point, taps, mixing, turned, info):
    taps[...] = jnp.concatenate([weights[a].astype(F32) for a in range(3)], axis=0)
    mixing[...] = point[...]
    turned[...] = point[...].astype(F32).T.astype(BF16)
    row = iota(info.shape, 0)
    value = scalars[...]
    for k, axis in enumerate(("gy", "gx", "slide")):
        position = lax.axis_index(axis).astype(jnp.int32).astype(F32)
        value = jnp.where(row == k + 2, position, value)
    info[...] = value


def forward_kernel(
    planes, grid_x, info, tile, up, down, left, right, weights, point, mapped, packed, ext, hidden, inner
):
    height, width, channels = tile.shape
    wide = ext.shape[1]
    assemble(ext, tile, up, down, left, right)
    valid = jnp.broadcast_to(info[0:1, :].astype(jnp.int32), (width, LANES))
    order = iota((width, LANES), 0)

    for lane in range(0, channels, LANES):
        part = slice(lane, lane + LANES)
        taps = [weights[k : k + 1, part] for k in range(9)]

        def body(r, carry, part=part, taps=taps):
            rows = [ext[r + a, :, part] for a in range(3)]
            cols = [sum(rows[a] * taps[3 * a + b] for a in range(3)) for b in range(3)]
            value = cols[1] + shifted(cols[0], 1) + shifted(cols[2], -1)
            hidden[pl.ds(pl.multiple_of(r * wide, 16), wide), part] = value.astype(BF16)

            @pl.when((r >= 1) & (r <= height))
            def _():
                kept = jnp.where(order < valid - (r - 1) * width, value[LEFT : LEFT + width], 0.0)
                start = pl.multiple_of((r - 1) * width, 16)
                inner[pl.ds(start, width), part] = kept.astype(BF16)

            return carry

        lax.fori_loop(0, height + 2, body, 0, unroll=2)

    kept = inner[...]
    gram = lax.dot_general(kept, kept, (((0,), (0,)), ((), ())), preferred_element_type=F32)
    mapped[...] = dot(hidden[...], point[...]).astype(BF16)
    ones = jnp.ones((16, height * width), BF16)
    sums = dot(ones, kept)[0:1]
    first = dot(ones, dot(kept, point[...]).astype(BF16))[0:1]
    upper, both, diag = tri_pack(gram)
    chunks = packed.shape[2] // LANES
    lines = [line[:, p : p + LANES] for line in (sums, first) for p in range(0, channels, LANES)]
    spot = info[2:3, :] * grid_x + info[3:4, :]
    lines.append(jnp.where(iota((1, LANES), 1).astype(F32) == spot, info[0:1, :], 0.0))
    spare = chunks * planes - 2 * LANES - 1 - len(lines)
    flat = jnp.concatenate(
        [upper, both, diag] + lines + [jnp.zeros((spare, LANES), F32)], axis=0
    )
    for q in range(chunks):
        packed[:, 0, q * LANES : (q + 1) * LANES] = flat[q * planes : (q + 1) * planes]


def plane_sum_kernel(terms, out):
    out[...] = jnp.broadcast_to(jnp.sum(terms[...], axis=0, keepdims=True), out.shape)


def cov_kernel(
    grid_y, grid_x, slides, info, gathered, ext, mapped, point, point_turned, classes,
    back_out, sent, back, classifier, sems,
):
    planes = grid_y * grid_x
    wide, channels = ext.shape[1:]
    height, width = ext.shape[0] - 2 * RIM, wide - 2 * LEFT
    half = channels // 2
    chunks = gathered.shape[2] // LANES

    fetch = pltpu.make_async_copy(classes, classifier, sems.at[0])
    fetch.start()
    flat = jnp.concatenate(
        [gathered[:, 0, q * LANES : (q + 1) * LANES] for q in range(chunks)], axis=0
    )
    counts = flat[2 * half + 5 : 2 * half + 6]
    inverse = 1.0 / jnp.sum(counts, axis=1, keepdims=True)
    gram = tri_unpack(flat[:half], flat[half : 2 * half], flat[2 * half : 2 * half + 1])
    sums = jnp.concatenate(
        [flat[2 * half + 1 : 2 * half + 2], flat[2 * half + 2 : 2 * half + 3]], axis=1
    )
    mapped_sum = jnp.concatenate(
        [flat[2 * half + 3 : 2 * half + 4], flat[2 * half + 4 : 2 * half + 5]], axis=1
    )
    center = sums * inverse
    spread = jnp.broadcast_to(center, (channels, channels))
    moment = gram * inverse - spread * spread.T

    mixing, mixing_turned = point[...], point_turned[...]
    high, low = split(moment)
    moved = dot(
        jnp.concatenate([high, low], axis=1), jnp.concatenate([mixing, mixing], axis=0)
    )
    moved_pair = split(moved)
    sigma = dot(
        jnp.concatenate([mixing_turned, mixing_turned], axis=1),
        jnp.concatenate(moved_pair, axis=0),
    )
    sigma = 0.5 * (sigma + sigma.T)
    eye = iota((channels, channels), 0) == iota((channels, channels), 1)
    trace = total(jnp.where(eye, sigma, 0.0))
    start = sigma * (1.0 / trace)

    fetch.wait()
    toward = classifier[0] - classifier[1]
    toward = toward + toward.T
    wmat, ymat, dw, dy = start, start, toward, toward
    for step in range(ITERS):
        w_pair, dw_pair = split(wmat), split(dw)
        both = beside(w_pair, dw_pair)
        if step == 0:
            first = mm(w_pair, both)
            square, cross = first[:, :channels], first[:, channels:]
            yw, dyw = square, cross + cross.T
        elif step + 1 < ITERS:
            first = mm(stack(w_pair, split(ymat)), both)
            square, cross = first[:channels, :channels], first[:channels, channels:]
            yw = first[channels:, :channels]
            dyw = first[channels:, channels:] + mm(split(dy), w_pair)
        else:
            first = mm(split(ymat), both)
            yw = first[:, :channels]
            dyw = first[:, channels:] + mm(split(dy), w_pair)
        ymat = 1.5 * ymat - 0.5 * yw
        dy = 1.5 * dy - 0.5 * dyw
        if step + 1 < ITERS:
            dsquare = cross + cross.T
            third = mm(split(square), both)
            dcube = third[:, channels:] + mm(split(dsquare), w_pair)
            wmat = 2.25 * wmat - 1.5 * square + 0.25 * third[:, :channels]
            dw = 2.25 * dw - 1.5 * dsquare + 0.25 * dcube

    root = jnp.sqrt(trace)
    pooled = root * ymat
    logit0 = total(classifier[0] * pooled)
    logit1 = total(classifier[1] * pooled)
    peak = jnp.maximum(logit0, logit1)
    lse = peak + jnp.log(jnp.exp(logit0 - peak) + jnp.exp(logit1 - peak))
    is_zero = info[1:2, 0:1] == 0.0
    slope = jnp.where(is_zero, -jnp.exp(logit1 - lse), jnp.exp(logit0 - lse)) * (1.0 / slides)
    loss = (lse - jnp.where(is_zero, logit0, logit1)) * (1.0 / slides)

    level = 0.5 * total(toward * ymat) - total(dy * start)
    slant = (dy + jnp.where(eye, level, 0.0)) * (slope / root)
    slant = 0.5 * (slant + slant.T)
    point_term = mm(moved_pair, split(slant))
    class_term = slope * pooled
    class_term = 0.5 * (class_term + class_term.T)

    symmetric = slant * inverse
    sym_pair = split(symmetric)
    mean = jnp.broadcast_to(mapped_sum * inverse, (8, channels))
    offset = -mm(split(mean), sym_pair)[0:1]

    place = iota((1, LANES), 1).astype(F32)
    spots = []
    for dy_ in (-1, 0, 1):
        for dx_ in (-1, 0, 1):
            near_y, near_x = info[2:3, 0:1] + dy_, info[3:4, 0:1] + dx_
            inside = (near_y >= 0) & (near_y < grid_y) & (near_x >= 0) & (near_x < grid_x)
            spot = jnp.where(inside, near_y * grid_x + near_x, -1.0)
            near = jnp.where(place == spot, counts, 0.0)
            spots.append(jnp.sum(near, axis=1, keepdims=True))

    both = dot(mapped[...], sym_pair[0]) + dot(mapped[...], sym_pair[1]) + offset
    lane_col = iota((wide, channels), 0) - LEFT
    inner_col = jnp.where(lane_col < 0, lane_col + width, jnp.where(lane_col >= width, lane_col - width, lane_col))
    seen = (lane_col >= -1) & (lane_col <= width)
    limits = []
    for k in range(3):
        limit = jnp.where(
            lane_col < 0, spots[3 * k], jnp.where(lane_col >= width, spots[3 * k + 2], spots[3 * k + 1])
        )
        limits.append(jnp.where(seen, limit, -1.0))
    pieces = []
    for r in range(height + 2):
        tile_row = (r - 1) % height
        limit = limits[0 if r == 0 else (2 if r == height + 1 else 1)]
        raster = (tile_row * width + inner_col).astype(F32)
        pieces.append(jnp.where(raster < limit, both[r * wide : (r + 1) * wide], 0.0).astype(BF16))
    back_mapped = jnp.concatenate(pieces, axis=0)
    back[...] = dot(back_mapped, mixing_turned).astype(BF16)
    copy = pltpu.make_async_copy(back, back_out, sems.at[1])
    copy.start()

    depth = []
    for lane in range(0, channels, LANES):
        part = slice(lane, lane + LANES)
        column = iota((wide, LANES), 0)
        within = (column >= LEFT) & (column < LEFT + width)

        def body(i, sums, part=part, within=within):
            start = pl.multiple_of((i + 1) * wide, 16)
            own = jnp.where(within, back[pl.ds(start, wide), part].astype(F32), 0.0)
            moved_own = [shifted(own, -1), own, shifted(own, 1)]
            feats = [ext[i + 1 + a, :, part] for a in range(3)]
            out = []
            for a in range(3):
                for b in range(3):
                    product = (feats[a] * moved_own[b]).reshape(wide // 8, 8, LANES)
                    out.append(sums[3 * a + b] + jnp.sum(product, axis=0))
            return tuple(out)

        sums = lax.fori_loop(
            0, height, body, tuple(jnp.zeros((8, LANES), F32) for _ in range(9)), unroll=2
        )
        depth.append(
            jnp.concatenate([jnp.sum(s, axis=0, keepdims=True) for s in sums], axis=0)
        )
    depth = jnp.concatenate(depth, axis=1)

    upper, tri, diag = tri_pack(class_term)
    class_flat = jnp.concatenate([upper, tri], axis=0)
    extra = jnp.concatenate([diag, jnp.broadcast_to(loss, (1, half))], axis=1)
    small = jnp.concatenate([depth, extra, jnp.zeros((6, channels), F32)], axis=0)
    rp, rc, rd = channels // slides, channels // slides // 2, 16 // slides
    pad = [jnp.zeros((8 - rd, channels), F32)] if rd < 8 else []
    for k in range(slides):
        sent[k, 0:rp, :] = point_term[k * rp : (k + 1) * rp]
        sent[k, rp : rp + rc, 0:half] = class_flat[k * rp : k * rp + rc]
        sent[k, rp : rp + rc, half:channels] = class_flat[k * rp + rc : (k + 1) * rp]
        sent[k, rp + rc : rp + rc + 8, :] = jnp.concatenate(
            [small[k * rd : (k + 1) * rd]] + pad, axis=0
        )
    copy.wait()


def spread_kernel(back, weights, gradient):
    height, width, channels = gradient.shape
    wide = width + 2 * LEFT
    for lane in range(0, channels, LANES):
        part = slice(lane, lane + LANES)
        taps = [weights[k : k + 1, part] for k in range(9)]

        def body(i, carry, part=part, taps=taps):
            rows = [
                back[pl.ds(pl.multiple_of((i + a) * wide, 16), wide), part].astype(F32)
                for a in range(3)
            ]
            cols = [sum(rows[2 - a] * taps[3 * a + b] for a in range(3)) for b in range(3)]
            value = cols[1] + shifted(cols[0], -1) + shifted(cols[2], 1)
            gradient[i, :, part] = value[LEFT : LEFT + width].astype(BF16)
            return carry

        lax.fori_loop(0, height, body, 0, unroll=2)


def slide_sum_kernel(rd, terms, shares, small, spread):
    slides, rows, channels = terms.shape
    main = rows - 8
    summed = terms[0]
    for k in range(1, slides):
        summed = summed + terms[k]
    shares[...] = summed[:main].astype(BF16)
    tail = summed[main:]
    small[...] = tail
    lines = jnp.concatenate(
        [tail[q : q + 1, p : p + LANES] for q in range(rd) for p in range(0, channels, LANES)],
        axis=0,
    )
    spread[...] = jnp.broadcast_to(lines.astype(BF16)[None], spread.shape)


def join_kernel(rd, info, shares, small, spread, out):
    slides, rows, channels = out.shape
    summed = jnp.sum(spread[...].astype(F32), axis=0)
    per = channels // LANES
    tail = jnp.concatenate(
        [
            jnp.concatenate([summed[per * q + p : per * q + p + 1] for p in range(per)], axis=1)
            for q in range(rd)
        ],
        axis=0,
    )
    line = info[4:5, 0:1] * rd + iota((rd, channels), 0).astype(F32)
    tail = jnp.where(line < 9, tail, small[:rd])
    high, low = split(tail)
    tail = jnp.concatenate([high, low, jnp.zeros((16 - 2 * rd, channels), BF16)], axis=0)
    for k in range(slides):
        out[k, 0 : rows - 16, :] = shares[...]
        out[k, rows - 16 : rows, :] = tail


def finish_kernel(terms, loss, depth, point, classes):
    slides, rows, channels = terms.shape
    half = channels // 2
    rp, rc, rd = channels // slides, channels // slides // 2, 16 // slides
    flat, small = [], []
    for k in range(slides):
        piece = terms[k].astype(F32)
        point[k * rp : (k + 1) * rp, :] = piece[:rp]
        flat += [piece[rp : rp + rc, :half], piece[rp : rp + rc, half:]]
        tail = piece[rp + rc :]
        small.append(tail[:rd] + tail[rd : 2 * rd])
    flat = jnp.concatenate(flat, axis=0)
    small = jnp.concatenate(small, axis=0)
    full = tri_unpack(flat[:half], flat[half:], small[9:10, :half])
    classes[0] = full
    classes[1] = -full
    for a in range(3):
        depth[a] = small[3 * a : 3 * a + 3]
    loss[...] = small[9:10, half : half + 1]


def per_device(features, depth_weight, point_weight, classifier, valid_count, labels):
    slides, grid_y, grid_x = (lax.axis_size(axis) for axis in ("slide", "gy", "gx"))
    planes = grid_y * grid_x
    tile = features[0]
    height, width, channels = tile.shape
    wide = width + 2 * LEFT

    def upward(part, axis):
        pairs = [(i, i + 1) for i in range(lax.axis_size(axis) - 1)]
        return lax.ppermute(part, axis, pairs)

    def downward(part, axis):
        pairs = [(i + 1, i) for i in range(lax.axis_size(axis) - 1)]
        return lax.ppermute(part, axis, pairs)

    square = jax.ShapeDtypeStruct((channels, channels), BF16)
    strip = jax.ShapeDtypeStruct((height, RIM, channels), BF16)
    up, down = upward(tile[height - RIM :], "gy"), downward(tile[:RIM], "gy")
    tile, low, high = pl.pallas_call(
        load_kernel,
        out_shape=(jax.ShapeDtypeStruct(tile.shape, BF16), strip, strip),
        in_specs=[VMEM],
        out_specs=(VMEM,) * 3,
        compiler_params=SMALL,
        name="load",
    )(tile)

    low_strip = jnp.concatenate([up[:, :RIM], low, down[:, :RIM]], axis=0)
    high_strip = jnp.concatenate(
        [up[:, width - RIM :], high, down[:, width - RIM :]], axis=0
    )
    left, right = upward(high_strip, "gx"), downward(low_strip, "gx")
    scalars = jnp.where(iota((8, LANES), 0) == 0, valid_count[0, 0, 0], labels[0]).astype(F32)
    weights, point, point_turned, info = pl.pallas_call(
        weights_kernel,
        out_shape=(
            jax.ShapeDtypeStruct((9, channels), F32),
            square,
            square,
            jax.ShapeDtypeStruct((8, LANES), F32),
        ),
        in_specs=[VMEM] * 4,
        out_specs=(VMEM,) * 4,
        compiler_params=SMALL,
        name="weights",
    )(scalars, low_strip, depth_weight, point_weight)

    halo = (tile, up, down, left, right)
    chunks = -(-(channels + 6) // planes)
    pixels = (height + 2) * wide
    ext_shape = (height + 2 * RIM, wide, channels)

    mapped, packed, ext = pl.pallas_call(
        functools.partial(forward_kernel, planes, grid_x),
        out_shape=(
            jax.ShapeDtypeStruct((pixels, channels), BF16),
            jax.ShapeDtypeStruct((planes, 1, chunks * LANES), F32),
            jax.ShapeDtypeStruct(ext_shape, F32),
        ),
        in_specs=[VMEM] * 8,
        out_specs=(VMEM,) * 3,
        scratch_shapes=[
            pltpu.VMEM((pixels, channels), BF16),
            pltpu.VMEM((height * width, channels), BF16),
        ],
        compiler_params=PARAMS,
        name="forward",
    )(info, *halo, weights, point)

    packed = lax.all_to_all(packed, ("gy", "gx"), 0, 0)

    packed = pl.pallas_call(
        plane_sum_kernel,
        out_shape=jax.ShapeDtypeStruct((planes, 1, chunks * LANES), F32),
        in_specs=[VMEM],
        out_specs=VMEM,
        compiler_params=SMALL,
        name="plane_sum",
    )(packed)
    gathered = lax.all_to_all(packed, ("gy", "gx"), 0, 0)

    rp, rd = channels // slides, 16 // slides
    main = rp + rp // 2
    back, sent = pl.pallas_call(
        functools.partial(cov_kernel, grid_y, grid_x, slides),
        out_shape=(
            jax.ShapeDtypeStruct((pixels, channels), BF16),
            jax.ShapeDtypeStruct((slides, main + 8, channels), F32),
        ),
        in_specs=[VMEM] * 6 + [HBM],
        out_specs=(HBM, VMEM),
        scratch_shapes=[
            pltpu.VMEM((pixels, channels), BF16),
            pltpu.VMEM(classifier.shape, F32),
            pltpu.SemaphoreType.DMA((2,)),
        ],
        compiler_params=PARAMS,
        name="covariance",
    )(info, gathered, ext, mapped, point, point_turned, classifier)

    received = lax.all_to_all(sent, "slide", 0, 0)
    gradient = pl.pallas_call(
        spread_kernel,
        out_shape=jax.ShapeDtypeStruct((height, width, channels), BF16),
        in_specs=[VMEM, VMEM],
        out_specs=VMEM,
        compiler_params=PARAMS,
        cost_estimate=pl.CostEstimate(
            flops=20 * pixels * channels, bytes_accessed=4 << 20, transcendentals=0
        ),
        name="spread",
    )(back, weights)
    shares, small, spread = pl.pallas_call(
        functools.partial(slide_sum_kernel, rd),
        out_shape=(
            jax.ShapeDtypeStruct((main, channels), BF16),
            jax.ShapeDtypeStruct((8, channels), F32),
            jax.ShapeDtypeStruct((planes, rd * channels // LANES, LANES), BF16),
        ),
        in_specs=[VMEM],
        out_specs=(VMEM, VMEM, VMEM),
        compiler_params=SMALL,
        name="slide_sum",
    )(received)
    spread = lax.all_to_all(spread, ("gy", "gx"), 0, 0)
    spread, gradient = lax.optimization_barrier((spread, gradient))
    joined = pl.pallas_call(
        functools.partial(join_kernel, rd),
        out_shape=jax.ShapeDtypeStruct((slides, main + 16, channels), BF16),
        in_specs=[VMEM] * 4,
        out_specs=VMEM,
        compiler_params=SMALL,
        name="join",
    )(info, shares, small, spread)
    joined = lax.all_to_all(joined, "slide", 0, 0)
    loss, depth, point_total, class_total = pl.pallas_call(
        finish_kernel,
        out_shape=(
            jax.ShapeDtypeStruct((1, 1), F32),
            jax.ShapeDtypeStruct((3, 3, channels), F32),
            jax.ShapeDtypeStruct((channels, channels), F32),
            jax.ShapeDtypeStruct(classifier.shape, F32),
        ),
        in_specs=[VMEM],
        out_specs=(VMEM, VMEM, VMEM, VMEM),
        compiler_params=SMALL,
        name="finish",
    )(joined)
    return loss.reshape(()), depth, point_total, class_total, gradient[None]


def solution(mesh):
    placed = (P("slide", "gy", "gx", None), P(), P(), P(), P("slide", "gy", "gx"), P("slide"))
    return jax.shard_map(
        per_device,
        mesh=mesh,
        in_specs=placed,
        out_specs=(P(), P(), P(), P(), P("slide", "gy", "gx", None)),
        check_vma=False,
    )
```

```python
import functools

import jax
import jax.numpy as jnp
from jax import lax
from jax.experimental import pallas as pl
from jax.experimental.pallas import tpu as pltpu
from jax.sharding import PartitionSpec as P

ITERS = 5
RIM = 2
LEFT = 8
LANES = 128
F32 = jnp.float32
BF16 = jnp.bfloat16
VMEM = pl.BlockSpec(memory_space=pltpu.VMEM)
HBM = pl.BlockSpec(memory_space=pltpu.HBM)
PARAMS = pltpu.CompilerParams(vmem_limit_bytes=16 * 1024 * 1024)
SMALL = pltpu.CompilerParams(vmem_limit_bytes=4 * 1024 * 1024)


def iota(shape, dim):
    return lax.broadcasted_iota(jnp.int32, shape, dim)


def total(x):
    return jnp.sum(jnp.sum(x, axis=1, keepdims=True), axis=0, keepdims=True)


def dot(left, right):
    return jnp.dot(left, right, preferred_element_type=F32)


def split(x):
    high = x.astype(BF16)
    return high, (x - high.astype(F32)).astype(BF16)


def mm(left, right):
    lhs = jnp.concatenate([left[0], left[1], left[0]], axis=1)
    rhs = jnp.concatenate([right[0], right[0], right[1]], axis=0)
    return dot(lhs, rhs)


def stack(*pairs):
    return tuple(jnp.concatenate([pair[i] for pair in pairs], axis=0) for i in range(2))


def beside(*pairs):
    return tuple(jnp.concatenate([pair[i] for pair in pairs], axis=1) for i in range(2))


def shifted(x, step):
    return pltpu.roll(x, step % x.shape[0], 0)


def tri_pack(full):
    half = full.shape[0] // 2
    row, col = iota((half, half), 0), iota((half, half), 1)
    first, upper, second = full[:half, :half], full[:half, half:], full[half:, half:]
    both = jnp.where(row <= col, first, second)
    diag = jnp.sum(jnp.where(row == col, second, 0.0), axis=0, keepdims=True)
    return upper, both, diag


def tri_unpack(upper, both, diag):
    half = both.shape[0]
    row, col = iota((half, half), 0), iota((half, half), 1)
    turned = both.T
    first = jnp.where(row <= col, both, turned)
    second = jnp.where(row > col, both, jnp.where(row == col, diag, turned))
    return jnp.concatenate(
        [jnp.concatenate([first, upper], axis=1), jnp.concatenate([upper.T, second], axis=1)],
        axis=0,
    )


def assemble(ext, tile, up, down, left, right):
    height, width, channels = tile.shape
    rows = height + 2 * RIM
    ext[:, 0:LEFT, :] = jnp.zeros((rows, LEFT, channels), F32)
    ext[:, LEFT + width : 2 * LEFT + width, :] = jnp.zeros((rows, LEFT, channels), F32)
    ext[RIM : RIM + height, LEFT : LEFT + width, :] = tile[...].astype(F32)
    ext[0:RIM, LEFT : LEFT + width, :] = up[...].astype(F32)
    ext[RIM + height : rows, LEFT : LEFT + width, :] = down[...].astype(F32)
    ext[:, LEFT - RIM : LEFT, :] = left[...].astype(F32)
    ext[:, LEFT + width : LEFT + width + RIM, :] = right[...].astype(F32)


def load_kernel(
    scalars, tile_in, weights, point, tile, low, high, taps, mixing, turned, info
):
    width = tile.shape[1]
    tile[...] = tile_in[...]
    low[...] = tile_in[:, :RIM, :]
    high[...] = tile_in[:, width - RIM :, :]
    taps[...] = jnp.concatenate([weights[a].astype(F32) for a in range(3)], axis=0)
    mixing[...] = point[...]
    turned[...] = point[...].astype(F32).T.astype(BF16)
    row = iota(info.shape, 0)
    value = scalars[...]
    for k, axis in enumerate(("gy", "gx", "slide")):
        position = lax.axis_index(axis).astype(jnp.int32).astype(F32)
        value = jnp.where(row == k + 2, position, value)
    info[...] = value


def forward_kernel(
    planes, grid_x, info, tile, up, down, left, right, weights, point, mapped, packed, ext, hidden, inner
):
    height, width, channels = tile.shape
    wide = ext.shape[1]
    assemble(ext, tile, up, down, left, right)
    valid = jnp.broadcast_to(info[0:1, :].astype(jnp.int32), (width, LANES))
    order = iota((width, LANES), 0)

    for lane in range(0, channels, LANES):
        part = slice(lane, lane + LANES)
        taps = [weights[k : k + 1, part] for k in range(9)]

        def body(r, carry, part=part, taps=taps):
            rows = [ext[r + a, :, part] for a in range(3)]
            cols = [sum(rows[a] * taps[3 * a + b] for a in range(3)) for b in range(3)]
            value = cols[1] + shifted(cols[0], 1) + shifted(cols[2], -1)
            hidden[pl.ds(pl.multiple_of(r * wide, 16), wide), part] = value.astype(BF16)

            @pl.when((r >= 1) & (r <= height))
            def _():
                kept = jnp.where(order < valid - (r - 1) * width, value[LEFT : LEFT + width], 0.0)
                start = pl.multiple_of((r - 1) * width, 16)
                inner[pl.ds(start, width), part] = kept.astype(BF16)

            return carry

        lax.fori_loop(0, height + 2, body, 0, unroll=2)

    kept = inner[...]
    gram = lax.dot_general(kept, kept, (((0,), (0,)), ((), ())), preferred_element_type=F32)
    mapped[...] = dot(hidden[...], point[...]).astype(BF16)
    ones = jnp.ones((16, height * width), BF16)
    sums = dot(ones, kept)[0:1]
    first = dot(ones, dot(kept, point[...]).astype(BF16))[0:1]
    upper, both, diag = tri_pack(gram)
    chunks = packed.shape[2] // LANES
    lines = [line[:, p : p + LANES] for line in (sums, first) for p in range(0, channels, LANES)]
    spot = info[2:3, :] * grid_x + info[3:4, :]
    lines.append(jnp.where(iota((1, LANES), 1).astype(F32) == spot, info[0:1, :], 0.0))
    spare = chunks * planes - 2 * LANES - 1 - len(lines)
    flat = jnp.concatenate(
        [upper, both, diag] + lines + [jnp.zeros((spare, LANES), F32)], axis=0
    )
    for q in range(chunks):
        packed[:, 0, q * LANES : (q + 1) * LANES] = flat[q * planes : (q + 1) * planes]


def plane_sum_kernel(terms, out):
    out[...] = jnp.broadcast_to(jnp.sum(terms[...], axis=0, keepdims=True), out.shape)


def cov_kernel(
    grid_y, grid_x, slides, info, gathered, ext, mapped, point, point_turned, classes,
    back_out, sent, back, classifier, sems,
):
    planes = grid_y * grid_x
    wide, channels = ext.shape[1:]
    height, width = ext.shape[0] - 2 * RIM, wide - 2 * LEFT
    half = channels // 2
    chunks = gathered.shape[2] // LANES

    fetch = pltpu.make_async_copy(classes, classifier, sems.at[0])
    fetch.start()
    flat = jnp.concatenate(
        [gathered[:, 0, q * LANES : (q + 1) * LANES] for q in range(chunks)], axis=0
    )
    counts = flat[2 * half + 5 : 2 * half + 6]
    inverse = 1.0 / jnp.sum(counts, axis=1, keepdims=True)
    gram = tri_unpack(flat[:half], flat[half : 2 * half], flat[2 * half : 2 * half + 1])
    sums = jnp.concatenate(
        [flat[2 * half + 1 : 2 * half + 2], flat[2 * half + 2 : 2 * half + 3]], axis=1
    )
    mapped_sum = jnp.concatenate(
        [flat[2 * half + 3 : 2 * half + 4], flat[2 * half + 4 : 2 * half + 5]], axis=1
    )
    center = sums * inverse
    spread = jnp.broadcast_to(center, (channels, channels))
    moment = gram * inverse - spread * spread.T

    mixing, mixing_turned = point[...], point_turned[...]
    high, low = split(moment)
    moved = dot(
        jnp.concatenate([high, low], axis=1), jnp.concatenate([mixing, mixing], axis=0)
    )
    moved_pair = split(moved)
    sigma = dot(
        jnp.concatenate([mixing_turned, mixing_turned], axis=1),
        jnp.concatenate(moved_pair, axis=0),
    )
    eye = iota((channels, channels), 0) == iota((channels, channels), 1)
    trace = total(jnp.where(eye, sigma, 0.0))
    start = sigma * (1.0 / trace)

    fetch.wait()
    toward = classifier[0] - classifier[1]
    toward = toward + toward.T
    wmat, ymat, dw, dy = start, start, toward, toward
    for step in range(ITERS):
        w_pair, dw_pair = split(wmat), split(dw)
        both = beside(w_pair, dw_pair)
        if step == 0:
            first = mm(w_pair, both)
            square, cross = first[:, :channels], first[:, channels:]
            yw, dyw = square, cross + cross.T
        elif step + 1 < ITERS:
            first = mm(stack(w_pair, split(ymat)), both)
            square, cross = first[:channels, :channels], first[:channels, channels:]
            yw = first[channels:, :channels]
            dyw = first[channels:, channels:] + mm(split(dy), w_pair)
        else:
            first = mm(split(ymat), both)
            yw = first[:, :channels]
            dyw = first[:, channels:] + mm(split(dy), w_pair)
        ymat = 1.5 * ymat - 0.5 * yw
        dy = 1.5 * dy - 0.5 * dyw
        if step + 1 < ITERS:
            dsquare = cross + cross.T
            third = mm(split(square), both)
            dcube = third[:, channels:] + mm(split(dsquare), w_pair)
            wmat = 2.25 * wmat - 1.5 * square + 0.25 * third[:, :channels]
            dw = 2.25 * dw - 1.5 * dsquare + 0.25 * dcube

    root = jnp.sqrt(trace)
    pooled = root * ymat
    logit0 = total(classifier[0] * pooled)
    logit1 = total(classifier[1] * pooled)
    peak = jnp.maximum(logit0, logit1)
    lse = peak + jnp.log(jnp.exp(logit0 - peak) + jnp.exp(logit1 - peak))
    is_zero = info[1:2, 0:1] == 0.0
    slope = jnp.where(is_zero, -jnp.exp(logit1 - lse), jnp.exp(logit0 - lse)) * (1.0 / slides)
    loss = (lse - jnp.where(is_zero, logit0, logit1)) * (1.0 / slides)

    level = 0.5 * total(toward * ymat) - total(dy * start)
    slant = (dy + jnp.where(eye, level, 0.0)) * (slope / root)
    point_term = mm(moved_pair, split(slant))
    class_term = slope * pooled

    symmetric = slant * inverse
    sym_pair = split(symmetric)
    mean = jnp.broadcast_to(mapped_sum * inverse, (8, channels))
    offset = -mm(split(mean), sym_pair)[0:1]

    place = iota((1, LANES), 1).astype(F32)
    spots = []
    for dy_ in (-1, 0, 1):
        for dx_ in (-1, 0, 1):
            near_y, near_x = info[2:3, 0:1] + dy_, info[3:4, 0:1] + dx_
            inside = (near_y >= 0) & (near_y < grid_y) & (near_x >= 0) & (near_x < grid_x)
            spot = jnp.where(inside, near_y * grid_x + near_x, -1.0)
            near = jnp.where(place == spot, counts, 0.0)
            spots.append(jnp.sum(near, axis=1, keepdims=True))

    both = dot(mapped[...], sym_pair[0]) + dot(mapped[...], sym_pair[1]) + offset
    lane_col = iota((wide, channels), 0) - LEFT
    inner_col = jnp.where(lane_col < 0, lane_col + width, jnp.where(lane_col >= width, lane_col - width, lane_col))
    seen = (lane_col >= -1) & (lane_col <= width)
    limits = []
    for k in range(3):
        limit = jnp.where(
            lane_col < 0, spots[3 * k], jnp.where(lane_col >= width, spots[3 * k + 2], spots[3 * k + 1])
        )
        limits.append(jnp.where(seen, limit, -1.0))
    pieces = []
    for r in range(height + 2):
        tile_row = (r - 1) % height
        limit = limits[0 if r == 0 else (2 if r == height + 1 else 1)]
        raster = (tile_row * width + inner_col).astype(F32)
        pieces.append(jnp.where(raster < limit, both[r * wide : (r + 1) * wide], 0.0).astype(BF16))
    back_mapped = jnp.concatenate(pieces, axis=0)
    back[...] = dot(back_mapped, mixing_turned).astype(BF16)
    copy = pltpu.make_async_copy(back, back_out, sems.at[1])
    copy.start()

    depth = []
    for lane in range(0, channels, LANES):
        part = slice(lane, lane + LANES)
        column = iota((wide, LANES), 0)
        within = (column >= LEFT) & (column < LEFT + width)

        def body(i, sums, part=part, within=within):
            start = pl.multiple_of((i + 1) * wide, 16)
            own = jnp.where(within, back[pl.ds(start, wide), part].astype(F32), 0.0)
            moved_own = [shifted(own, -1), own, shifted(own, 1)]
            feats = [ext[i + 1 + a, :, part] for a in range(3)]
            out = []
            for a in range(3):
                for b in range(3):
                    product = (feats[a] * moved_own[b]).reshape(wide // 8, 8, LANES)
                    out.append(sums[3 * a + b] + jnp.sum(product, axis=0))
            return tuple(out)

        sums = lax.fori_loop(
            0, height, body, tuple(jnp.zeros((8, LANES), F32) for _ in range(9)), unroll=2
        )
        depth.append(
            jnp.concatenate([jnp.sum(s, axis=0, keepdims=True) for s in sums], axis=0)
        )
    depth = jnp.concatenate(depth, axis=1)

    upper, tri, diag = tri_pack(class_term)
    class_flat = jnp.concatenate([upper, tri], axis=0)
    extra = jnp.concatenate([diag, jnp.broadcast_to(loss, (1, half))], axis=1)
    small = jnp.concatenate([depth, extra, jnp.zeros((6, channels), F32)], axis=0)
    rp, rc, rd = channels // slides, channels // slides // 2, 16 // slides
    pad = [jnp.zeros((8 - rd, channels), F32)] if rd < 8 else []
    for k in range(slides):
        sent[k, 0:rp, :] = point_term[k * rp : (k + 1) * rp]
        sent[k, rp : rp + rc, 0:half] = class_flat[k * rp : k * rp + rc]
        sent[k, rp : rp + rc, half:channels] = class_flat[k * rp + rc : (k + 1) * rp]
        sent[k, rp + rc : rp + rc + 8, :] = jnp.concatenate(
            [small[k * rd : (k + 1) * rd]] + pad, axis=0
        )
    copy.wait()


def spread_kernel(back, weights, gradient):
    height, width, channels = gradient.shape
    wide = width + 2 * LEFT
    for lane in range(0, channels, LANES):
        part = slice(lane, lane + LANES)
        taps = [weights[k : k + 1, part] for k in range(9)]

        def body(i, carry, part=part, taps=taps):
            rows = [
                back[pl.ds(pl.multiple_of((i + a) * wide, 16), wide), part].astype(F32)
                for a in range(3)
            ]
            cols = [sum(rows[2 - a] * taps[3 * a + b] for a in range(3)) for b in range(3)]
            value = cols[1] + shifted(cols[0], -1) + shifted(cols[2], 1)
            gradient[i, :, part] = value[LEFT : LEFT + width].astype(BF16)
            return carry

        lax.fori_loop(0, height, body, 0, unroll=2)


def slide_sum_kernel(rd, terms, shares, small, spread):
    slides, rows, channels = terms.shape
    main = rows - 8
    summed = terms[0]
    for k in range(1, slides):
        summed = summed + terms[k]
    shares[...] = summed[:main].astype(BF16)
    tail = summed[main:]
    small[...] = tail
    lines = jnp.concatenate(
        [tail[q : q + 1, p : p + LANES] for q in range(rd) for p in range(0, channels, LANES)],
        axis=0,
    )
    spread[...] = jnp.broadcast_to(lines.astype(BF16)[None], spread.shape)


def join_kernel(rd, info, shares, small, spread, out):
    slides, rows, channels = out.shape
    summed = jnp.sum(spread[...].astype(F32), axis=0)
    per = channels // LANES
    tail = jnp.concatenate(
        [
            jnp.concatenate([summed[per * q + p : per * q + p + 1] for p in range(per)], axis=1)
            for q in range(rd)
        ],
        axis=0,
    )
    line = info[4:5, 0:1] * rd + iota((rd, channels), 0).astype(F32)
    tail = jnp.where(line < 9, tail, small[:rd])
    high, low = split(tail)
    tail = jnp.concatenate([high, low, jnp.zeros((16 - 2 * rd, channels), BF16)], axis=0)
    for k in range(slides):
        out[k, 0 : rows - 16, :] = shares[...]
        out[k, rows - 16 : rows, :] = tail


def finish_kernel(terms, loss, depth, point, classes):
    slides, rows, channels = terms.shape
    half = channels // 2
    rp, rc, rd = channels // slides, channels // slides // 2, 16 // slides
    flat, small = [], []
    for k in range(slides):
        piece = terms[k].astype(F32)
        point[k * rp : (k + 1) * rp, :] = piece[:rp]
        flat += [piece[rp : rp + rc, :half], piece[rp : rp + rc, half:]]
        tail = piece[rp + rc :]
        small.append(tail[:rd] + tail[rd : 2 * rd])
    flat = jnp.concatenate(flat, axis=0)
    small = jnp.concatenate(small, axis=0)
    full = tri_unpack(flat[:half], flat[half:], small[9:10, :half])
    classes[0] = full
    classes[1] = -full
    for a in range(3):
        depth[a] = small[3 * a : 3 * a + 3]
    loss[...] = small[9:10, half : half + 1]


def per_device(features, depth_weight, point_weight, classifier, valid_count, labels):
    slides, grid_y, grid_x = (lax.axis_size(axis) for axis in ("slide", "gy", "gx"))
    planes = grid_y * grid_x
    tile = features[0]
    height, width, channels = tile.shape
    wide = width + 2 * LEFT

    def upward(part, axis):
        pairs = [(i, i + 1) for i in range(lax.axis_size(axis) - 1)]
        return lax.ppermute(part, axis, pairs)

    def downward(part, axis):
        pairs = [(i + 1, i) for i in range(lax.axis_size(axis) - 1)]
        return lax.ppermute(part, axis, pairs)

    square = jax.ShapeDtypeStruct((channels, channels), BF16)
    strip = jax.ShapeDtypeStruct((height, RIM, channels), BF16)
    up, down = upward(tile[height - RIM :], "gy"), downward(tile[:RIM], "gy")
    scalars = jnp.where(iota((8, LANES), 0) == 0, valid_count[0, 0, 0], labels[0]).astype(F32)
    tile, low, high, weights, point, point_turned, info = pl.pallas_call(
        load_kernel,
        out_shape=(
            jax.ShapeDtypeStruct(tile.shape, BF16),
            strip,
            strip,
            jax.ShapeDtypeStruct((9, channels), F32),
            square,
            square,
            jax.ShapeDtypeStruct((8, LANES), F32),
        ),
        in_specs=[VMEM] * 4,
        out_specs=(VMEM,) * 7,
        compiler_params=SMALL,
        name="load",
    )(scalars, tile, depth_weight, point_weight)

    low_strip = jnp.concatenate([up[:, :RIM], low, down[:, :RIM]], axis=0)
    high_strip = jnp.concatenate(
        [up[:, width - RIM :], high, down[:, width - RIM :]], axis=0
    )
    left, right = upward(high_strip, "gx"), downward(low_strip, "gx")

    halo = (tile, up, down, left, right)
    chunks = -(-(channels + 6) // planes)
    pixels = (height + 2) * wide
    ext_shape = (height + 2 * RIM, wide, channels)

    mapped, packed, ext = pl.pallas_call(
        functools.partial(forward_kernel, planes, grid_x),
        out_shape=(
            jax.ShapeDtypeStruct((pixels, channels), BF16),
            jax.ShapeDtypeStruct((planes, 1, chunks * LANES), F32),
            jax.ShapeDtypeStruct(ext_shape, F32),
        ),
        in_specs=[VMEM] * 8,
        out_specs=(VMEM,) * 3,
        scratch_shapes=[
            pltpu.VMEM((pixels, channels), BF16),
            pltpu.VMEM((height * width, channels), BF16),
        ],
        compiler_params=PARAMS,
        name="forward",
    )(info, *halo, weights, point)

    packed = lax.all_to_all(packed, ("gy", "gx"), 0, 0)

    packed = pl.pallas_call(
        plane_sum_kernel,
        out_shape=jax.ShapeDtypeStruct((planes, 1, chunks * LANES), F32),
        in_specs=[VMEM],
        out_specs=VMEM,
        compiler_params=SMALL,
        name="plane_sum",
    )(packed)
    gathered = lax.all_to_all(packed, ("gy", "gx"), 0, 0)

    rp, rd = channels // slides, 16 // slides
    main = rp + rp // 2
    back, sent = pl.pallas_call(
        functools.partial(cov_kernel, grid_y, grid_x, slides),
        out_shape=(
            jax.ShapeDtypeStruct((pixels, channels), BF16),
            jax.ShapeDtypeStruct((slides, main + 8, channels), F32),
        ),
        in_specs=[VMEM] * 6 + [HBM],
        out_specs=(HBM, VMEM),
        scratch_shapes=[
            pltpu.VMEM((pixels, channels), BF16),
            pltpu.VMEM(classifier.shape, F32),
            pltpu.SemaphoreType.DMA((2,)),
        ],
        compiler_params=PARAMS,
        name="covariance",
    )(info, gathered, ext, mapped, point, point_turned, classifier)

    received = lax.all_to_all(sent, "slide", 0, 0)
    gradient = pl.pallas_call(
        spread_kernel,
        out_shape=jax.ShapeDtypeStruct((height, width, channels), BF16),
        in_specs=[VMEM, VMEM],
        out_specs=VMEM,
        compiler_params=PARAMS,
        cost_estimate=pl.CostEstimate(
            flops=20 * pixels * channels, bytes_accessed=4 << 20, transcendentals=0
        ),
        name="spread",
    )(back, weights)
    shares, small, spread = pl.pallas_call(
        functools.partial(slide_sum_kernel, rd),
        out_shape=(
            jax.ShapeDtypeStruct((main, channels), BF16),
            jax.ShapeDtypeStruct((8, channels), F32),
            jax.ShapeDtypeStruct((planes, rd * channels // LANES, LANES), BF16),
        ),
        in_specs=[VMEM],
        out_specs=(VMEM, VMEM, VMEM),
        compiler_params=SMALL,
        name="slide_sum",
    )(received)
    spread = lax.all_to_all(spread, ("gy", "gx"), 0, 0)
    spread, gradient = lax.optimization_barrier((spread, gradient))
    joined = pl.pallas_call(
        functools.partial(join_kernel, rd),
        out_shape=jax.ShapeDtypeStruct((slides, main + 16, channels), BF16),
        in_specs=[VMEM] * 4,
        out_specs=VMEM,
        compiler_params=SMALL,
        name="join",
    )(info, shares, small, spread)
    joined = lax.all_to_all(joined, "slide", 0, 0)
    loss, depth, point_total, class_total = pl.pallas_call(
        finish_kernel,
        out_shape=(
            jax.ShapeDtypeStruct((1, 1), F32),
            jax.ShapeDtypeStruct((3, 3, channels), F32),
            jax.ShapeDtypeStruct((channels, channels), F32),
            jax.ShapeDtypeStruct(classifier.shape, F32),
        ),
        in_specs=[VMEM],
        out_specs=(VMEM, VMEM, VMEM, VMEM),
        compiler_params=SMALL,
        name="finish",
    )(joined)
    return loss.reshape(()), depth, point_total, class_total, gradient[None]


def solution(mesh):
    placed = (P("slide", "gy", "gx", None), P(), P(), P(), P("slide", "gy", "gx"), P("slide"))
    return jax.shard_map(
        per_device,
        mesh=mesh,
        in_specs=placed,
        out_specs=(P(), P(), P(), P(), P("slide", "gy", "gx", None)),
        check_vma=False,
    )
```

```python
import functools

import jax
import jax.numpy as jnp
from jax import lax
from jax.experimental import pallas as pl
from jax.experimental.pallas import tpu as pltpu
from jax.sharding import PartitionSpec as P

ITERS = 5
RIM = 2
LEFT = 8
LANES = 128
F32 = jnp.float32
BF16 = jnp.bfloat16
VMEM = pl.BlockSpec(memory_space=pltpu.VMEM)
SMEM = pl.BlockSpec(memory_space=pltpu.SMEM)
HBM = pl.BlockSpec(memory_space=pltpu.HBM)
PARAMS = pltpu.CompilerParams(vmem_limit_bytes=16 * 1024 * 1024)
SMALL = pltpu.CompilerParams(vmem_limit_bytes=4 * 1024 * 1024)


def iota(shape, dim):
    return lax.broadcasted_iota(jnp.int32, shape, dim)


def total(x):
    return jnp.sum(jnp.sum(x, axis=1, keepdims=True), axis=0, keepdims=True)


def dot(left, right):
    return jnp.dot(left, right, preferred_element_type=F32)


def split(x):
    high = x.astype(BF16)
    return high, (x - high.astype(F32)).astype(BF16)


def mm(left, right):
    lhs = jnp.concatenate([left[0], left[1], left[0]], axis=1)
    rhs = jnp.concatenate([right[0], right[0], right[1]], axis=0)
    return dot(lhs, rhs)


def stack(*pairs):
    return tuple(jnp.concatenate([pair[i] for pair in pairs], axis=0) for i in range(2))


def beside(*pairs):
    return tuple(jnp.concatenate([pair[i] for pair in pairs], axis=1) for i in range(2))


def shifted(x, step):
    return pltpu.roll(x, step % x.shape[0], 0)


def tri_pack(full):
    half = full.shape[0] // 2
    row, col = iota((half, half), 0), iota((half, half), 1)
    first, upper, second = full[:half, :half], full[:half, half:], full[half:, half:]
    both = jnp.where(row <= col, first, second)
    diag = jnp.sum(jnp.where(row == col, second, 0.0), axis=0, keepdims=True)
    return upper, both, diag


def tri_unpack(upper, both, diag):
    half = both.shape[0]
    row, col = iota((half, half), 0), iota((half, half), 1)
    turned = both.T
    first = jnp.where(row <= col, both, turned)
    second = jnp.where(row > col, both, jnp.where(row == col, diag, turned))
    return jnp.concatenate(
        [jnp.concatenate([first, upper], axis=1), jnp.concatenate([upper.T, second], axis=1)],
        axis=0,
    )


def assemble(ext, tile, up, down, left, right):
    height, width, channels = tile.shape
    rows = height + 2 * RIM
    ext[:, 0:LEFT, :] = jnp.zeros((rows, LEFT, channels), F32)
    ext[:, LEFT + width : 2 * LEFT + width, :] = jnp.zeros((rows, LEFT, channels), F32)
    ext[RIM : RIM + height, LEFT : LEFT + width, :] = tile[...].astype(F32)
    ext[0:RIM, LEFT : LEFT + width, :] = up[...].astype(F32)
    ext[RIM + height : rows, LEFT : LEFT + width, :] = down[...].astype(F32)
    ext[:, LEFT - RIM : LEFT, :] = left[...].astype(F32)
    ext[:, LEFT + width : LEFT + width + RIM, :] = right[...].astype(F32)


def load_kernel(
    tile_in, weights, point, tile, low, high, taps, mixing, turned
):
    width = tile.shape[1]
    tile[...] = tile_in[...]
    low[...] = tile_in[:, :RIM, :]
    high[...] = tile_in[:, width - RIM :, :]
    taps[...] = jnp.concatenate([weights[a].astype(F32) for a in range(3)], axis=0)
    mixing[...] = point[...]
    turned[...] = point[...].astype(F32).T.astype(BF16)


def info_kernel(count, label, strip, info):
    row = iota(info.shape, 0)
    value = jnp.zeros(info.shape, F32)
    scalars = [count[0], label[0]] + [lax.axis_index(axis) for axis in ("gy", "gx", "slide")]
    for k, scalar in enumerate(scalars):
        value = jnp.where(row == k, scalar.astype(jnp.int32).astype(F32), value)
    info[...] = value


def forward_kernel(
    planes, grid_x, info, tile, up, down, left, right, weights, point, mapped, packed, ext, hidden, inner
):
    height, width, channels = tile.shape
    wide = ext.shape[1]
    assemble(ext, tile, up, down, left, right)
    valid = jnp.broadcast_to(info[0:1, :].astype(jnp.int32), (width, LANES))
    order = iota((width, LANES), 0)

    for lane in range(0, channels, LANES):
        part = slice(lane, lane + LANES)
        taps = [weights[k : k + 1, part] for k in range(9)]

        def body(r, carry, part=part, taps=taps):
            rows = [ext[r + a, :, part] for a in range(3)]
            cols = [sum(rows[a] * taps[3 * a + b] for a in range(3)) for b in range(3)]
            value = cols[1] + shifted(cols[0], 1) + shifted(cols[2], -1)
            hidden[pl.ds(pl.multiple_of(r * wide, 16), wide), part] = value.astype(BF16)

            @pl.when((r >= 1) & (r <= height))
            def _():
                kept = jnp.where(order < valid - (r - 1) * width, value[LEFT : LEFT + width], 0.0)
                start = pl.multiple_of((r - 1) * width, 16)
                inner[pl.ds(start, width), part] = kept.astype(BF16)

            return carry

        lax.fori_loop(0, height + 2, body, 0, unroll=2)

    kept = inner[...]
    gram = lax.dot_general(kept, kept, (((0,), (0,)), ((), ())), preferred_element_type=F32)
    mapped[...] = dot(hidden[...], point[...]).astype(BF16)
    ones = jnp.ones((16, height * width), BF16)
    sums = dot(ones, kept)[0:1]
    first = dot(ones, dot(kept, point[...]).astype(BF16))[0:1]
    upper, both, diag = tri_pack(gram)
    chunks = packed.shape[2] // LANES
    lines = [line[:, p : p + LANES] for line in (sums, first) for p in range(0, channels, LANES)]
    spot = info[2:3, :] * grid_x + info[3:4, :]
    lines.append(jnp.where(iota((1, LANES), 1).astype(F32) == spot, info[0:1, :], 0.0))
    spare = chunks * planes - 2 * LANES - 1 - len(lines)
    flat = jnp.concatenate(
        [upper, both, diag] + lines + [jnp.zeros((spare, LANES), F32)], axis=0
    )
    for q in range(chunks):
        packed[:, 0, q * LANES : (q + 1) * LANES] = flat[q * planes : (q + 1) * planes]


def plane_sum_kernel(terms, out):
    out[...] = jnp.broadcast_to(jnp.sum(terms[...], axis=0, keepdims=True), out.shape)


def cov_kernel(
    grid_y, grid_x, slides, info, gathered, ext, mapped, point, point_turned, classes,
    back_out, sent, back, classifier, sems,
):
    planes = grid_y * grid_x
    wide, channels = ext.shape[1:]
    height, width = ext.shape[0] - 2 * RIM, wide - 2 * LEFT
    half = channels // 2
    chunks = gathered.shape[2] // LANES

    fetch = pltpu.make_async_copy(classes, classifier, sems.at[0])
    fetch.start()
    flat = jnp.concatenate(
        [gathered[:, 0, q * LANES : (q + 1) * LANES] for q in range(chunks)], axis=0
    )
    counts = flat[2 * half + 5 : 2 * half + 6]
    inverse = 1.0 / jnp.sum(counts, axis=1, keepdims=True)
    gram = tri_unpack(flat[:half], flat[half : 2 * half], flat[2 * half : 2 * half + 1])
    sums = jnp.concatenate(
        [flat[2 * half + 1 : 2 * half + 2], flat[2 * half + 2 : 2 * half + 3]], axis=1
    )
    mapped_sum = jnp.concatenate(
        [flat[2 * half + 3 : 2 * half + 4], flat[2 * half + 4 : 2 * half + 5]], axis=1
    )
    center = sums * inverse
    spread = jnp.broadcast_to(center, (channels, channels))
    moment = gram * inverse - spread * spread.T

    mixing, mixing_turned = point[...], point_turned[...]
    high, low = split(moment)
    moved = dot(
        jnp.concatenate([high, low], axis=1), jnp.concatenate([mixing, mixing], axis=0)
    )
    moved_pair = split(moved)
    sigma = dot(
        jnp.concatenate([mixing_turned, mixing_turned], axis=1),
        jnp.concatenate(moved_pair, axis=0),
    )
    eye = iota((channels, channels), 0) == iota((channels, channels), 1)
    trace = total(jnp.where(eye, sigma, 0.0))
    start = sigma * (1.0 / trace)

    fetch.wait()
    toward = classifier[0] - classifier[1]
    toward = toward + toward.T
    wmat, ymat, dw, dy = start, start, toward, toward
    for step in range(ITERS):
        w_pair, dw_pair = split(wmat), split(dw)
        both = beside(w_pair, dw_pair)
        if step == 0:
            first = mm(w_pair, both)
            square, cross = first[:, :channels], first[:, channels:]
            yw, dyw = square, cross + cross.T
        elif step + 1 < ITERS:
            first = mm(stack(w_pair, split(ymat)), both)
            square, cross = first[:channels, :channels], first[:channels, channels:]
            yw = first[channels:, :channels]
            dyw = first[channels:, channels:] + mm(split(dy), w_pair)
        else:
            first = mm(split(ymat), both)
            yw = first[:, :channels]
            dyw = first[:, channels:] + mm(split(dy), w_pair)
        ymat = 1.5 * ymat - 0.5 * yw
        dy = 1.5 * dy - 0.5 * dyw
        if step + 1 < ITERS:
            dsquare = cross + cross.T
            third = mm(split(square), both)
            dcube = third[:, channels:] + mm(split(dsquare), w_pair)
            wmat = 2.25 * wmat - 1.5 * square + 0.25 * third[:, :channels]
            dw = 2.25 * dw - 1.5 * dsquare + 0.25 * dcube

    root = jnp.sqrt(trace)
    pooled = root * ymat
    logit0 = total(classifier[0] * pooled)
    logit1 = total(classifier[1] * pooled)
    peak = jnp.maximum(logit0, logit1)
    lse = peak + jnp.log(jnp.exp(logit0 - peak) + jnp.exp(logit1 - peak))
    is_zero = info[1:2, 0:1] == 0.0
    slope = jnp.where(is_zero, -jnp.exp(logit1 - lse), jnp.exp(logit0 - lse)) * (1.0 / slides)
    loss = (lse - jnp.where(is_zero, logit0, logit1)) * (1.0 / slides)

    level = 0.5 * total(toward * ymat) - total(dy * start)
    slant = (dy + jnp.where(eye, level, 0.0)) * (slope / root)
    point_term = mm(moved_pair, split(slant))
    class_term = slope * pooled

    symmetric = slant * inverse
    sym_pair = split(symmetric)
    mean = jnp.broadcast_to(mapped_sum * inverse, (8, channels))
    offset = -mm(split(mean), sym_pair)[0:1]

    place = iota((1, LANES), 1).astype(F32)
    spots = []
    for dy_ in (-1, 0, 1):
        for dx_ in (-1, 0, 1):
            near_y, near_x = info[2:3, 0:1] + dy_, info[3:4, 0:1] + dx_
            inside = (near_y >= 0) & (near_y < grid_y) & (near_x >= 0) & (near_x < grid_x)
            spot = jnp.where(inside, near_y * grid_x + near_x, -1.0)
            near = jnp.where(place == spot, counts, 0.0)
            spots.append(jnp.sum(near, axis=1, keepdims=True))

    both = dot(mapped[...], sym_pair[0]) + dot(mapped[...], sym_pair[1]) + offset
    lane_col = iota((wide, channels), 0) - LEFT
    inner_col = jnp.where(lane_col < 0, lane_col + width, jnp.where(lane_col >= width, lane_col - width, lane_col))
    seen = (lane_col >= -1) & (lane_col <= width)
    limits = []
    for k in range(3):
        limit = jnp.where(
            lane_col < 0, spots[3 * k], jnp.where(lane_col >= width, spots[3 * k + 2], spots[3 * k + 1])
        )
        limits.append(jnp.where(seen, limit, -1.0))
    pieces = []
    for r in range(height + 2):
        tile_row = (r - 1) % height
        limit = limits[0 if r == 0 else (2 if r == height + 1 else 1)]
        raster = (tile_row * width + inner_col).astype(F32)
        pieces.append(jnp.where(raster < limit, both[r * wide : (r + 1) * wide], 0.0).astype(BF16))
    back_mapped = jnp.concatenate(pieces, axis=0)
    back[...] = dot(back_mapped, mixing_turned).astype(BF16)
    copy = pltpu.make_async_copy(back, back_out, sems.at[1])
    copy.start()

    depth = []
    for lane in range(0, channels, LANES):
        part = slice(lane, lane + LANES)
        column = iota((wide, LANES), 0)
        within = (column >= LEFT) & (column < LEFT + width)

        def body(i, sums, part=part, within=within):
            start = pl.multiple_of((i + 1) * wide, 16)
            own = jnp.where(within, back[pl.ds(start, wide), part].astype(F32), 0.0)
            moved_own = [shifted(own, -1), own, shifted(own, 1)]
            feats = [ext[i + 1 + a, :, part] for a in range(3)]
            out = []
            for a in range(3):
                for b in range(3):
                    product = (feats[a] * moved_own[b]).reshape(wide // 8, 8, LANES)
                    out.append(sums[3 * a + b] + jnp.sum(product, axis=0))
            return tuple(out)

        sums = lax.fori_loop(
            0, height, body, tuple(jnp.zeros((8, LANES), F32) for _ in range(9)), unroll=2
        )
        depth.append(
            jnp.concatenate([jnp.sum(s, axis=0, keepdims=True) for s in sums], axis=0)
        )
    depth = jnp.concatenate(depth, axis=1)

    upper, tri, diag = tri_pack(class_term)
    class_flat = jnp.concatenate([upper, tri], axis=0)
    extra = jnp.concatenate([diag, jnp.broadcast_to(loss, (1, half))], axis=1)
    small = jnp.concatenate([depth, extra, jnp.zeros((6, channels), F32)], axis=0)
    rp, rc, rd = channels // slides, channels // slides // 2, 16 // slides
    pad = [jnp.zeros((8 - rd, channels), F32)] if rd < 8 else []
    for k in range(slides):
        sent[k, 0:rp, :] = point_term[k * rp : (k + 1) * rp]
        sent[k, rp : rp + rc, 0:half] = class_flat[k * rp : k * rp + rc]
        sent[k, rp : rp + rc, half:channels] = class_flat[k * rp + rc : (k + 1) * rp]
        sent[k, rp + rc : rp + rc + 8, :] = jnp.concatenate(
            [small[k * rd : (k + 1) * rd]] + pad, axis=0
        )
    copy.wait()


def spread_kernel(back, weights, gradient):
    height, width, channels = gradient.shape
    wide = width + 2 * LEFT
    for lane in range(0, channels, LANES):
        part = slice(lane, lane + LANES)
        taps = [weights[k : k + 1, part] for k in range(9)]

        def body(i, carry, part=part, taps=taps):
            rows = [
                back[pl.ds(pl.multiple_of((i + a) * wide, 16), wide), part].astype(F32)
                for a in range(3)
            ]
            cols = [sum(rows[2 - a] * taps[3 * a + b] for a in range(3)) for b in range(3)]
            value = cols[1] + shifted(cols[0], -1) + shifted(cols[2], 1)
            gradient[i, :, part] = value[LEFT : LEFT + width].astype(BF16)
            return carry

        lax.fori_loop(0, height, body, 0, unroll=2)


def slide_sum_kernel(rd, terms, shares, small, spread):
    slides, rows, channels = terms.shape
    main = rows - 8
    summed = terms[0]
    for k in range(1, slides):
        summed = summed + terms[k]
    shares[...] = summed[:main].astype(BF16)
    tail = summed[main:]
    small[...] = tail
    lines = jnp.concatenate(
        [tail[q : q + 1, p : p + LANES] for q in range(rd) for p in range(0, channels, LANES)],
        axis=0,
    )
    spread[...] = jnp.broadcast_to(lines.astype(BF16)[None], spread.shape)


def join_kernel(rd, info, shares, small, spread, out):
    slides, rows, channels = out.shape
    summed = jnp.sum(spread[...].astype(F32), axis=0)
    per = channels // LANES
    tail = jnp.concatenate(
        [
            jnp.concatenate([summed[per * q + p : per * q + p + 1] for p in range(per)], axis=1)
            for q in range(rd)
        ],
        axis=0,
    )
    line = info[4:5, 0:1] * rd + iota((rd, channels), 0).astype(F32)
    tail = jnp.where(line < 9, tail, small[:rd])
    high, low = split(tail)
    tail = jnp.concatenate([high, low, jnp.zeros((16 - 2 * rd, channels), BF16)], axis=0)
    for k in range(slides):
        out[k, 0 : rows - 16, :] = shares[...]
        out[k, rows - 16 : rows, :] = tail


def finish_kernel(terms, loss, depth, point, classes):
    slides, rows, channels = terms.shape
    half = channels // 2
    rp, rc, rd = channels // slides, channels // slides // 2, 16 // slides
    flat, small = [], []
    for k in range(slides):
        piece = terms[k].astype(F32)
        point[k * rp : (k + 1) * rp, :] = piece[:rp]
        flat += [piece[rp : rp + rc, :half], piece[rp : rp + rc, half:]]
        tail = piece[rp + rc :]
        small.append(tail[:rd] + tail[rd : 2 * rd])
    flat = jnp.concatenate(flat, axis=0)
    small = jnp.concatenate(small, axis=0)
    full = tri_unpack(flat[:half], flat[half:], small[9:10, :half])
    classes[0] = full
    classes[1] = -full
    for a in range(3):
        depth[a] = small[3 * a : 3 * a + 3]
    loss[...] = small[9:10, half : half + 1]


def per_device(features, depth_weight, point_weight, classifier, valid_count, labels):
    slides, grid_y, grid_x = (lax.axis_size(axis) for axis in ("slide", "gy", "gx"))
    planes = grid_y * grid_x
    tile = features[0]
    height, width, channels = tile.shape
    wide = width + 2 * LEFT

    def upward(part, axis):
        pairs = [(i, i + 1) for i in range(lax.axis_size(axis) - 1)]
        return lax.ppermute(part, axis, pairs)

    def downward(part, axis):
        pairs = [(i + 1, i) for i in range(lax.axis_size(axis) - 1)]
        return lax.ppermute(part, axis, pairs)

    square = jax.ShapeDtypeStruct((channels, channels), BF16)
    strip = jax.ShapeDtypeStruct((height, RIM, channels), BF16)
    up, down = upward(tile[height - RIM :], "gy"), downward(tile[:RIM], "gy")
    tile, low, high, weights, point, point_turned = pl.pallas_call(
        load_kernel,
        out_shape=(
            jax.ShapeDtypeStruct(tile.shape, BF16),
            strip,
            strip,
            jax.ShapeDtypeStruct((9, channels), F32),
            square,
            square,
        ),
        in_specs=[VMEM] * 3,
        out_specs=(VMEM,) * 6,
        compiler_params=SMALL,
        name="load",
    )(tile, depth_weight, point_weight)

    low_strip = jnp.concatenate([up[:, :RIM], low, down[:, :RIM]], axis=0)
    high_strip = jnp.concatenate(
        [up[:, width - RIM :], high, down[:, width - RIM :]], axis=0
    )
    left, right = upward(high_strip, "gx"), downward(low_strip, "gx")
    info = pl.pallas_call(
        info_kernel,
        out_shape=jax.ShapeDtypeStruct((8, LANES), F32),
        in_specs=[SMEM, SMEM, VMEM],
        out_specs=VMEM,
        compiler_params=SMALL,
        name="info",
    )(valid_count.reshape(1), labels, low_strip)

    halo = (tile, up, down, left, right)
    chunks = -(-(channels + 6) // planes)
    pixels = (height + 2) * wide
    ext_shape = (height + 2 * RIM, wide, channels)

    mapped, packed, ext = pl.pallas_call(
        functools.partial(forward_kernel, planes, grid_x),
        out_shape=(
            jax.ShapeDtypeStruct((pixels, channels), BF16),
            jax.ShapeDtypeStruct((planes, 1, chunks * LANES), F32),
            jax.ShapeDtypeStruct(ext_shape, F32),
        ),
        in_specs=[VMEM] * 8,
        out_specs=(VMEM,) * 3,
        scratch_shapes=[
            pltpu.VMEM((pixels, channels), BF16),
            pltpu.VMEM((height * width, channels), BF16),
        ],
        compiler_params=PARAMS,
        name="forward",
    )(info, *halo, weights, point)

    packed = lax.all_to_all(packed, ("gy", "gx"), 0, 0)

    packed = pl.pallas_call(
        plane_sum_kernel,
        out_shape=jax.ShapeDtypeStruct((planes, 1, chunks * LANES), F32),
        in_specs=[VMEM],
        out_specs=VMEM,
        compiler_params=SMALL,
        name="plane_sum",
    )(packed)
    gathered = lax.all_to_all(packed, ("gy", "gx"), 0, 0)

    rp, rd = channels // slides, 16 // slides
    main = rp + rp // 2
    back, sent = pl.pallas_call(
        functools.partial(cov_kernel, grid_y, grid_x, slides),
        out_shape=(
            jax.ShapeDtypeStruct((pixels, channels), BF16),
            jax.ShapeDtypeStruct((slides, main + 8, channels), F32),
        ),
        in_specs=[VMEM] * 6 + [HBM],
        out_specs=(HBM, VMEM),
        scratch_shapes=[
            pltpu.VMEM((pixels, channels), BF16),
            pltpu.VMEM(classifier.shape, F32),
            pltpu.SemaphoreType.DMA((2,)),
        ],
        compiler_params=PARAMS,
        name="covariance",
    )(info, gathered, ext, mapped, point, point_turned, classifier)

    received = lax.all_to_all(sent, "slide", 0, 0)
    gradient = pl.pallas_call(
        spread_kernel,
        out_shape=jax.ShapeDtypeStruct((height, width, channels), BF16),
        in_specs=[VMEM, VMEM],
        out_specs=VMEM,
        compiler_params=PARAMS,
        cost_estimate=pl.CostEstimate(
            flops=20 * pixels * channels, bytes_accessed=4 << 20, transcendentals=0
        ),
        name="spread",
    )(back, weights)
    shares, small, spread = pl.pallas_call(
        functools.partial(slide_sum_kernel, rd),
        out_shape=(
            jax.ShapeDtypeStruct((main, channels), BF16),
            jax.ShapeDtypeStruct((8, channels), F32),
            jax.ShapeDtypeStruct((planes, rd * channels // LANES, LANES), BF16),
        ),
        in_specs=[VMEM],
        out_specs=(VMEM, VMEM, VMEM),
        compiler_params=SMALL,
        name="slide_sum",
    )(received)
    spread = lax.all_to_all(spread, ("gy", "gx"), 0, 0)
    spread, gradient = lax.optimization_barrier((spread, gradient))
    joined = pl.pallas_call(
        functools.partial(join_kernel, rd),
        out_shape=jax.ShapeDtypeStruct((slides, main + 16, channels), BF16),
        in_specs=[VMEM] * 4,
        out_specs=VMEM,
        compiler_params=SMALL,
        name="join",
    )(info, shares, small, spread)
    joined = lax.all_to_all(joined, "slide", 0, 0)
    loss, depth, point_total, class_total = pl.pallas_call(
        finish_kernel,
        out_shape=(
            jax.ShapeDtypeStruct((1, 1), F32),
            jax.ShapeDtypeStruct((3, 3, channels), F32),
            jax.ShapeDtypeStruct((channels, channels), F32),
            jax.ShapeDtypeStruct(classifier.shape, F32),
        ),
        in_specs=[VMEM],
        out_specs=(VMEM, VMEM, VMEM, VMEM),
        compiler_params=SMALL,
        name="finish",
    )(joined)
    return loss.reshape(()), depth, point_total, class_total, gradient[None]


def solution(mesh):
    placed = (P("slide", "gy", "gx", None), P(), P(), P(), P("slide", "gy", "gx"), P("slide"))
    return jax.shard_map(
        per_device,
        mesh=mesh,
        in_specs=placed,
        out_specs=(P(), P(), P(), P(), P("slide", "gy", "gx", None)),
        check_vma=False,
    )
```
